128 devices in a mesh: dp: 32 (over z, x, y_lo), blk: 4 (over y_hi, core).
Axes of the slice: x: 4, y: 4 (y_hi: 2, y_lo: 2; y = y_hi * 2 + y_lo), z: 4, core: 2. Of those that a mesh axis runs over, the one named last changes fastest.
Arguments:
- hidden: bfloat16 [32, 1536, 768], P('dp', 'blk'), may hold values from -6 to 6
- output_grad: bfloat16 [32, 1536, 768], P('dp', 'blk'), may hold values from -6 to 6
- block_counts: int32 [32], P('dp'), may hold values from 2 to 3, as said below
- slot_table: int32 [32, 3], P('dp'), may hold values from 0 to 2, as said below
- block_order_two: int32 [12, 2], replicated, may hold values from 0 to 1, each once within a row
- block_order_three: int32 [12, 3], replicated, may hold values from 0 to 2, each once within a row
- query_weight: bfloat16 [2, 768, 768], replicated, may hold values from -0.21875 to 0.21875
- key_weight: bfloat16 [2, 768, 768], replicated, may hold values from -0.21875 to 0.21875
- value_weight: bfloat16 [2, 768, 768], replicated, may hold values from -0.21875 to 0.21875
- output_weight: bfloat16 [2, 768, 768], replicated, may hold values from -3.5 to 3.5
- query_bias: bfloat16 [2, 768], replicated, may hold values from -2 to 2
- value_bias: bfloat16 [2, 768], replicated, may hold values from -2 to 2
- output_bias: bfloat16 [2, 768], replicated, may hold values from -2 to 2
- expand_weight: bfloat16 [2, 768, 3072], replicated, may hold values from -0.21875 to 0.21875
- expand_bias: bfloat16 [2, 3072], replicated, may hold values from -2 to 2
- reduce_weight: bfloat16 [2, 3072, 768], replicated, may hold values from -0.109375 to 0.109375
- reduce_bias: bfloat16 [2, 768], replicated, may hold values from -2 to 2
- first_gain: bfloat16 [2, 768], replicated, may hold values from 0.5 to 1.5
- first_shift: bfloat16 [2, 768], replicated, may hold values from -2 to 2
- second_gain: bfloat16 [2, 768], replicated, may hold values from 0.5 to 1.5
- second_shift: bfloat16 [2, 768], replicated, may hold values from -2 to 2
Outputs:
- activations: bfloat16 [32, 1536, 768], P('dp', 'blk')
- input_grad: bfloat16 [32, 1536, 768], P('dp', 'blk')
- grad_query_weight: float32 [2, 768, 768], P(None, ('dp', 'blk'))
- grad_key_weight: float32 [2, 768, 768], P(None, ('dp', 'blk'))
- grad_value_weight: float32 [2, 768, 768], P(None, ('dp', 'blk'))
- grad_output_weight: float32 [2, 768, 768], P(None, ('dp', 'blk'))
- grad_query_bias: float32 [2, 768], P(None, ('dp', 'blk'))
- grad_value_bias: float32 [2, 768], P(None, ('dp', 'blk'))
- grad_output_bias: float32 [2, 768], P(None, ('dp', 'blk'))
- grad_expand_weight: float32 [2, 768, 3072], P(None, ('dp', 'blk'))
- grad_expand_bias: float32 [2, 3072], P(None, ('dp', 'blk'))
- grad_reduce_weight: float32 [2, 3072, 768], P(None, ('dp', 'blk'))
- grad_reduce_bias: float32 [2, 768], P(None, ('dp', 'blk'))
- grad_first_gain: float32 [2, 768], P(None, ('dp', 'blk'))
- grad_first_shift: float32 [2, 768], P(None, ('dp', 'blk'))
- grad_second_gain: float32 [2, 768], P(None, ('dp', 'blk'))
- grad_second_shift: float32 [2, 768], P(None, ('dp', 'blk'))
The draws below stay inside these ranges and needn't reach their ends.
Inputs may be any that keep to these rules, and one draw needn't show every extreme that they name: `block_counts`: blocks of each sequence; its remaining slots are padding. Each row is a permutation: slot_table[s, j] is the slot of block j of sequence s; where block_counts[s] = 2, block 2 sits in slot 1. `block_order_two`: each row is a permutation. `block_order_three`: each row is a permutation.
All inputs are finite; a program needn't handle non-finite values.
Results may differ from the reference program's by a relative error of at most 0.03.
Values may be sent and summed in bfloat16 or wider, within the bound.
A program may use at most 320 MiB of HBM per device.

```python
import jax
import jax.numpy as jnp
from jax import lax

D = 768
HEADS = 12
FF = 3072
HD = 64
BLOCK = 512
SLOTS = 3
LENGTH = 1536
SEQS = 32


def one_order(row_key):
    return jax.random.permutation(row_key, SLOTS)


def shared_layout(key):
    base = jax.random.fold_in(key, 11)
    count_key, pick_key, order_key, flip_key = jax.random.split(base, 4)
    counts = jax.random.randint(count_key, (SEQS,), 2, 4).astype(jnp.int32)
    picked = jax.random.randint(pick_key, (), 0, SEQS).astype(jnp.int32)
    counts = counts.at[picked].set(3)
    counts = counts.at[(picked + 1) % SEQS].set(2)
    row_keys = jax.random.split(order_key, SEQS)
    orders = jax.vmap(one_order)(row_keys).astype(jnp.int32)
    flips = jax.random.randint(flip_key, (SEQS,), 0, 2).astype(jnp.int32)
    two_rows = jnp.stack([2 * flips, 2 - 2 * flips, jnp.ones_like(flips)], axis=1)
    table = jnp.where(counts[:, None] == 3, orders, two_rows)
    return (counts.astype(jnp.int32), table.astype(jnp.int32))


def draw_block_counts(key, part):
    counts, table = shared_layout(key)
    return counts


def draw_slot_table(key, part):
    counts, table = shared_layout(key)
    return table


def shard_levels(key, extent, cuts, low, top_value):
    def one(axis_at, parts):
        heights = jax.random.uniform(jax.random.fold_in(jax.random.fold_in(key, 6), axis_at), (parts,), jnp.float32, low / len(cuts), top_value / len(cuts))
        return jnp.repeat(jnp.exp(heights), extent[axis_at] // parts).reshape((-1,) + (1,) * (len(extent) - axis_at - 1))

    level = one(*cuts[0])
    for cut in cuts[1:]:
        level = level * one(*cut)
    return level


def noise(key, extent, spread, bound, pieces=(), held_as=jnp.bfloat16):
    values = jax.random.normal(key, extent, jnp.float32) * spread
    if len(pieces) > 0:
        values = shard_levels(key, extent, pieces, -0.22, 0.18) * values
    return jnp.clip(values, min=-bound, max=bound).astype(held_as)


def setup_inputs(seed: int = 0) -> dict:
    seeds = jax.random.split(jax.random.key(seed), 22)
    return {
        "hidden": noise(seeds[0], (SEQS, LENGTH, D), 1.0, 6.0, ((0, 32), (1, 4))),
        "output_grad": noise(seeds[1], (SEQS, LENGTH, D), 1.0, 6.0, ((0, 32), (1, 4))),
        "block_counts": draw_block_counts(jax.random.fold_in(seeds[21], 71), 0),
        "slot_table": draw_slot_table(jax.random.fold_in(seeds[21], 71), 0),
        "block_order_two": jax.vmap(lambda own: jax.random.permutation(own, 2))(jax.random.split(seeds[4], HEADS)).reshape((HEADS, 2)).astype(jnp.int32),
        "block_order_three": jax.vmap(lambda own: jax.random.permutation(own, 3))(jax.random.split(seeds[5], HEADS)).reshape((HEADS, 3)).astype(jnp.int32),
        "query_weight": noise(seeds[6], (2, D, D), D ** -0.5, 0.21875),
        "key_weight": noise(seeds[7], (2, D, D), D ** -0.5, 0.21875),
        "value_weight": noise(seeds[8], (2, D, D), D ** -0.5, 0.21875),
        "output_weight": noise(seeds[9], (2, D, D), (max(D // 256, 1)) ** -0.5, 3.5),
        "query_bias": noise(seeds[10], (2, D), 0.3, 2.0),
        "value_bias": noise(seeds[11], (2, D), 0.3, 2.0),
        "output_bias": noise(seeds[12], (2, D), 0.3, 2.0),
        "expand_weight": noise(seeds[13], (2, D, FF), D ** -0.5, 0.21875),
        "expand_bias": noise(seeds[14], (2, FF), 0.3, 2.0),
        "reduce_weight": noise(seeds[15], (2, FF, D), FF ** -0.5, 0.109375),
        "reduce_bias": noise(seeds[16], (2, D), 0.3, 2.0),
        "first_gain": jnp.clip(1.0 + 0.1 * jax.random.normal(seeds[17], (2, D), jnp.float32), 0.5, 1.5).astype(jnp.bfloat16),
        "first_shift": noise(seeds[18], (2, D), 0.3, 2.0),
        "second_gain": jnp.clip(1.0 + 0.1 * jax.random.normal(seeds[19], (2, D), jnp.float32), 0.5, 1.5).astype(jnp.bfloat16),
        "second_shift": noise(seeds[20], (2, D), 0.3, 2.0),
    }


@jax.custom_vjp
def low(v):
    return lax.optimization_barrier(v.astype(jnp.bfloat16)).astype(jnp.float32)

@jax.custom_vjp
def low_back(v):
    return v

def low_keep(v):
    return (low(v), None)

def low_pass(kept, grad):
    return (grad,)

def back_keep(v):
    return (v, None)

def back_low(kept, grad):
    return (low(grad),)
low.defvjp(low_keep, low_pass)
low_back.defvjp(back_keep, back_low)
HIGHEST = lax.Precision.HIGHEST
EPSILON = 1e-06

def matmul(left, right):
    return jnp.dot(left, right, precision=HIGHEST, preferred_element_type=jnp.float32)

def norm_layer(residual, norm_gain, norm_shift):
    row_mean = lax.optimization_barrier(jnp.mean(residual, axis=-1, keepdims=True))
    centred = residual - row_mean
    row_variance = lax.optimization_barrier(jnp.mean(centred * centred, axis=-1, keepdims=True))
    return centred * lax.rsqrt(row_variance + EPSILON) * norm_gain + norm_shift

def key_slots(slot_row, count, order_two, order_three, swapped):
    positions = jnp.arange(SLOTS, dtype=jnp.int32)
    inverse = lax.optimization_barrier(jnp.sum(positions[None, :] * (slot_row[None, :] == positions[:, None]), axis=1)).astype(jnp.int32)
    live_slots = (inverse < count).astype(jnp.float32)
    if swapped:
        from_three = order_three[:, inverse].T
        from_two = order_two[:, jnp.minimum(inverse, 1)].T
        own_block = jnp.broadcast_to(inverse[:, None], (SLOTS, HEADS))
        chosen = jnp.where(count == SLOTS, from_three, jnp.where(own_block < 2, from_two, own_block))
    else:
        chosen = jnp.broadcast_to(inverse[:, None], (SLOTS, HEADS))
    return (slot_row[chosen], live_slots)

def attend(queries, keys_all, values_all, target, live_slots):
    shaped = queries.reshape(SLOTS, BLOCK, HEADS, HD)
    key_heads = keys_all.reshape(SLOTS, BLOCK, HEADS, HD).transpose(0, 2, 1, 3)
    value_heads = values_all.reshape(SLOTS, BLOCK, HEADS, HD).transpose(0, 2, 1, 3)
    head_ids = jnp.arange(HEADS)
    key_sel = key_heads[target, head_ids[None, :]]
    value_sel = value_heads[target, head_ids[None, :]]
    scores = jnp.einsum('tqhd,thkd->thqk', shaped, key_sel, precision=HIGHEST) * HD ** (-0.5)
    scores = low_back(scores)
    weights = low(jax.nn.softmax(scores, axis=-1))
    mixed_heads = jnp.einsum('thqk,thkd->tqhd', weights, value_sel, precision=HIGHEST)
    mixed_heads = mixed_heads * live_slots[:, None, None, None]
    return mixed_heads.reshape(LENGTH, D)

def encoder_layer(hidden_seq, params, target, live_slots):
    query_weight, key_weight, value_weight, output_weight, query_bias, value_bias, output_bias, expand_weight, expand_bias, reduce_weight, reduce_bias, first_gain, first_shift, second_gain, second_shift = params
    hidden_low = low(hidden_seq)
    queries = low_back(low(matmul(hidden_low, query_weight) + query_bias))
    keys_all = low_back(low(matmul(hidden_low, key_weight)))
    values_all = low_back(low(matmul(hidden_low, value_weight) + value_bias))
    mixed_heads = low_back(low(attend(queries, keys_all, values_all, target, live_slots)))
    attn_out = low_back(matmul(mixed_heads, output_weight) + output_bias)
    first_norm = norm_layer(hidden_seq + attn_out, first_gain, first_shift)
    inner_pre = low_back(matmul(low(first_norm), expand_weight) + expand_bias)
    activated = low(jax.nn.gelu(inner_pre, approximate=False))
    outer_out = low_back(matmul(activated, reduce_weight) + reduce_bias)
    return norm_layer(first_norm + outer_out, second_gain, second_shift)

def two_layers(hidden_seq, slot_row, count, layer_one, layer_two, order_two, order_three):
    target_one, live_one = key_slots(slot_row, count, order_two, order_three, False)
    target_two, live_two = key_slots(slot_row, count, order_two, order_three, True)
    middle = encoder_layer(hidden_seq, layer_one, target_one, live_one)
    return encoder_layer(middle, layer_two, target_two, live_two)

def reference(hidden, output_grad, block_counts, slot_table, block_order_two, block_order_three, query_weight, key_weight, value_weight, output_weight, query_bias, value_bias, output_bias, expand_weight, expand_bias, reduce_weight, reduce_bias, first_gain, first_shift, second_gain, second_shift):
    params = tuple((tensor.astype(jnp.float32) for tensor in (query_weight, key_weight, value_weight, output_weight, query_bias, value_bias, output_bias, expand_weight, expand_bias, reduce_weight, reduce_bias, first_gain, first_shift, second_gain, second_shift)))

    def forward_all(inputs, weights):
        layer_one = tuple((tensor[0] for tensor in weights))
        layer_two = tuple((tensor[1] for tensor in weights))

        def sequence_forward(sequence_item):
            hidden_seq, slot_row, count = sequence_item
            return two_layers(hidden_seq, slot_row, count, layer_one, layer_two, block_order_two, block_order_three)
        return lax.map(jax.checkpoint(sequence_forward), (inputs, slot_table, block_counts))
    outputs, pullback = jax.vjp(forward_all, hidden.astype(jnp.float32), params)
    grad_hidden, grads = pullback(output_grad.astype(jnp.float32))
    grad_query_weight, grad_key_weight, grad_value_weight, grad_output_weight, grad_query_bias, grad_value_bias, grad_output_bias, grad_expand_weight, grad_expand_bias, grad_reduce_weight, grad_reduce_bias, grad_first_gain, grad_first_shift, grad_second_gain, grad_second_shift = grads
    return (outputs.astype(jnp.bfloat16), grad_hidden.astype(jnp.bfloat16), grad_query_weight, grad_key_weight, grad_value_weight, grad_output_weight, grad_query_bias, grad_value_bias, grad_output_bias, grad_expand_weight, grad_expand_bias, grad_reduce_weight, grad_reduce_bias, grad_first_gain, grad_first_shift, grad_second_gain, grad_second_shift)
```

```python
import jax
import jax.numpy as jnp
from jax import lax
from jax.experimental import pallas as pl
from jax.experimental.pallas import tpu as pltpu
from jax.sharding import Mesh
from jax.sharding import PartitionSpec as P

D = 768
HEADS = 12
HD = 64
BLOCK = 512
SLOTS = 3
BLK = ("blk_0", "blk_1")
DP_BLK = ("dp_0", "dp_1", "dp_2", "blk_0", "blk_1")
DP = ("dp_0", "dp_1", "dp_2")


EPSILON = 1e-06
MESH = pl.DeviceIdType.MESH
BF = jnp.bfloat16
F32 = jnp.float32
ROOT_HALF = 0.7071067811865476
INV_ROOT_TAU = 0.3989422804014327


def with_halo(array, sides, width):
    for axis, dim in sides:
        size, length = (lax.axis_size(axis), array.shape[dim])
        up = [(i, (i + 1) % size) for i in range(size - 1)]
        down = [(j, i) for i, j in up]
        last = lax.slice_in_dim(array, length - width, length, axis=dim)
        leading = lax.slice_in_dim(array, 0, width, axis=dim)
        before = lax.ppermute(last, axis, up)
        after = lax.ppermute(leading, axis, down)
        array = jnp.concatenate([before, array, after], axis=dim)
    return array


def from_behind(block, axis, distance):
    devices = range(lax.axis_size(axis))
    route = [(i - distance, i) for i in devices if i - distance in devices]
    return lax.ppermute(block, axis, route)


def side_by_side(arrays, axis, dim, along):
    widths = [a.shape[along] for a in arrays]
    both = jnp.concatenate(arrays, axis=along)
    filled = lax.all_gather(both, axis, axis=dim, tiled=True)
    return tuple(jnp.split(filled, [sum(widths[:k]) for k in range(1, len(widths))], axis=along))


def split_up(array, dim, size):
    shape = array.shape
    pieces = array.reshape(*shape[:dim], size, shape[dim] // size, *shape[dim + 1 :])
    return jnp.moveaxis(pieces, dim, 0)


def summed_rows(array, chips, core, dim):
    sizes = (lax.axis_size(chips), lax.axis_size(core))
    pieces = split_up(array, dim, sizes[0] * sizes[1])
    inside = pieces.shape[1:]
    pieces = pieces.reshape(*sizes, *inside).swapaxes(0, 1).reshape(-1, *inside)
    pieces = lax.psum_scatter(pieces, core, scatter_dimension=0, tiled=True)
    return lax.psum_scatter(pieces, chips, scatter_dimension=0, tiled=True)[0]


def side_by_side_2(arrays, axis, dim, along):
    ends, at = ([], 0)
    for a in arrays[:-1]:
        at += a.shape[along]
        ends.append(at)
    both = jnp.concatenate(arrays, axis=along)
    return tuple(
        jnp.split(lax.psum_scatter(both, axis, scatter_dimension=dim, tiled=True), ends, axis=along)
    )


def matmul(left, right):
    return jnp.dot(left, right, preferred_element_type=jnp.float32)


def contract_rows(left, right):
    return lax.dot_general(
        left, right, (((0,), (0,)), ((), ())), preferred_element_type=jnp.float32
    )


def times_transpose(left, right):
    return lax.dot_general(
        left, right, (((1,), (1,)), ((), ())), preferred_element_type=jnp.float32
    )


def norm_forward(residual, norm_gain, norm_shift):
    row_mean = jnp.mean(residual, axis=-1, keepdims=True)
    centred = residual - row_mean
    row_variance = jnp.mean(centred * centred, axis=-1, keepdims=True)
    inv_std = lax.rsqrt(row_variance + EPSILON)
    normed = centred * inv_std
    return (normed * norm_gain + norm_shift, normed, inv_std)


def norm_backward(grad_out, norm_gain, normed, inv_std):
    scaled = grad_out * norm_gain
    grad_input = inv_std * (
        scaled
        - jnp.mean(scaled, axis=-1, keepdims=True)
        - normed * jnp.mean(scaled * normed, axis=-1, keepdims=True)
    )
    return (grad_input, jnp.sum(grad_out * normed, axis=0), jnp.sum(grad_out, axis=0))


def gelu_slope(inner_pre):
    return 0.5 * (1.0 + lax.erf(inner_pre * ROOT_HALF)) + inner_pre * INV_ROOT_TAU * jnp.exp(
        -0.5 * inner_pre * inner_pre
    )


def live_pieces(slot_table, block_counts, piece_slot):
    positions = jnp.arange(SLOTS, dtype=jnp.int32)
    inverse = jnp.sum(
        positions[None, None, :] * (slot_table[:, None, :] == positions[None, :, None]), axis=2
    )
    block_number = jnp.sum(
        inverse[:, None, :] * (piece_slot[None, :, None] == positions[None, None, :]), axis=2
    )
    return (block_number, (block_number < block_counts[:, None]).astype(jnp.bfloat16))


def selection(slot_table, block_counts, order_two, order_three, block_number, swapped):
    positions = jnp.arange(SLOTS, dtype=jnp.int32)
    own_block = jnp.broadcast_to(block_number[:, :, None], block_number.shape + (HEADS,))
    if swapped:
        from_three = jnp.sum(
            (block_number[:, :, None, None] == positions[None, None, None, :])
            * order_three[None, None, :, :],
            axis=3,
        )
        pairs = jnp.arange(2, dtype=jnp.int32)
        from_two = jnp.sum(
            (jnp.minimum(block_number, 1)[:, :, None, None] == pairs[None, None, None, :])
            * order_two[None, None, :, :],
            axis=3,
        )
        chosen = jnp.where(
            block_counts[:, None, None] == SLOTS,
            from_three,
            jnp.where(own_block < 2, from_two, own_block),
        )
    else:
        chosen = own_block
    target = jnp.sum(
        (chosen[:, :, :, None] == positions[None, None, None, :]) * slot_table[:, None, None, :],
        axis=3,
    )
    return (target[:, :, :, None] == positions[None, None, None, :]).astype(jnp.bfloat16)


def pick_slots(picker, gathered):
    shaped = gathered.reshape(gathered.shape[0], SLOTS, BLOCK, HEADS, HD)
    return jnp.einsum(
        "spht,stkhd->sphkd", picker, shaped, preferred_element_type=jnp.float32
    ).astype(jnp.bfloat16)


def place_rims(widened, piece):
    seq_count = widened.shape[1]
    total_rows = piece * lax.axis_size(BLK)
    empty = jnp.zeros((2, seq_count, total_rows + 2 * piece, widened.shape[3]), widened.dtype)
    placed = lax.dynamic_update_slice_in_dim(empty, widened, lax.axis_index(BLK) * piece, 2)
    inside = placed[:, :, piece : piece + total_rows]
    return (inside[0], inside[1])


def neighbour_rows(key_local, value_local):
    piece = key_local.shape[1]
    stacked = jnp.stack([key_local, value_local])
    widened = with_halo(stacked, ((BLK, 2),), piece)
    return place_rims(widened, piece)


def return_rims(grad_keys, grad_values, piece):
    stacked = jnp.stack([grad_keys, grad_values])
    padded = jnp.pad(stacked, ((0, 0), (0, 0), (piece, piece), (0, 0)))
    window = lax.dynamic_slice_in_dim(padded, lax.axis_index(BLK) * piece, 3 * piece, 2)
    own_part = window[:, :, piece : 2 * piece]
    from_below = from_behind(window[:, :, 2 * piece :].astype(jnp.bfloat16), BLK, 1).astype(
        jnp.float32
    )
    from_above = from_behind(window[:, :, :piece].astype(jnp.bfloat16), BLK, -1).astype(jnp.float32)
    total = own_part + from_below + from_above
    return (total[0], total[1])


def attend_forward(queries, all_keys, all_values, picker, live_rows):
    shaped = queries.reshape(all_keys.shape[0], SLOTS, -1, HEADS, HD)
    key_sel = pick_slots(picker, all_keys)
    value_sel = pick_slots(picker, all_values)
    scores = jnp.einsum(
        "spqhd,sphkd->sphqk", shaped, key_sel, preferred_element_type=jnp.float32
    ) * HD ** (-0.5)
    row_max = jnp.max(scores, axis=-1, keepdims=True)
    log_total = row_max + jnp.log(jnp.sum(jnp.exp(scores - row_max), axis=-1, keepdims=True))
    weights_low = jnp.exp(scores - log_total).astype(jnp.bfloat16)
    mixed_heads = jnp.einsum(
        "sphqk,sphkd->spqhd", weights_low, value_sel, preferred_element_type=jnp.float32
    )
    mixed_heads = mixed_heads * live_rows[:, :, None, None, None].astype(jnp.float32)
    return (mixed_heads.reshape(queries.shape), log_total)


def attend_backward(queries, all_keys, all_values, log_total, grad_mixed, picker, live_rows):
    scale_factor = HD ** (-0.5)
    shaped = queries.reshape(all_keys.shape[0], SLOTS, -1, HEADS, HD)
    grad_shaped = grad_mixed.reshape(shaped.shape) * live_rows[:, :, None, None, None]
    key_sel = pick_slots(picker, all_keys)
    value_sel = pick_slots(picker, all_values)
    scores = (
        jnp.einsum("spqhd,sphkd->sphqk", shaped, key_sel, preferred_element_type=jnp.float32)
        * scale_factor
    )
    weights_full = jnp.exp(scores - log_total)
    grad_weights = jnp.einsum(
        "spqhd,sphkd->sphqk", grad_shaped, value_sel, preferred_element_type=jnp.float32
    )
    delta_rows = jnp.sum(weights_full * grad_weights, axis=-1, keepdims=True)
    grad_scores = (weights_full * (grad_weights - delta_rows)).astype(jnp.bfloat16)
    grad_query = (
        jnp.einsum("sphqk,sphkd->spqhd", grad_scores, key_sel, preferred_element_type=jnp.float32)
        * scale_factor
    )
    grad_key_sel = (
        jnp.einsum("sphqk,spqhd->sphkd", grad_scores, shaped, preferred_element_type=jnp.float32)
        * scale_factor
    )
    grad_value_sel = jnp.einsum(
        "sphqk,spqhd->sphkd",
        weights_full.astype(jnp.bfloat16),
        grad_shaped,
        preferred_element_type=jnp.float32,
    )
    picker_wide = picker.astype(jnp.float32)
    grad_keys = jnp.einsum(
        "spht,sphkd->stkhd", picker_wide, grad_key_sel, precision=lax.Precision.HIGHEST
    ).reshape(all_keys.shape)
    grad_values = jnp.einsum(
        "spht,sphkd->stkhd", picker_wide, grad_value_sel, precision=lax.Precision.HIGHEST
    ).reshape(all_values.shape)
    return (grad_query.reshape(queries.shape), grad_keys, grad_values)


def layer_forward(hidden_in, weights, picker, live_rows, swapped):
    (
        query_weight,
        key_weight,
        value_weight,
        output_weight,
        query_bias,
        value_bias,
        output_bias,
        expand_weight,
        expand_bias,
        reduce_weight,
        reduce_bias,
        first_gain,
        first_shift,
        second_gain,
        second_shift,
    ) = weights
    seq_count = live_rows.shape[0]
    hidden_low = hidden_in.astype(jnp.bfloat16)
    queries = (matmul(hidden_low, query_weight) + query_bias.astype(jnp.float32)).astype(
        jnp.bfloat16
    )
    key_local = matmul(hidden_low, key_weight).astype(jnp.bfloat16).reshape(seq_count, -1, D)
    value_local = (
        (matmul(hidden_low, value_weight) + value_bias.astype(jnp.float32))
        .astype(jnp.bfloat16)
        .reshape(seq_count, -1, D)
    )
    if swapped:
        all_keys, all_values = side_by_side((key_local, value_local), BLK, 1, 0)
    else:
        all_keys, all_values = neighbour_rows(key_local, value_local)
    mixed_heads, log_total = attend_forward(queries, all_keys, all_values, picker, live_rows)
    mixed_low = mixed_heads.astype(jnp.bfloat16)
    attn_out = matmul(mixed_low, output_weight) + output_bias.astype(jnp.float32)
    first_norm, normed_one, inv_std_one = norm_forward(
        hidden_in + attn_out, first_gain.astype(jnp.float32), first_shift.astype(jnp.float32)
    )
    first_low = first_norm.astype(jnp.bfloat16)
    inner_pre = matmul(first_low, expand_weight) + expand_bias.astype(jnp.float32)
    act_low = jax.nn.gelu(inner_pre, approximate=False).astype(jnp.bfloat16)
    outer_out = matmul(act_low, reduce_weight) + reduce_bias.astype(jnp.float32)
    layer_out, normed_two, inv_std_two = norm_forward(
        first_norm + outer_out, second_gain.astype(jnp.float32), second_shift.astype(jnp.float32)
    )
    saved = (
        hidden_low,
        queries,
        key_local,
        value_local,
        all_keys,
        all_values,
        log_total,
        mixed_low,
        normed_one,
        inv_std_one,
        first_low,
        inner_pre,
        act_low,
        normed_two,
        inv_std_two,
    )
    return (layer_out, saved)


def peer_of(axis, place, offset):
    at = lax.rem(place[axis] + offset, 4)
    if axis == 0:
        return {"dp_0": at}
    if axis == 1:
        return {"dp_1": at}
    return {"dp_2": lax.rem(at, 2), "blk_0": at // 2}


ORDERS = ((0, 1, 2), (1, 2, 0), (2, 0, 1))


def piece(ref, part, at, core):
    z, x, y = at
    if part < 2:
        return ref.at[pl.ds(pl.multiple_of((z * 4 + x) * 48, 16), 48), pl.ds(pl.multiple_of(y * 768 + core * 384, 128), 384)]
    yy = lax.rem(y, 2) * 2 + y // 2
    return ref.at[pl.ds(pl.multiple_of((z * 4 + x) * 192 + yy * 48, 16), 48), pl.ds(pl.multiple_of(core * 384, 128), 384)]


def block(ref, part, a1, core):
    order = ORDERS[part]
    out = []
    for b in range(4):
        for c in range(4):
            at = [None, None, None]
            at[order[0]], at[order[1]], at[order[2]] = a1, b, c
            out.append((piece(ref, part, at, core), (b, c)))
    return out


def scatter_kernel(
    p0, p1, p2, vec,
    q_out, r_out, v_out,
    mine, theirs, got1, sum1, got2, sum2, got3, last, fix_send, fix_got, rfix_send, rfix_got,
    vcore, vy, vz, vx, vsum,
    local_sem, send0, recv0, send1, recv1, send2, recv2, send3, recv3, fsend, frecv, vsend, vrecv,
):
    z, x = lax.axis_index("dp_0"), lax.axis_index("dp_1")
    y_lo, y_hi, core = lax.axis_index("dp_2"), lax.axis_index("blk_0"), lax.axis_index("blk_1")
    place = (z, x, y_hi * 2 + y_lo)
    pos = y_lo * 4 + y_hi * 2 + core
    other = 1 - core
    grads = (p0, p1, p2)

    barrier = pltpu.get_barrier_semaphore()
    peers = [peer_of(a, place, d) for a in (0, 1) for d in (1, 2, 3)]
    for d in range(1, 8):
        t = lax.rem(pos + d, 8)
        peers.append({"dp_2": t // 4, "blk_0": lax.rem(t // 2, 2), "blk_1": lax.rem(t, 2)})
    for p in peers:
        pl.semaphore_signal(barrier, inc=1, device_id=p, device_id_type=MESH)
    pl.semaphore_wait(barrier, len(peers))

    def remote(src, dst, s, r, device):
        return pltpu.make_async_remote_copy(src_ref=src, dst_ref=dst, send_sem=s, recv_sem=r, device_id=device, device_id_type=MESH)

    sibling = {"blk_1": other}
    vc = remote(vec, vcore, vsend.at[0], vrecv.at[0], sibling)
    vc.start()
    halves = {}
    for i in (1, 2, 3, 0):
        for part in range(3):
            a1 = lax.rem(place[ORDERS[part][0]] + i, 4)
            for k, (src, (b, c)) in enumerate(block(grads[part], part, a1, other)):
                halves[part, i, k] = remote(src, theirs.at[part, i, b, c], send0.at[part, i], recv0.at[part, i], sibling)
                halves[part, i, k].start()
            for k, (src, (b, c)) in enumerate(block(grads[part], part, a1, core)):
                pltpu.make_async_copy(src, mine.at[part, i, b, c], local_sem.at[part, i]).start()

    def wait_all(part, i):
        whole = theirs.at[part, i]
        pltpu.make_async_copy(whole, mine.at[part, i], local_sem.at[part, i]).wait()
        remote(whole, whole, send0.at[part, i], recv0.at[part, i], sibling).wait()

    first = {}
    for i in (1, 2, 3, 0):
        for part in range(3):
            wait_all(part, i)

            @pl.loop(0, 16)
            def _(k, part=part, i=i):
                b, c = k // 4, lax.rem(k, 4)
                mine[part, i, b, c] = mine[part, i, b, c] + theirs[part, i, b, c]

            if i:
                first[part, i] = remote(mine.at[part, i], got1.at[part, i - 1], send1.at[part, i - 1], recv1.at[part, i - 1], peer_of(ORDERS[part][0], place, i))
                first[part, i].start()
    vc.wait()
    vsum[...] = vec[...] + vcore[...]
    vys = [remote(vsum, vy.at[d - 1], vsend.at[d], vrecv.at[d], peer_of(2, place, d)) for d in (1, 2, 3)]
    for c in vys:
        c.start()
    second = {}
    for part in range(3):
        for i in (1, 2, 3):
            first[part, i].wait()
        a = ORDERS[part][1]

        @pl.loop(0, 16)
        def _(k, part=part):
            b, c = k // 4, lax.rem(k, 4)
            total = mine[part, 0, b, c].astype(F32) + got1[part, 0, b, c].astype(F32)
            total += got1[part, 1, b, c].astype(F32) + got1[part, 2, b, c].astype(F32)
            sum1[part, b, c] = total.astype(BF)

        for i in (1, 2, 3):
            at = lax.rem(place[a] + i, 4)
            second[part, i] = remote(sum1.at[part, at], got2.at[part, i - 1], send2.at[part, i - 1], recv2.at[part, i - 1], peer_of(a, place, i))
            second[part, i].start()
    for c in vys:
        c.wait()
    vsum[...] = vsum[...] + vy[0] + vy[1] + vy[2]
    vzs = []
    for d in (1, 2, 3):
        at = lax.rem(z + d, 4)
        vzs.append(remote(vsum.at[pl.ds(pl.multiple_of(at * 32, 8), 32)], vz.at[d - 1], vsend.at[3 + d], vrecv.at[3 + d], peer_of(0, place, d)))
        vzs[-1].start()
    third = {}
    for part in range(3):
        for i in (1, 2, 3):
            second[part, i].wait()
        a = ORDERS[part][1]
        own = place[a]
        for c in range(4):
            total = sum1[part, own, c].astype(F32) + got2[part, 0, c].astype(F32)
            total += got2[part, 1, c].astype(F32) + got2[part, 2, c].astype(F32)
            sum2[part, c] = total.astype(BF)
        a = ORDERS[part][2]
        for i in (1, 2, 3):
            at = lax.rem(place[a] + i, 4)
            third[part, i] = remote(sum2.at[part, at], got3.at[part, i - 1], send3.at[part, i - 1], recv3.at[part, i - 1], peer_of(a, place, i))
            third[part, i].start()
    for c in vzs:
        c.wait()
    vrow = vsum[pl.ds(pl.multiple_of(z * 32, 8), 32)] + vz[0] + vz[1] + vz[2]
    vsum[0:32] = vrow
    vxs = []
    for d in (1, 2, 3):
        at = lax.rem(x + d, 4)
        vxs.append(remote(vsum.at[pl.ds(pl.multiple_of(at * 8, 8), 8)], vx.at[d - 1], vsend.at[6 + d], vrecv.at[6 + d], peer_of(1, place, d)))
        vxs[-1].start()
    for part in range(3):
        for i in (1, 2, 3):
            third[part, i].wait()
        own = place[ORDERS[part][2]]
        total = sum2[part, own].astype(F32) + got3[part, 0].astype(F32) + got3[part, 1].astype(F32) + got3[part, 2].astype(F32)
        if part < 2:
            for k in range(8):
                fix_send[k, part, 0:6] = total[6 * k : 6 * k + 6]
        else:
            rfix_send[...] = total
    fixes = []
    for d in range(1, 8):
        t = lax.rem(pos + d, 8)
        device = {"dp_2": t // 4, "blk_0": lax.rem(t // 2, 2), "blk_1": lax.rem(t, 2)}
        fixes.append(remote(fix_send.at[t], fix_got.at[pos], fsend.at[d], frecv.at[d], device))
        fixes[-1].start()
    there = pl.multiple_of(other * 24, 8)
    here = pl.multiple_of(core * 24, 8)
    rfix = remote(rfix_send.at[pl.ds(there, 24)], rfix_got, fsend.at[0], frecv.at[0], sibling)
    rfix.start()
    for c in vxs:
        c.wait()
    v_out[...] = vsum[pl.ds(pl.multiple_of(x * 8, 8), 8)] + vx[0] + vx[1] + vx[2]
    rfix.wait()
    for c in fixes:
        c.wait()
    fix_got[pos] = fix_send[pos]
    for s in range(8):
        y, c = (s // 2 % 2) * 2 + s // 4, s % 2
        for part in range(2):
            q_out[part, y, :, c * 384 : (c + 1) * 384] = fix_got[s, part, 0:6]
    r_out[:, pl.ds(pl.multiple_of(core * 384, 128), 384)] = rfix_send[pl.ds(here, 24)]
    r_out[:, pl.ds(pl.multiple_of(other * 384, 128), 384)] = rfix_got[...]


def reduce_scatter(p0, p1, p2, vec):
    dma = pltpu.SemaphoreType.DMA
    return pl.pallas_call(
        scatter_kernel,
        out_shape=(
            jax.ShapeDtypeStruct((2, 4, 6, 768), F32),
            jax.ShapeDtypeStruct((24, 768), F32),
            jax.ShapeDtypeStruct((8, 128), F32),
        ),
        in_specs=[pl.BlockSpec(memory_space=pl.ANY)] * 3 + [pl.BlockSpec(memory_space=pltpu.VMEM)],
        out_specs=[pl.BlockSpec(memory_space=pltpu.VMEM)] * 3,
        scratch_shapes=[
            pltpu.VMEM((3, 4, 4, 4, 48, 384), BF),
            pltpu.VMEM((3, 4, 4, 4, 48, 384), BF),
            pltpu.VMEM((3, 3, 4, 4, 48, 384), BF),
            pltpu.VMEM((3, 4, 4, 48, 384), BF),
            pltpu.VMEM((3, 3, 4, 48, 384), BF),
            pltpu.VMEM((3, 4, 48, 384), BF),
            pltpu.VMEM((3, 3, 48, 384), BF),
            pltpu.VMEM((8, 128), F32),
            pltpu.VMEM((8, 2, 8, 384), F32),
            pltpu.VMEM((8, 2, 8, 384), F32),
            pltpu.VMEM((48, 384), F32),
            pltpu.VMEM((24, 384), F32),
            pltpu.VMEM((128, 128), F32),
            pltpu.VMEM((3, 128, 128), F32),
            pltpu.VMEM((3, 32, 128), F32),
            pltpu.VMEM((3, 8, 128), F32),
            pltpu.VMEM((128, 128), F32),
            dma((3, 4)), dma((3, 4)), dma((3, 4)),
            dma((3, 3)), dma((3, 3)), dma((3, 3)), dma((3, 3)), dma((3, 3)), dma((3, 3)),
            dma((8,)), dma((8,)), dma((10,)), dma((10,)),
        ],
        compiler_params=pltpu.CompilerParams(collective_id=0, has_side_effects=True, vmem_limit_bytes=56 * 1024 * 1024),
    )(p0, p1, p2, vec)


def reduce_grads(grads):
    (gq, gk, gv, go, gqb, gvb, gob, ge, geb, gr, grb, gfg, gfs, gsg, gss) = grads
    p0 = jnp.concatenate([gq.astype(BF), gk.astype(BF), gv.astype(BF), go.astype(BF)], axis=1)
    vecs = [v.reshape(128, -1) for v in (gqb, gvb, gob, grb, gfg, gfs, gsg, gss, geb)]
    vec = jnp.concatenate(vecs + [jnp.zeros((128, 128 - 72), F32)], axis=1)
    quads, r_rows, v_rows = reduce_scatter(p0, ge.astype(BF), gr.astype(BF), vec)
    pos = lax.axis_index("dp_2") * 4 + lax.axis_index("blk_0") * 2 + lax.axis_index("blk_1")
    row = lax.dynamic_index_in_dim(v_rows, pos, 0, keepdims=False)
    small = [row[6 * i : 6 * i + 6] for i in range(8)]
    e_rows = quads[1].transpose(1, 0, 2).reshape(6, 3072)
    return (
        quads[0, 0], quads[0, 1], quads[0, 2], quads[0, 3], small[0], small[1], small[2],
        e_rows, row[48:72], r_rows, small[3], small[4], small[5], small[6], small[7],
    )


def layer_backward(grad_out, weights, saved, picker, live_rows, swapped):
    (
        query_weight,
        key_weight,
        value_weight,
        output_weight,
        query_bias,
        value_bias,
        output_bias,
        expand_weight,
        expand_bias,
        reduce_weight,
        reduce_bias,
        first_gain,
        first_shift,
        second_gain,
        second_shift,
    ) = weights
    (
        hidden_low,
        queries,
        key_local,
        value_local,
        all_keys,
        all_values,
        log_total,
        mixed_low,
        normed_one,
        inv_std_one,
        first_low,
        inner_pre,
        act_low,
        normed_two,
        inv_std_two,
    ) = saved
    grad_second, grad_second_gain, grad_second_shift = norm_backward(
        grad_out, second_gain.astype(jnp.float32), normed_two, inv_std_two
    )
    grad_outer = grad_second.astype(jnp.bfloat16)
    grad_reduce_weight = contract_rows(act_low, grad_outer)
    grad_reduce_bias = jnp.sum(grad_outer.astype(jnp.float32), axis=0)
    grad_inner = (times_transpose(grad_outer, reduce_weight) * gelu_slope(inner_pre)).astype(
        jnp.bfloat16
    )
    grad_expand_weight = contract_rows(first_low, grad_inner)
    grad_expand_bias = jnp.sum(grad_inner.astype(jnp.float32), axis=0)
    grad_first = grad_second + times_transpose(grad_inner, expand_weight)
    grad_residual, grad_first_gain, grad_first_shift = norm_backward(
        grad_first, first_gain.astype(jnp.float32), normed_one, inv_std_one
    )
    grad_attn = grad_residual.astype(jnp.bfloat16)
    grad_output_weight = contract_rows(mixed_low, grad_attn)
    grad_output_bias = jnp.sum(grad_attn.astype(jnp.float32), axis=0)
    grad_mixed = times_transpose(grad_attn, output_weight).astype(jnp.bfloat16)
    grad_query, grad_keys, grad_values = attend_backward(
        queries, all_keys, all_values, log_total, grad_mixed, picker, live_rows
    )
    if swapped:
        grad_key_local, grad_value_local = tuple(
            (
                part.astype(jnp.float32)
                for part in side_by_side_2(
                    (grad_keys.astype(jnp.bfloat16), grad_values.astype(jnp.bfloat16)), BLK, 1, 0
                )
            )
        )
    else:
        grad_key_local, grad_value_local = return_rims(grad_keys, grad_values, key_local.shape[1])
    query_low = grad_query.astype(jnp.bfloat16)
    key_low = grad_key_local.reshape(-1, D).astype(jnp.bfloat16)
    value_low = grad_value_local.reshape(-1, D).astype(jnp.bfloat16)
    grad_query_weight = contract_rows(hidden_low, query_low)
    grad_key_weight = contract_rows(hidden_low, key_low)
    grad_value_weight = contract_rows(hidden_low, value_low)
    grad_query_bias = jnp.sum(query_low.astype(jnp.float32), axis=0)
    grad_value_bias = jnp.sum(value_low.astype(jnp.float32), axis=0)
    grad_input = (
        grad_residual
        + times_transpose(query_low, query_weight)
        + times_transpose(key_low, key_weight)
        + times_transpose(value_low, value_weight)
    )
    grads = (
        grad_query_weight,
        grad_key_weight,
        grad_value_weight,
        grad_output_weight,
        grad_query_bias,
        grad_value_bias,
        grad_output_bias,
        grad_expand_weight,
        grad_expand_bias,
        grad_reduce_weight,
        grad_reduce_bias,
        grad_first_gain,
        grad_first_shift,
        grad_second_gain,
        grad_second_shift,
    )
    return (grad_input, reduce_grads(grads))


def local(
    hidden,
    output_grad,
    block_counts,
    slot_table,
    block_order_two,
    block_order_three,
    query_weight,
    key_weight,
    value_weight,
    output_weight,
    query_bias,
    value_bias,
    output_bias,
    expand_weight,
    expand_bias,
    reduce_weight,
    reduce_bias,
    first_gain,
    first_shift,
    second_gain,
    second_shift,
):
    seq_count, row_count, model_width = hidden.shape
    piece_rows = row_count // SLOTS
    block_index = lax.axis_index(BLK)
    piece_slot = (SLOTS * block_index + jnp.arange(SLOTS, dtype=jnp.int32)) * piece_rows // BLOCK
    block_number, live_rows = live_pieces(slot_table, block_counts, piece_slot)
    picker_one = selection(
        slot_table, block_counts, block_order_two, block_order_three, block_number, False
    )
    picker_two = selection(
        slot_table, block_counts, block_order_two, block_order_three, block_number, True
    )
    stacked = (
        query_weight,
        key_weight,
        value_weight,
        output_weight,
        query_bias,
        value_bias,
        output_bias,
        expand_weight,
        expand_bias,
        reduce_weight,
        reduce_bias,
        first_gain,
        first_shift,
        second_gain,
        second_shift,
    )
    layer_one = tuple((tensor[0] for tensor in stacked))
    layer_two = tuple((tensor[1] for tensor in stacked))
    hidden_flat = hidden.reshape(-1, model_width).astype(jnp.float32)
    middle, saved_one = layer_forward(hidden_flat, layer_one, picker_one, live_rows, False)
    final_out, saved_two = layer_forward(middle, layer_two, picker_two, live_rows, True)
    grad_middle, reduced_two = layer_backward(
        output_grad.reshape(-1, model_width).astype(jnp.float32),
        layer_two,
        saved_two,
        picker_two,
        live_rows,
        True,
    )
    grad_hidden, reduced_one = layer_backward(
        grad_middle, layer_one, saved_one, picker_one, live_rows, False
    )
    stacked_grads = tuple(
        (
            jnp.stack([first_part, second_part])
            for first_part, second_part in zip(reduced_one, reduced_two)
        )
    )
    return (
        final_out.astype(jnp.bfloat16).reshape(hidden.shape),
        grad_hidden.astype(jnp.bfloat16).reshape(hidden.shape),
    ) + stacked_grads


def solution(mesh):
    finer = Mesh(mesh.devices.reshape(4, 4, 2, 2, 2), ("dp_0", "dp_1", "dp_2", "blk_0", "blk_1"))
    in_specs = (
        P(DP, BLK, None),
        P(DP, BLK, None),
        P(DP),
        P(DP, None),
        P(),
        P(),
        P(),
        P(),
        P(),
        P(),
        P(),
        P(),
        P(),
        P(),
        P(),
        P(),
        P(),
        P(),
        P(),
        P(),
        P(),
    )
    out_specs = (
        P(DP, BLK, None),
        P(DP, BLK, None),
        P(None, DP_BLK, None),
        P(None, DP_BLK, None),
        P(None, DP_BLK, None),
        P(None, DP_BLK, None),
        P(None, DP_BLK),
        P(None, DP_BLK),
        P(None, DP_BLK),
        P(None, DP_BLK, None),
        P(None, DP_BLK),
        P(None, DP_BLK, None),
        P(None, DP_BLK),
        P(None, DP_BLK),
        P(None, DP_BLK),
        P(None, DP_BLK),
        P(None, DP_BLK),
    )
    return jax.shard_map(local, mesh=finer, in_specs=in_specs, out_specs=out_specs, check_vma=False)
```

```python
import functools

import jax
import jax.numpy as jnp
from jax import lax
from jax.experimental import pallas as pl
from jax.experimental.pallas import tpu as pltpu
from jax.sharding import Mesh
from jax.sharding import PartitionSpec as P

D = 768
FF = 3072
HEADS = 12
HD = 64
BLOCK = 512
SLOTS = 3
ROWS = 384
PIECE = 128
CHUNK = 512
BLK = ("blk_0", "blk_1")
DP_BLK = ("dp_0", "dp_1", "dp_2", "blk_0", "blk_1")
DP = ("dp_0", "dp_1", "dp_2")
EPSILON = 1e-06
ROOT_HALF = 0.7071067811865476
INV_ROOT_TAU = 0.3989422804014327
SCALE = HD ** (-0.5)
MESH = pl.DeviceIdType.MESH
BF = jnp.bfloat16
F32 = jnp.float32
MIB = 1024 * 1024
VMEM = pl.BlockSpec(memory_space=pltpu.VMEM)
SMEM = pl.BlockSpec(memory_space=pltpu.SMEM)
ANY = pl.BlockSpec(memory_space=pl.ANY)


def dot(left, right):
    return jnp.dot(left, right, preferred_element_type=F32)


def dot_nt(left, right):
    return lax.dot_general(left, right, (((1,), (1,)), ((), ())), preferred_element_type=F32)


def dot_tn(left, right):
    return lax.dot_general(left, right, (((0,), (0,)), ((), ())), preferred_element_type=F32)


def params(limit=48):
    return pltpu.CompilerParams(vmem_limit_bytes=limit * MIB)


def row_of(ref, layer):
    return ref[layer : layer + 1, :].astype(F32)


def norm_parts(residual):
    mean = jnp.mean(residual, axis=-1, keepdims=True)
    centred = residual - mean
    inv_std = lax.rsqrt(jnp.mean(centred * centred, axis=-1, keepdims=True) + EPSILON)
    return centred * inv_std, inv_std


def norm_backward(grad, gain, normed, inv_std):
    scaled = grad * gain
    return inv_std * (
        scaled
        - jnp.mean(scaled, axis=-1, keepdims=True)
        - normed * jnp.mean(scaled * normed, axis=-1, keepdims=True)
    )


def layer_block(layer, shape, index):
    return pl.BlockSpec((None,) + shape, lambda j: (layer,) + index(j))


def places():
    y_hi, core = lax.axis_index("blk_0"), lax.axis_index("blk_1")
    return y_hi, core, y_hi * 2 + core


def remote(src, dst, send, recv, device):
    return pltpu.make_async_remote_copy(
        src_ref=src, dst_ref=dst, send_sem=send, recv_sem=recv, device_id=device, device_id_type=MESH
    )


def rows_at(start, count):
    return pl.ds(pl.multiple_of(start, PIECE), count)


def greet(devices):
    barrier = pltpu.get_barrier_semaphore()
    for device in devices:
        pl.semaphore_signal(barrier, inc=1, device_id=device, device_id_type=MESH)
    pl.semaphore_wait(barrier, len(devices))


FAR = (256, ROWS)


def far_plan(layer, y_hi, core, block):
    if layer == 0:
        partner = {"blk_0": 1 - y_hi, "blk_1": 1 - core}
        return partner, jnp.where(block == 1, 128, 0), jnp.where(block == 1, 768, 512)
    return {"blk_0": 1 - y_hi}, 0, lax.rem(block + 2, 4) * ROWS


def is_middle(block):
    return jnp.logical_and(block >= 1, block <= 2)


def project_kernel(layer, h, wq, wk, wv, bq, bv, q, kv_all, other, low, kv, far, kv_far, local, send, recv):
    y_hi, core, block = places()
    far_rows = FAR[layer]
    sibling = {"blk_1": 1 - core}
    partner, give, theirs = far_plan(layer, y_hi, core, block)
    low[...] = h[...].astype(BF)
    greet([sibling, partner])
    hidden = remote(low.at[rows_at(give, far_rows)], far, send.at[0], recv.at[0], partner)

    def talk(step):
        if layer == 0:
            pl.when(is_middle(block))(step)
        else:
            step()

    talk(lambda: hidden.start())
    own_place = kv_all.at[:, rows_at(block * ROWS, ROWS)]
    kv[0] = dot(low[...], wk[...]).astype(BF)
    kv[1] = (dot(low[...], wv[...]) + row_of(bv, layer)).astype(BF)
    near = remote(kv, own_place, send.at[1], recv.at[1], sibling)
    near.start()
    keep = pltpu.make_async_copy(kv, own_place, local.at[0])
    keep.start()
    q[...] = (dot(low[...], wq[...]) + row_of(bq, layer)).astype(BF)
    far_place = kv_all.at[:, rows_at(theirs, far_rows)]
    keep_far = pltpu.make_async_copy(kv_far, far_place, local.at[1])

    def far_part():
        hidden.wait()
        other[...] = far[...]
        kv_far[0] = dot(far[...], wk[...]).astype(BF)
        kv_far[1] = (dot(far[...], wv[...]) + row_of(bv, layer)).astype(BF)
        keep_far.start()
        if layer == 1:
            relay = remote(kv_far, far_place, send.at[2], recv.at[2], sibling)
            relay.start()
            relay.wait()
        keep_far.wait()

    talk(far_part)
    if layer == 0:

        @pl.when(jnp.logical_not(is_middle(block)))
        def _():
            other[...] = jnp.zeros_like(other)

    near.wait()
    keep.wait()


def project(layer, h, w):
    whole = layer_block(layer, (D, D), lambda j: (0, 0))
    shape, dma, far_rows = jax.ShapeDtypeStruct, pltpu.SemaphoreType.DMA, FAR[layer]
    q, kv_all, other = pl.pallas_call(
        functools.partial(project_kernel, layer),
        grid=(1,),
        out_shape=(shape((ROWS, D), BF), shape((2, SLOTS * BLOCK, D), BF), shape((far_rows, D), BF)),
        in_specs=[VMEM, whole, whole, whole, VMEM, VMEM],
        out_specs=(VMEM, ANY, VMEM),
        scratch_shapes=[
            pltpu.VMEM((ROWS, D), BF), pltpu.VMEM((2, ROWS, D), BF), pltpu.VMEM((far_rows, D), BF),
            pltpu.VMEM((2, far_rows, D), BF), dma((2,)), dma((3,)), dma((3,)),
        ],
        compiler_params=pltpu.CompilerParams(collective_id=1 + layer, has_side_effects=True, vmem_limit_bytes=48 * MIB),
        name=f"project_{layer}",
    )(h, w["query_weight"], w["key_weight"], w["value_weight"], w["query_bias"], w["value_bias"])
    return q, kv_all.reshape(2, SLOTS, BLOCK, D), other


def project_back_kernel(
    layer, h, other, gq, parts, gres, wq, wk, wv, dw, gh, vec,
    rows, grads, near, far_near, gh_send, gh_got, local, send, recv,
):
    y_hi, core, block = places()
    far_rows = FAR[layer]
    sibling = {"blk_1": 1 - core}
    partner, give, theirs = far_plan(layer, y_hi, core, block)

    def talk(step):
        if layer == 0:
            pl.when(is_middle(block))(step)
        else:
            step()

    greet([sibling, partner])
    beside = y_hi * 2 + 1 - core
    copies = []
    if layer == 1:
        at = (1 - y_hi) * 2 + 1 - core
        copies.append(remote(parts.at[:, rows_at(at * ROWS, ROWS)], far_near, send.at[0], recv.at[0], sibling))
    copies.append(remote(parts.at[:, rows_at(beside * ROWS, ROWS)], near, send.at[1], recv.at[1], sibling))
    own = [
        pltpu.make_async_copy(parts.at[:, rows_at(theirs, far_rows)], grads.at[:, pl.ds(ROWS, far_rows)], local.at[0]),
        pltpu.make_async_copy(parts.at[:, rows_at(block * ROWS, ROWS)], grads.at[:, pl.ds(0, ROWS)], local.at[1]),
    ]
    for c in copies + own:
        c.start()
    rows[0:ROWS] = h[...].astype(BF)
    rows[ROWS:] = other[...]
    dw[:, 0:D] = dot_tn(rows[0:ROWS], gq[...]).astype(BF)
    own[0].wait()
    if layer == 1:
        copies[0].wait()
        grads[:, ROWS:] = (grads[:, ROWS:].astype(F32) + far_near[...].astype(F32)).astype(BF)
    hidden = remote(gh_send, gh_got, send.at[2], recv.at[2], partner)

    def far_part():
        gh_send[...] = (dot_nt(grads[0, ROWS:], wk[...]) + dot_nt(grads[1, ROWS:], wv[...])).astype(BF)
        hidden.start()

    talk(far_part)
    own[1].wait()
    copies[-1].wait()
    grads[:, 0:ROWS] = (grads[:, 0:ROWS].astype(F32) + near[...].astype(F32)).astype(BF)
    dw[:, D : 2 * D] = dot_tn(rows[...], grads[0]).astype(BF)
    dw[:, 2 * D : 3 * D] = dot_tn(rows[...], grads[1]).astype(BF)
    vec[0:1] = jnp.sum(gq[...].astype(F32), axis=0, keepdims=True)
    vec[1:2] = jnp.sum(grads[1].astype(F32), axis=0, keepdims=True)
    total = gres[...] + dot_nt(gq[...], wq[...]) + dot_nt(grads[0, 0:ROWS], wk[...]) + dot_nt(grads[1, 0:ROWS], wv[...])
    if layer == 1:
        hidden.wait()
        gh[...] = (total + gh_got[...].astype(F32)).astype(gh.dtype)
    else:
        gh[...] = total.astype(gh.dtype)

        @pl.when(is_middle(block))
        def _():
            hidden.wait()
            here = rows_at(give, far_rows)
            gh[here, :] = (gh[here, :].astype(F32) + gh_got[...].astype(F32)).astype(gh.dtype)


def project_back(layer, h, other, gq, parts, gres, w, out_type):
    whole = layer_block(layer, (D, D), lambda j: (0, 0))
    shape, dma, far_rows = jax.ShapeDtypeStruct, pltpu.SemaphoreType.DMA, FAR[layer]
    return pl.pallas_call(
        functools.partial(project_back_kernel, layer),
        grid=(1,),
        out_shape=(shape((D, 3 * D), BF), shape((ROWS, D), out_type), shape((2, D), F32)),
        in_specs=[VMEM, VMEM, VMEM, ANY, VMEM] + [whole] * 3,
        out_specs=(VMEM, VMEM, VMEM),
        scratch_shapes=[
            pltpu.VMEM((ROWS + far_rows, D), BF), pltpu.VMEM((2, ROWS + far_rows, D), BF), pltpu.VMEM((2, ROWS, D), BF),
            pltpu.VMEM((2, far_rows, D), BF), pltpu.VMEM((far_rows, D), BF), pltpu.VMEM((far_rows, D), BF),
            dma((2,)), dma((3,)), dma((3,)),
        ],
        compiler_params=pltpu.CompilerParams(collective_id=3 + layer, has_side_effects=True, vmem_limit_bytes=48 * MIB),
        name=f"project_back_{layer}",
    )(h, other, gq, parts.reshape(2, SLOTS * BLOCK, D), gres, w["query_weight"], w["key_weight"], w["value_weight"])


def slots_of(layer, tab, cnt, two, three, piece, head):
    block = lax.axis_index("blk_0") * 2 + lax.axis_index("blk_1")
    t = (3 * block + piece) // 4
    j = jnp.where(tab[0, 1] == t, 1, 0) + jnp.where(tab[0, 2] == t, 2, 0)
    live = jnp.where(j < cnt[0], 1.0, 0.0)
    if layer == 0:
        return t, live
    from_two = jnp.where(j < 2, two[head, jnp.minimum(j, 1)], j)
    chosen = jnp.where(cnt[0] == SLOTS, three[head, j], from_two)
    return tab[0, chosen], live


def two_heads(tile):
    left = lax.broadcasted_iota(jnp.int32, tile.shape, 1) < HD
    none = jnp.zeros_like(tile)
    first = jnp.concatenate([jnp.where(left, tile, none), none], axis=1)
    second = jnp.concatenate([none, jnp.where(left, none, tile)], axis=1)
    return jnp.concatenate([first, second], axis=0)


def own_columns(both):
    left = lax.broadcasted_iota(jnp.int32, (PIECE, 2 * HD), 1) < HD
    return jnp.where(left, both[:PIECE, : 2 * HD], both[PIECE:, 2 * HD :])


def soft(scores):
    top = jnp.max(scores, axis=0, keepdims=True)
    e = jnp.exp((scores - top) * SCALE)
    return e * (1.0 / jnp.sum(e, axis=0, keepdims=True))


def attend_kernel(layer, tab, cnt, two, three, q, k, v, mixed):
    pair = pl.program_id(0)
    for i in range(3):
        rows = pl.ds(i * PIECE, PIECE)
        s0, live = slots_of(layer, tab, cnt, two, three, i, 2 * pair)
        s1, _ = slots_of(layer, tab, cnt, two, three, i, 2 * pair + 1)
        keys = jnp.concatenate([k[s0], k[s1]], axis=1)
        values = jnp.concatenate([v[s0], v[s1]], axis=1)
        weights = soft(dot_nt(keys, two_heads(q[rows, :]))).astype(BF)
        mixed[rows, :] = (own_columns(dot_tn(weights, values)) * live).astype(BF)


def attend_specs():
    tile = pl.BlockSpec((ROWS, 2 * HD), lambda p: (0, p))
    keys = pl.BlockSpec((None, SLOTS, BLOCK, 2 * HD), lambda p: (0, 0, 0, p))
    values = pl.BlockSpec((None, SLOTS, BLOCK, 2 * HD), lambda p: (1, 0, 0, p))
    return tile, keys, values


def attend(layer, table, q, kv_all):
    tile, keys, values = attend_specs()
    return pl.pallas_call(
        functools.partial(attend_kernel, layer),
        grid=(HEADS // 2,),
        out_shape=jax.ShapeDtypeStruct((ROWS, D), BF),
        in_specs=[SMEM] * 4 + [tile, keys, values],
        out_specs=tile,
        compiler_params=params(),
        name=f"attend_{layer}",
    )(*table, q, kv_all, kv_all)


def attend_back_kernel(layer, tab, cnt, two, three, q, k, v, gm, gq, gkv, acc):
    pair = pl.program_id(0)
    acc[...] = jnp.zeros_like(acc)
    for i in range(3):
        rows = pl.ds(i * PIECE, PIECE)
        s0, live = slots_of(layer, tab, cnt, two, three, i, 2 * pair)
        s1, _ = slots_of(layer, tab, cnt, two, three, i, 2 * pair + 1)
        keys = jnp.concatenate([k[s0], k[s1]], axis=1)
        values = jnp.concatenate([v[s0], v[s1]], axis=1)
        qq = two_heads(q[rows, :])
        gg = two_heads((gm[rows, :].astype(F32) * live).astype(BF))
        weights = soft(dot_nt(keys, qq))
        grad_weights = dot_nt(values, gg)
        delta = jnp.sum(weights * grad_weights, axis=0, keepdims=True)
        grad_scores = (weights * (grad_weights - delta)).astype(BF)
        gq[rows, :] = (own_columns(dot_tn(grad_scores, keys)) * SCALE).astype(BF)
        gk = dot(grad_scores, qq) * SCALE
        gv = dot(weights.astype(BF), gg)
        acc[0, s0] += gk[:, : 2 * HD]
        acc[0, s1] += gk[:, 2 * HD :]
        acc[1, s0] += gv[:, : 2 * HD]
        acc[1, s1] += gv[:, 2 * HD :]
    gkv[...] = acc[...].astype(BF)


def attend_back(layer, table, q, kv_all, gm):
    tile, keys, values = attend_specs()
    both = pl.BlockSpec((2, SLOTS, BLOCK, 2 * HD), lambda p: (0, 0, 0, p))
    return pl.pallas_call(
        functools.partial(attend_back_kernel, layer),
        grid=(HEADS // 2,),
        out_shape=(jax.ShapeDtypeStruct((ROWS, D), BF), jax.ShapeDtypeStruct((2, SLOTS, BLOCK, D), BF)),
        in_specs=[SMEM] * 4 + [tile, keys, values, tile],
        out_specs=(tile, both),
        scratch_shapes=[pltpu.VMEM((2, SLOTS, BLOCK, 2 * HD), F32)],
        compiler_params=params(),
        name=f"attend_back_{layer}",
    )(*table, q, kv_all, kv_all, gm)


def tail_kernel(layer, steps, mixed, h, wo, bo, g1, s1, we, be, wr, br, g2, s2, r1, r2, low, out, act, slope, first, total):
    j = pl.program_id(0)

    @pl.when(j == 0)
    def _():
        residual = h[...].astype(F32) + dot(mixed[...], wo[...]) + row_of(bo, layer)
        r1[...] = residual
        normed, _ = norm_parts(residual)
        first[...] = normed * row_of(g1, layer) + row_of(s1, layer)
        low[...] = first[...].astype(BF)
        total[...] = jnp.zeros_like(total)

    inner = dot(low[...], we[...]) + be[layer : layer + 1, pl.ds(pl.multiple_of(j * CHUNK, CHUNK), CHUNK)].astype(F32)
    phi = 0.5 * (1.0 + lax.erf(inner * ROOT_HALF))
    low_act = (inner * phi).astype(BF)
    act[...] = low_act
    slope[...] = (phi + inner * (INV_ROOT_TAU * jnp.exp(-0.5 * inner * inner))).astype(BF)
    total[...] += dot(low_act, wr[...])

    @pl.when(j == steps - 1)
    def _():
        residual = first[...] + total[...] + row_of(br, layer)
        r2[...] = residual
        normed, _ = norm_parts(residual)
        out[...] = (normed * row_of(g2, layer) + row_of(s2, layer)).astype(out.dtype)


def tail(layer, mixed, h, w, out_type):
    steps = FF // CHUNK
    square = layer_block(layer, (D, D), lambda j: (0, 0))
    wide = layer_block(layer, (D, CHUNK), lambda j: (0, j))
    tall = layer_block(layer, (CHUNK, D), lambda j: (j, 0))
    cols = pl.BlockSpec((ROWS, CHUNK), lambda j: (0, j))
    full = pl.BlockSpec((ROWS, D), lambda j: (0, 0))
    vec = VMEM
    rows = lambda t: jax.ShapeDtypeStruct((ROWS, D), t)
    hidden = jax.ShapeDtypeStruct((ROWS, FF), BF)
    return pl.pallas_call(
        functools.partial(tail_kernel, layer, steps),
        grid=(steps,),
        out_shape=(rows(F32), rows(F32), rows(BF), rows(out_type), hidden, hidden),
        in_specs=[full, full, square, vec, vec, vec, wide, vec, tall, vec, vec, vec],
        out_specs=(full, full, full, full, cols, cols),
        scratch_shapes=[pltpu.VMEM((ROWS, D), F32)] * 2,
        compiler_params=params(),
        name=f"tail_{layer}",
    )(mixed, h, w["output_weight"], w["output_bias"], w["first_gain"], w["first_shift"], w["expand_weight"], w["expand_bias"],
      w["reduce_weight"], w["reduce_bias"], w["second_gain"], w["second_shift"])


def tail_back_kernel(
    layer, steps, g, r1, r2, low, act, slope, mixed, wo, we, wr, g1, g2,
    dwr, dwe, dwo, gres, gm, vec, vec_e, gr, go, total,
):
    j = pl.program_id(0)

    @pl.when(j == 0)
    def _():
        grad = g[...].astype(F32)
        normed, inv_std = norm_parts(r2[...])
        grad_r = norm_backward(grad, row_of(g2, layer), normed, inv_std)
        vec[0:1] = jnp.sum(grad * normed, axis=0, keepdims=True)
        vec[1:2] = jnp.sum(grad, axis=0, keepdims=True)
        total[...] = grad_r
        go[...] = grad_r.astype(BF)
        vec[2:3] = jnp.sum(go[...].astype(F32), axis=0, keepdims=True)

    dwr[...] = dot_tn(act[...], go[...]).astype(BF)
    grad_inner = (dot_nt(go[...], wr[...]) * slope[...].astype(F32)).astype(BF)
    vec_e[...] = jnp.sum(grad_inner.astype(F32), axis=0, keepdims=True)
    dwe[...] = dot_tn(low[...], grad_inner).astype(BF)
    total[...] += dot_nt(grad_inner, we[...])

    @pl.when(j == steps - 1)
    def _():
        grad = total[...]
        normed, inv_std = norm_parts(r1[...])
        grad_r = norm_backward(grad, row_of(g1, layer), normed, inv_std)
        vec[3:4] = jnp.sum(grad * normed, axis=0, keepdims=True)
        vec[4:5] = jnp.sum(grad, axis=0, keepdims=True)
        gres[...] = grad_r
        ga = grad_r.astype(BF)
        vec[5:6] = jnp.sum(ga.astype(F32), axis=0, keepdims=True)
        dwo[...] = dot_tn(mixed[...], ga).astype(BF)
        gm[...] = dot_nt(ga, wo[...]).astype(BF)


def tail_back(layer, g, saved, w):
    steps = FF // CHUNK
    square = layer_block(layer, (D, D), lambda j: (0, 0))
    wide = layer_block(layer, (D, CHUNK), lambda j: (0, j))
    tall = layer_block(layer, (CHUNK, D), lambda j: (j, 0))
    cols = pl.BlockSpec((ROWS, CHUNK), lambda j: (0, j))
    full = pl.BlockSpec((ROWS, D), lambda j: (0, 0))
    vec = VMEM
    shape = jax.ShapeDtypeStruct
    return pl.pallas_call(
        functools.partial(tail_back_kernel, layer, steps),
        grid=(steps,),
        out_shape=(
            shape((FF, D), BF), shape((D, FF), BF), shape((D, D), BF), shape((ROWS, D), F32), shape((ROWS, D), BF),
            shape((8, D), F32), shape((1, FF), F32),
        ),
        in_specs=[full, full, full, full, cols, cols, full, square, wide, tall, vec, vec],
        out_specs=(
            pl.BlockSpec((CHUNK, D), lambda j: (j, 0)), pl.BlockSpec((D, CHUNK), lambda j: (0, j)),
            pl.BlockSpec((D, D), lambda j: (0, 0)), full, full,
            pl.BlockSpec((8, D), lambda j: (0, 0)), pl.BlockSpec((1, CHUNK), lambda j: (0, j)),
        ),
        scratch_shapes=[pltpu.VMEM((ROWS, D), F32), pltpu.VMEM((ROWS, D), BF), pltpu.VMEM((ROWS, D), F32)],
        compiler_params=params(),
        name=f"tail_back_{layer}",
    )(g, saved["r1"], saved["r2"], saved["low"], saved["act"], saved["slope"], saved["mixed"],
      w["output_weight"], w["expand_weight"], w["reduce_weight"], w["first_gain"], w["second_gain"])


def peer_of(axis, place, offset):
    at = lax.rem(place[axis] + offset, 4)
    if axis == 0:
        return {"dp_0": at}
    if axis == 1:
        return {"dp_1": at}
    return {"dp_2": lax.rem(at, 2), "blk_0": at // 2}


ORDERS = ((0, 1, 2), (1, 2, 0), (2, 0, 1))


def piece(ref, part, at, core):
    z, x, y = at
    if part == 0:
        ref, y = (ref[0], y) if y < 3 else (ref[1], 0)
    if part < 2:
        return ref.at[pl.ds(pl.multiple_of((z * 4 + x) * 48, 16), 48), pl.ds(pl.multiple_of(y * 768 + core * 384, 128), 384)]
    yy = lax.rem(y, 2) * 2 + y // 2
    return ref.at[pl.ds(pl.multiple_of((z * 4 + x) * 192 + yy * 48, 16), 48), pl.ds(pl.multiple_of(core * 384, 128), 384)]


def block(ref, part, a1, core):
    order = ORDERS[part]
    out = []
    for b in range(4):
        for c in range(4):
            at = [None, None, None]
            at[order[0]], at[order[1]], at[order[2]] = a1, b, c
            out.append((piece(ref, part, at, core), (b, c)))
    return out


def scatter_kernel(
    dw, dwo, p1, p2, vec,
    q_out, r_out, v_out,
    mine, theirs, got1, sum1, got2, sum2, got3, last, fix_send, fix_got, rfix_send, rfix_got,
    vcore, vy, vz, vx, vsum,
    local_sem, send0, recv0, send1, recv1, send2, recv2, send3, recv3, fsend, frecv, vsend, vrecv,
):
    z, x = lax.axis_index("dp_0"), lax.axis_index("dp_1")
    y_lo, y_hi, core = lax.axis_index("dp_2"), lax.axis_index("blk_0"), lax.axis_index("blk_1")
    place = (z, x, y_hi * 2 + y_lo)
    pos = y_lo * 4 + y_hi * 2 + core
    other = 1 - core
    grads = ((dw, dwo), p1, p2)

    barrier = pltpu.get_barrier_semaphore()
    peers = [peer_of(a, place, d) for a in (0, 1) for d in (1, 2, 3)]
    for d in range(1, 8):
        t = lax.rem(pos + d, 8)
        peers.append({"dp_2": t // 4, "blk_0": lax.rem(t // 2, 2), "blk_1": lax.rem(t, 2)})
    for p in peers:
        pl.semaphore_signal(barrier, inc=1, device_id=p, device_id_type=MESH)
    pl.semaphore_wait(barrier, len(peers))

    sibling = {"blk_1": other}
    vc = remote(vec, vcore, vsend.at[0], vrecv.at[0], sibling)
    vc.start()
    halves = {}
    for i in (1, 2, 3, 0):
        for part in range(3):
            a1 = lax.rem(place[ORDERS[part][0]] + i, 4)
            for k, (src, (b, c)) in enumerate(block(grads[part], part, a1, other)):
                halves[part, i, k] = remote(src, theirs.at[part, i, b, c], send0.at[part, i], recv0.at[part, i], sibling)
                halves[part, i, k].start()
            for k, (src, (b, c)) in enumerate(block(grads[part], part, a1, core)):
                pltpu.make_async_copy(src, mine.at[part, i, b, c], local_sem.at[part, i]).start()

    def wait_all(part, i):
        whole = theirs.at[part, i]
        pltpu.make_async_copy(whole, mine.at[part, i], local_sem.at[part, i]).wait()
        remote(whole, whole, send0.at[part, i], recv0.at[part, i], sibling).wait()

    first = {}
    for i in (1, 2, 3, 0):
        for part in range(3):
            wait_all(part, i)

            @pl.loop(0, 16)
            def _(k, part=part, i=i):
                b, c = k // 4, lax.rem(k, 4)
                mine[part, i, b, c] = mine[part, i, b, c] + theirs[part, i, b, c]

            if i:
                first[part, i] = remote(mine.at[part, i], got1.at[part, i - 1], send1.at[part, i - 1], recv1.at[part, i - 1], peer_of(ORDERS[part][0], place, i))
                first[part, i].start()
    vc.wait()
    vsum[...] = vec[...] + vcore[...]
    vys = [remote(vsum, vy.at[d - 1], vsend.at[d], vrecv.at[d], peer_of(2, place, d)) for d in (1, 2, 3)]
    for c in vys:
        c.start()
    second = {}
    for part in range(3):
        for i in (1, 2, 3):
            first[part, i].wait()
        a = ORDERS[part][1]

        @pl.loop(0, 16)
        def _(k, part=part):
            b, c = k // 4, lax.rem(k, 4)
            total = mine[part, 0, b, c].astype(F32) + got1[part, 0, b, c].astype(F32)
            total += got1[part, 1, b, c].astype(F32) + got1[part, 2, b, c].astype(F32)
            sum1[part, b, c] = total.astype(BF)

        for i in (1, 2, 3):
            at = lax.rem(place[a] + i, 4)
            second[part, i] = remote(sum1.at[part, at], got2.at[part, i - 1], send2.at[part, i - 1], recv2.at[part, i - 1], peer_of(a, place, i))
            second[part, i].start()
    for c in vys:
        c.wait()
    vsum[...] = vsum[...] + vy[0] + vy[1] + vy[2]
    vzs = []
    for d in (1, 2, 3):
        at = lax.rem(z + d, 4)
        vzs.append(remote(vsum.at[pl.ds(pl.multiple_of(at * 32, 8), 32)], vz.at[d - 1], vsend.at[3 + d], vrecv.at[3 + d], peer_of(0, place, d)))
        vzs[-1].start()
    third = {}
    for part in range(3):
        for i in (1, 2, 3):
            second[part, i].wait()
        a = ORDERS[part][1]
        own = place[a]
        for c in range(4):
            total = sum1[part, own, c].astype(F32) + got2[part, 0, c].astype(F32)
            total += got2[part, 1, c].astype(F32) + got2[part, 2, c].astype(F32)
            sum2[part, c] = total.astype(BF)
        a = ORDERS[part][2]
        for i in (1, 2, 3):
            at = lax.rem(place[a] + i, 4)
            third[part, i] = remote(sum2.at[part, at], got3.at[part, i - 1], send3.at[part, i - 1], recv3.at[part, i - 1], peer_of(a, place, i))
            third[part, i].start()
    for c in vzs:
        c.wait()
    vrow = vsum[pl.ds(pl.multiple_of(z * 32, 8), 32)] + vz[0] + vz[1] + vz[2]
    vsum[0:32] = vrow
    vxs = []
    for d in (1, 2, 3):
        at = lax.rem(x + d, 4)
        vxs.append(remote(vsum.at[pl.ds(pl.multiple_of(at * 8, 8), 8)], vx.at[d - 1], vsend.at[6 + d], vrecv.at[6 + d], peer_of(1, place, d)))
        vxs[-1].start()
    for part in range(3):
        for i in (1, 2, 3):
            third[part, i].wait()
        own = place[ORDERS[part][2]]
        total = sum2[part, own].astype(F32) + got3[part, 0].astype(F32) + got3[part, 1].astype(F32) + got3[part, 2].astype(F32)
        if part < 2:
            for k in range(8):
                fix_send[k, part, 0:6] = total[6 * k : 6 * k + 6]
        else:
            rfix_send[...] = total
    fixes = []
    for d in range(1, 8):
        t = lax.rem(pos + d, 8)
        device = {"dp_2": t // 4, "blk_0": lax.rem(t // 2, 2), "blk_1": lax.rem(t, 2)}
        fixes.append(remote(fix_send.at[t], fix_got.at[pos], fsend.at[d], frecv.at[d], device))
        fixes[-1].start()
    there = pl.multiple_of(other * 24, 8)
    here = pl.multiple_of(core * 24, 8)
    rfix = remote(rfix_send.at[pl.ds(there, 24)], rfix_got, fsend.at[0], frecv.at[0], sibling)
    rfix.start()
    for c in vxs:
        c.wait()
    v_out[...] = vsum[pl.ds(pl.multiple_of(x * 8, 8), 8)] + vx[0] + vx[1] + vx[2]
    rfix.wait()
    for c in fixes:
        c.wait()
    fix_got[pos] = fix_send[pos]
    for s in range(8):
        y, c = (s // 2 % 2) * 2 + s // 4, s % 2
        for part in range(2):
            q_out[part, y, :, c * 384 : (c + 1) * 384] = fix_got[s, part, 0:6]
    r_out[:, pl.ds(pl.multiple_of(core * 384, 128), 384)] = rfix_send[pl.ds(here, 24)]
    r_out[:, pl.ds(pl.multiple_of(other * 384, 128), 384)] = rfix_got[...]


def reduce_scatter(dw, dwo, p1, p2, vec):
    dma = pltpu.SemaphoreType.DMA
    return pl.pallas_call(
        scatter_kernel,
        out_shape=(
            jax.ShapeDtypeStruct((2, 4, 6, 768), F32),
            jax.ShapeDtypeStruct((24, 768), F32),
            jax.ShapeDtypeStruct((8, 128), F32),
        ),
        in_specs=[ANY] * 4 + [VMEM],
        out_specs=[pl.BlockSpec(memory_space=pltpu.VMEM)] * 3,
        scratch_shapes=[
            pltpu.VMEM((3, 4, 4, 4, 48, 384), BF),
            pltpu.VMEM((3, 4, 4, 4, 48, 384), BF),
            pltpu.VMEM((3, 3, 4, 4, 48, 384), BF),
            pltpu.VMEM((3, 4, 4, 48, 384), BF),
            pltpu.VMEM((3, 3, 4, 48, 384), BF),
            pltpu.VMEM((3, 4, 48, 384), BF),
            pltpu.VMEM((3, 3, 48, 384), BF),
            pltpu.VMEM((8, 128), F32),
            pltpu.VMEM((8, 2, 8, 384), F32),
            pltpu.VMEM((8, 2, 8, 384), F32),
            pltpu.VMEM((48, 384), F32),
            pltpu.VMEM((24, 384), F32),
            pltpu.VMEM((128, 128), F32),
            pltpu.VMEM((3, 128, 128), F32),
            pltpu.VMEM((3, 32, 128), F32),
            pltpu.VMEM((3, 8, 128), F32),
            pltpu.VMEM((128, 128), F32),
            dma((3, 4)), dma((3, 4)), dma((3, 4)),
            dma((3, 3)), dma((3, 3)), dma((3, 3)), dma((3, 3)), dma((3, 3)), dma((3, 3)),
            dma((8,)), dma((8,)), dma((10,)), dma((10,)),
        ],
        compiler_params=pltpu.CompilerParams(collective_id=0, has_side_effects=True, vmem_limit_bytes=56 * 1024 * 1024),
    )(dw, dwo, p1, p2, vec)


def layer_forward(layer, h, table, w, out_type):
    q, kv_all, other = project(layer, h, w)
    mixed = attend(layer, table, q, kv_all)
    r1, r2, low, out, act, slope = tail(layer, mixed, h, w, out_type)
    return out, dict(h=h, other=other, q=q, kv_all=kv_all, mixed=mixed, r1=r1, r2=r2, low=low, act=act, slope=slope)


def layer_backward(layer, g, saved, table, w, out_type):
    dwr, dwe, dwo, gres, gm, vec, vec_e = tail_back(layer, g, saved, w)
    gq, parts = attend_back(layer, table, saved["q"], saved["kv_all"], gm)
    dw, gh, vec_p = project_back(layer, saved["h"], saved["other"], gq, parts, gres, w, out_type)
    small = jnp.concatenate([vec_p, vec[:6]], axis=0).reshape(8, 128, 6).transpose(1, 0, 2).reshape(128, 48)
    packed = jnp.concatenate([small, vec_e.reshape(128, 24), jnp.zeros((128, 56), F32)], axis=1)
    return gh, reduce_scatter(dw, dwo, dwe, dwr, packed)


def finish(parts):
    pos = lax.axis_index("dp_2") * 4 + lax.axis_index("blk_0") * 2 + lax.axis_index("blk_1")
    quads = jnp.stack([p[0] for p in parts])
    r_rows = jnp.stack([p[1] for p in parts])
    row = lax.dynamic_index_in_dim(jnp.stack([p[2] for p in parts]), pos, 1, keepdims=False)
    q_bias, v_bias, s_gain, s_shift, r_bias, f_gain, f_shift, o_bias = [row[:, 6 * i : 6 * i + 6] for i in range(8)]
    square = quads[:, 0]
    e_rows = quads[:, 1].transpose(0, 2, 1, 3).reshape(2, 6, FF)
    return (
        square[:, 0], square[:, 1], square[:, 2], square[:, 3], q_bias, v_bias, o_bias, e_rows, row[:, 48:72],
        r_rows, r_bias, f_gain, f_shift, s_gain, s_shift,
    )


NAMES = (
    "query_weight", "key_weight", "value_weight", "output_weight", "query_bias", "value_bias", "output_bias", "expand_weight",
    "expand_bias", "reduce_weight", "reduce_bias", "first_gain", "first_shift", "second_gain", "second_shift",
)


def local(hidden, output_grad, block_counts, slot_table, block_order_two, block_order_three, *weights):
    w = dict(zip(NAMES, weights))
    table = (slot_table, block_counts, block_order_two, block_order_three)
    middle, saved_one = layer_forward(0, hidden[0], table, w, F32)
    final, saved_two = layer_forward(1, middle, table, w, BF)
    grad_middle, sums_two = layer_backward(1, output_grad[0], saved_two, table, w, F32)
    grad_hidden, sums_one = layer_backward(0, grad_middle, saved_one, table, w, BF)
    return (final[None], grad_hidden[None]) + finish((sums_one, sums_two))


def solution(mesh):
    finer = Mesh(mesh.devices.reshape(4, 4, 2, 2, 2), DP_BLK)
    in_specs = (P(DP, BLK, None), P(DP, BLK, None), P(DP), P(DP, None)) + (P(),) * 17
    wide, flat = P(None, DP_BLK, None), P(None, DP_BLK)
    out_specs = (P(DP, BLK, None), P(DP, BLK, None), wide, wide, wide, wide, flat, flat, flat, wide, flat, wide) + (flat,) * 5
    return jax.shard_map(local, mesh=finer, in_specs=in_specs, out_specs=out_specs, check_vma=False)
```

```python
import functools

import jax
import jax.numpy as jnp
from jax import lax
from jax.experimental import pallas as pl
from jax.experimental.pallas import tpu as pltpu
from jax.sharding import Mesh
from jax.sharding import PartitionSpec as P

D = 768
FF = 3072
HEADS = 12
HD = 64
BLOCK = 512
SLOTS = 3
ROWS = 384
PIECE = 128
CHUNK = 768
HALF = 384
BLK = ("blk_0", "blk_1")
DP_BLK = ("dp_0", "dp_1", "dp_2", "blk_0", "blk_1")
DP = ("dp_0", "dp_1", "dp_2")
EPSILON = 1e-06
ROOT_HALF = 0.7071067811865476
INV_ROOT_TAU = 0.3989422804014327
SCALE = HD ** (-0.5)
MESH = pl.DeviceIdType.MESH
BF = jnp.bfloat16
F32 = jnp.float32
MIB = 1024 * 1024
VMEM = pl.BlockSpec(memory_space=pltpu.VMEM)
SMEM = pl.BlockSpec(memory_space=pltpu.SMEM)
ANY = pl.BlockSpec(memory_space=pl.ANY)


def dot(left, right):
    return jnp.dot(left, right, preferred_element_type=F32)


def dot_nt(left, right):
    return lax.dot_general(left, right, (((1,), (1,)), ((), ())), preferred_element_type=F32)


def dot_tn(left, right):
    return lax.dot_general(left, right, (((0,), (0,)), ((), ())), preferred_element_type=F32)


def params(limit=60):
    return pltpu.CompilerParams(vmem_limit_bytes=limit * MIB)


def row_of(ref, layer):
    return ref[layer : layer + 1, :].astype(F32)


def norm_parts(residual):
    mean = jnp.mean(residual, axis=-1, keepdims=True)
    centred = residual - mean
    inv_std = lax.rsqrt(jnp.mean(centred * centred, axis=-1, keepdims=True) + EPSILON)
    return centred * inv_std, inv_std


def norm_backward(grad, gain, normed, inv_std):
    scaled = grad * gain
    return inv_std * (
        scaled
        - jnp.mean(scaled, axis=-1, keepdims=True)
        - normed * jnp.mean(scaled * normed, axis=-1, keepdims=True)
    )


def layer_block(layer, shape, index):
    return pl.BlockSpec((None,) + shape, lambda j: (layer,) + index(j))


def peer_of(axis, place, offset):
    at = lax.rem(place[axis] + offset, 4)
    if axis == 0:
        return {"dp_0": at}
    if axis == 1:
        return {"dp_1": at}
    return {"dp_2": lax.rem(at, 2), "blk_0": at // 2}


def pos_device(t):
    return {"dp_2": t // 4, "blk_0": lax.rem(t // 2, 2), "blk_1": lax.rem(t, 2)}


def columns_at(start, count):
    return pl.ds(pl.multiple_of(start, 128), count)


STREAM_ORDERS = ((2, 0, 1), (1, 2, 0), (0, 1, 2))
LAYOUT = {"q": (2, 0, 1), "e": (2, 0, 1), "r": (0, 1, 2)}
PIECES = (48, 128)
LEFT = ((4, 4) + PIECES, (4,) + PIECES, PIECES)
WHOLE = (3, 4) + LEFT[0]


def share(group, stage, stream, ref, at):
    order, left = STREAM_ORDERS[stream], list(LAYOUT[group])
    for done in order[:stage]:
        left.remove(done)
    if group == "r" and order[stage] == 2:
        at = lax.rem(at, 2) * 2 + at // 2
    index = [slice(None)] * left.index(order[stage]) + [at]
    return ref.at[(stream, *index)]


def add_up(own, got, out, streams=3):
    count = out.shape[1] * out.shape[2] if len(out.shape) == 5 else out.shape[1]
    for n in range(streams):

        @pl.loop(0, count)
        def _(k, n=n):
            at = (k // 4, lax.rem(k, 4)) if len(out.shape) == 5 else (k,)
            total = own[n](at).astype(F32)
            for d in range(3):
                total += got[(n, d) + at].astype(F32)
            out[(n,) + at] = total.astype(out.dtype)


def chip_place():
    y = lax.axis_index("blk_0") * 2 + lax.axis_index("dp_2")
    return (lax.axis_index("dp_0"), lax.axis_index("dp_1"), y)


def stage_copies(group, stage, source, got, send, recv):
    place = chip_place()
    copies = []
    for d in (2, 1, 3):
        for n in range(3):
            axis = STREAM_ORDERS[n][stage]
            src = share(group, stage, n, source, lax.rem(place[axis] + d, 4))
            copies.append(remote(src, got.at[n, d - 1], send.at[n, d - 1], recv.at[n, d - 1], peer_of(axis, place, d)))
    return copies


def own_share(group, stage, stream, source):
    return share(group, stage, stream, source, chip_place()[STREAM_ORDERS[stream][stage]])


def own_loads(group, stage, source, held, got, got_held, sems):
    out = [pltpu.make_async_copy(own_share(group, stage, n, source), held.at[n], sems.at[n]) for n in range(3)]
    return out + [pltpu.make_async_copy(got, got_held, sems.at[3])]


def add_held(held, got, out):
    add_up([lambda at, n=n: held[(n,) + at] for n in range(3)], got, out)


def add_direct(group, stage, source, got, out):
    views = [own_share(group, stage, n, source) for n in range(3)]
    add_up([lambda at, v=v: v[at] for v in views], got, out)


def axis_peers(axes, offsets=(1, 2, 3)):
    place = chip_place()
    return [peer_of(a, place, d) for a in axes for d in offsets]


def landing(stage):
    return jax.ShapeDtypeStruct((3, 3) + LEFT[stage], BF)


def summed(stage):
    return (3,) + LEFT[stage]


def begin(copies):
    for c in copies:
        c.start()
    return copies


def end(copies):
    for c in copies:
        c.wait()


def pieces_of(grad):
    return [grad[:, k * 128 : (k + 1) * 128].reshape(4, 4, 48, 128) for k in range(3)]


def places():
    y_hi, core = lax.axis_index("blk_0"), lax.axis_index("blk_1")
    return y_hi, core, y_hi * 2 + core


def remote(src, dst, send, recv, device):
    return pltpu.make_async_remote_copy(
        src_ref=src, dst_ref=dst, send_sem=send, recv_sem=recv, device_id=device, device_id_type=MESH
    )


def rows_at(start, count):
    return pl.ds(pl.multiple_of(start, PIECE), count)


def greet(devices):
    barrier = pltpu.get_barrier_semaphore()
    for device in devices:
        pl.semaphore_signal(barrier, inc=1, device_id=device, device_id_type=MESH)
    pl.semaphore_wait(barrier, len(devices))


FAR = (256, ROWS)


def far_plan(layer, y_hi, core, block):
    if layer == 0:
        partner = {"blk_0": 1 - y_hi, "blk_1": 1 - core}
        return partner, jnp.where(block == 1, 128, 0), jnp.where(block == 1, 768, 512)
    return {"blk_0": 1 - y_hi}, 0, lax.rem(block + 2, 4) * ROWS


def is_middle(block):
    return jnp.logical_and(block >= 1, block <= 2)


def project_kernel(layer, h, wq, wk, wv, bq, bv, q, kv_all, rows_all, low, kv, far, kv_far, local, send, recv):
    y_hi, core, block = places()
    far_rows = FAR[layer]
    sibling = {"blk_1": 1 - core}
    partner, give, theirs = far_plan(layer, y_hi, core, block)
    low[...] = h[...].astype(BF)
    greet([sibling, partner])
    hidden = remote(low.at[rows_at(give, far_rows)], far, send.at[0], recv.at[0], partner)

    def talk(step):
        if layer == 0:
            pl.when(is_middle(block))(step)
        else:
            step()

    def both(src, dst, n):
        return [remote(src, dst, send.at[n], recv.at[n], sibling), pltpu.make_async_copy(src, dst, local.at[n])]

    talk(lambda: hidden.start())
    copies = both(low, rows_all.at[core, pl.ds(0, ROWS)], 1)
    kv[0] = dot(low[...], wk[...]).astype(BF)
    kv[1] = (dot(low[...], wv[...]) + row_of(bv, layer)).astype(BF)
    copies += both(kv, kv_all.at[:, rows_at(block * ROWS, ROWS)], 2)
    for c in copies:
        c.start()
    q[...] = (dot(low[...], wq[...]) + row_of(bq, layer)).astype(BF)
    far_place = kv_all.at[:, rows_at(theirs, far_rows)]
    keep_far = pltpu.make_async_copy(kv_far, far_place, local.at[3])

    def far_keys():
        kv_far[0] = dot(far[...], wk[...]).astype(BF)
        kv_far[1] = (dot(far[...], wv[...]) + row_of(bv, layer)).astype(BF)
        keep_far.start()

    talk(lambda: hidden.wait())
    if layer == 0:

        @pl.when(jnp.logical_not(is_middle(block)))
        def _():
            far[...] = jnp.zeros_like(far)

    last = both(far, rows_all.at[core, pl.ds(ROWS, far_rows)], 4)
    for c in last:
        c.start()
    talk(far_keys)
    if layer == 1:
        relay = remote(kv_far, far_place, send.at[3], recv.at[3], sibling)
        relay.start()
        relay.wait()
    talk(lambda: keep_far.wait())
    for c in copies + last:
        c.wait()


def project(layer, h, w):
    whole = layer_block(layer, (D, D), lambda j: (0, 0))
    shape, dma, far_rows = jax.ShapeDtypeStruct, pltpu.SemaphoreType.DMA, FAR[layer]
    q, kv_all, rows_all = pl.pallas_call(
        functools.partial(project_kernel, layer),
        grid=(1,),
        out_shape=(shape((ROWS, D), BF), shape((2, SLOTS * BLOCK, D), BF), shape((2, ROWS + far_rows, D), BF)),
        in_specs=[VMEM, whole, whole, whole, VMEM, VMEM],
        out_specs=(VMEM, ANY, ANY),
        scratch_shapes=[
            pltpu.VMEM((ROWS, D), BF), pltpu.VMEM((2, ROWS, D), BF), pltpu.VMEM((far_rows, D), BF),
            pltpu.VMEM((2, far_rows, D), BF), dma((5,)), dma((5,)), dma((5,)),
        ],
        compiler_params=pltpu.CompilerParams(collective_id=1 + layer, has_side_effects=True, vmem_limit_bytes=60 * MIB),
        name=f"project_{layer}",
    )(h, w["query_weight"], w["key_weight"], w["value_weight"], w["query_bias"], w["value_bias"])
    return q, kv_all.reshape(2, SLOTS, BLOCK, D), rows_all


def project_back_body(layer, rows, gq, parts, gres, dwo, wq, wk, wv, p0, gh, scratch, peers, carry, squares_done):
    grads, near, far_near, gh_send, gh_got, qcat, kvcat, local, send, recv = scratch
    y_hi, core, block = places()
    far_rows = FAR[layer]
    sibling = {"blk_1": 1 - core}
    partner, give, theirs = far_plan(layer, y_hi, core, block)
    mine = columns_at(core * HALF, HALF)
    yours = columns_at((1 - core) * HALF, HALF)

    def talk(step):
        if layer == 0:
            pl.when(is_middle(block))(step)
        else:
            step()

    greet(peers or [sibling, partner] + axis_peers((0, 1, 2), (1, 2, 3)))
    beside = y_hi * 2 + 1 - core
    copies = []
    if layer == 1:
        at = (1 - y_hi) * 2 + 1 - core
        copies.append(remote(parts.at[:, rows_at(at * ROWS, ROWS)], far_near, send.at[0], recv.at[0], sibling))
    copies.append(remote(parts.at[:, rows_at(beside * ROWS, ROWS)], near, send.at[1], recv.at[1], sibling))
    half_q = remote(gq.at[:, yours], qcat.at[core], send.at[3], recv.at[3], sibling)
    own = [
        pltpu.make_async_copy(parts.at[:, rows_at(theirs, far_rows)], grads.at[:, pl.ds(ROWS, far_rows)], local.at[0]),
        pltpu.make_async_copy(parts.at[:, rows_at(block * ROWS, ROWS)], grads.at[:, pl.ds(0, ROWS)], local.at[1]),
    ]
    begin(copies + own + [half_q])
    qcat[core] = gq[:, mine]

    def place_square(y, grad):
        for k, piece in enumerate(pieces_of(grad)):
            p0[k, y] = piece

    place_square(3, dwo[...])
    own[0].wait()
    if layer == 1:
        copies[0].wait()
        grads[:, ROWS:] = (grads[:, ROWS:].astype(F32) + far_near[...].astype(F32)).astype(BF)
    hidden = remote(gh_send, gh_got, send.at[2], recv.at[2], partner)

    def far_part():
        gh_send[...] = (dot_nt(grads[0, ROWS:], wk[...]) + dot_nt(grads[1, ROWS:], wv[...])).astype(BF)
        hidden.start()

    talk(far_part)
    own[1].wait()
    copies[-1].wait()
    grads[:, 0:ROWS] = (grads[:, 0:ROWS].astype(F32) + near[...].astype(F32)).astype(BF)
    half_kv = remote(grads.at[:, :, yours], kvcat.at[:, core], send.at[4], recv.at[4], sibling)
    half_kv.start()
    kvcat[:, core] = grads[:, :, mine]
    carry()
    half_q.wait()
    place_square(0, (dot_tn(rows[0, 0:ROWS], qcat[0]) + dot_tn(rows[1, 0:ROWS], qcat[1])).astype(BF))
    half_kv.wait()
    for side in (0, 1):
        cat = kvcat[side].reshape(2 * (ROWS + far_rows), HALF)
        place_square(1 + side, dot_tn(rows[...].reshape(2 * (ROWS + far_rows), D), cat).astype(BF))
    squares_done()
    total = gres[...] + dot_nt(gq[...], wq[...]) + dot_nt(grads[0, 0:ROWS], wk[...]) + dot_nt(grads[1, 0:ROWS], wv[...])
    if layer == 1:
        hidden.wait()
        gh[...] = (total + gh_got[...].astype(F32)).astype(gh.dtype)
    else:
        gh[...] = total.astype(gh.dtype)

        @pl.when(is_middle(block))
        def _():
            hidden.wait()
            here = rows_at(give, far_rows)
            gh[here, :] = (gh[here, :].astype(F32) + gh_got[...].astype(F32)).astype(gh.dtype)


def project_back_scratch(layer):
    far_rows, dma = FAR[layer], pltpu.SemaphoreType.DMA
    return [
        pltpu.VMEM((2, ROWS + far_rows, D), BF), pltpu.VMEM((2, ROWS, D), BF),
        pltpu.VMEM((2, far_rows, D), BF), pltpu.VMEM((far_rows, D), BF), pltpu.VMEM((far_rows, D), BF),
        pltpu.VMEM((2, ROWS, HALF), BF), pltpu.VMEM((2, 2, ROWS + far_rows, HALF), BF),
        dma((2,)), dma((5,)), dma((5,)),
    ]


def own_scratch(stage):
    return pltpu.VMEM(summed(stage), BF)


def got_scratch(stage):
    return pltpu.VMEM((3, 3) + LEFT[stage], BF)


def project_back_two_kernel(
    rows, gq, parts, gres, dwo, wq, wk, wv, e0, got_e0, r0, got_r0, p0, gh, s_e, got_e, s_r, got_r, *refs
):
    scratch, (own_e, own_r, held_e, held_r, csems, csend, crecv) = refs[:10], refs[10:]
    loads_e = begin(own_loads("e", 0, e0, own_e, got_e0, held_e, csems.at[0]))
    loads_r = begin(own_loads("r", 0, r0, own_r, got_r0, held_r, csems.at[1]))
    carried = []

    def carry():
        end(loads_e)
        add_held(own_e, held_e, s_e)
        carried.extend(begin(stage_copies("e", 1, s_e, got_e, csend.at[0], crecv.at[0])))
        end(loads_r)
        add_held(own_r, held_r, s_r)
        carried.extend(begin(stage_copies("r", 1, s_r, got_r, csend.at[1], crecv.at[1])))

    project_back_body(1, rows, gq, parts, gres, dwo, wq, wk, wv, p0, gh, scratch, None, carry, lambda: None)
    end(carried)


def project_back_two(rows_all, gq, parts, gres, dwo, w, carry):
    whole = layer_block(1, (D, D), lambda j: (0, 0))
    shape, dma = jax.ShapeDtypeStruct, pltpu.SemaphoreType.DMA
    return pl.pallas_call(
        project_back_two_kernel,
        grid=(1,),
        out_shape=(shape(WHOLE, BF), shape((ROWS, D), F32)) + (shape(summed(0), BF), landing(1)) * 2,
        in_specs=[VMEM, VMEM, ANY, VMEM, VMEM] + [whole] * 3 + [ANY] * 4,
        out_specs=(VMEM, VMEM, VMEM, ANY, VMEM, ANY),
        scratch_shapes=project_back_scratch(1)
        + [own_scratch(0)] * 2 + [got_scratch(0)] * 2 + [dma((2, 4)), dma((2, 3, 3)), dma((2, 3, 3))],
        compiler_params=pltpu.CompilerParams(collective_id=4, has_side_effects=True, vmem_limit_bytes=60 * MIB),
        name="project_back_1",
    )(rows_all, gq, parts.reshape(2, SLOTS * BLOCK, D), gres, dwo, w["query_weight"], w["key_weight"], w["value_weight"], *carry)


def slots_of(layer, tab, cnt, two, three, piece, head):
    block = lax.axis_index("blk_0") * 2 + lax.axis_index("blk_1")
    t = (3 * block + piece) // 4
    j = jnp.where(tab[0, 1] == t, 1, jnp.where(tab[0, 2] == t, 2, 0))
    live = jnp.where(j < cnt[0], 1.0, 0.0)
    if layer == 0:
        return t, live
    from_two = jnp.where(j < 2, two[head, jnp.minimum(j, 1)], j)
    chosen = jnp.where(cnt[0] == SLOTS, three[head, j], from_two)
    return tab[0, chosen], live


def left_lanes(rows=1):
    return lax.broadcasted_iota(jnp.int32, (rows, 2 * HD), 1) < HD


def two_heads(tile):
    left, none = left_lanes(PIECE), jnp.zeros_like(tile)
    return jnp.concatenate([jnp.where(left, tile, none), jnp.where(left, none, tile)], axis=0)


def own_columns(both):
    return jnp.where(left_lanes(PIECE), both[:PIECE], both[PIECE:])


def slot_mask(s0, s1, t, kind):
    first, second = jnp.where(s0 == t, 1.0, 0.0), jnp.where(s1 == t, 1.0, 0.0)
    return jnp.where(left_lanes(), first, second).astype(kind)


def soft(scores):
    top = jnp.max(scores, axis=0, keepdims=True)
    e = jnp.exp((scores - top) * SCALE)
    return e * (1.0 / jnp.sum(e, axis=0, keepdims=True))


def attend_kernel(layer, tab, cnt, two, three, q, k, v, mixed):
    pair = pl.program_id(0)
    left = left_lanes(BLOCK)
    for i in range(3):
        rows = pl.ds(i * PIECE, PIECE)
        s0, live = slots_of(layer, tab, cnt, two, three, i, 2 * pair)
        if layer == 0:
            keys, values = k[s0], v[s0]
        else:
            s1, _ = slots_of(layer, tab, cnt, two, three, i, 2 * pair + 1)
            keys, values = jnp.where(left, k[s0], k[s1]), jnp.where(left, v[s0], v[s1])
        weights = soft(dot_nt(keys, two_heads(q[rows, :]))).astype(BF)
        mixed[rows, :] = (own_columns(dot_tn(weights, values)) * live).astype(BF)


def attend_specs():
    tile = pl.BlockSpec((ROWS, 2 * HD), lambda p: (0, p))
    keys = pl.BlockSpec((None, SLOTS, BLOCK, 2 * HD), lambda p: (0, 0, 0, p))
    values = pl.BlockSpec((None, SLOTS, BLOCK, 2 * HD), lambda p: (1, 0, 0, p))
    return tile, keys, values


def attend(layer, table, q, kv_all):
    tile, keys, values = attend_specs()
    return pl.pallas_call(
        functools.partial(attend_kernel, layer),
        grid=(HEADS // 2,),
        out_shape=jax.ShapeDtypeStruct((ROWS, D), BF),
        in_specs=[SMEM] * 4 + [tile, keys, values],
        out_specs=tile,
        compiler_params=params(),
        name=f"attend_{layer}",
    )(*table, q, kv_all, kv_all)


def attend_back_step(layer, tab, cnt, two, three, q, k, v, gm, gq, gkv, acc):
    pair = pl.program_id(0)
    masks = []
    if layer == 0:
        acc[...] = jnp.zeros_like(acc)
    for i in range(3):
        rows = pl.ds(i * PIECE, PIECE)
        s0, live = slots_of(layer, tab, cnt, two, three, i, 2 * pair)
        if layer == 0:
            keys, values = k[s0], v[s0]
        else:
            s1, _ = slots_of(layer, tab, cnt, two, three, i, 2 * pair + 1)
            low = [slot_mask(s0, s1, t, BF) for t in range(SLOTS)]
            masks.append([slot_mask(s0, s1, t, F32) for t in range(SLOTS)])
            keys = k[0] * low[0] + k[1] * low[1] + k[2] * low[2]
            values = v[0] * low[0] + v[1] * low[1] + v[2] * low[2]
        qq = two_heads(q[rows, :])
        gg = two_heads((gm[rows, :].astype(F32) * live).astype(BF))
        weights = soft(dot_nt(keys, qq))
        grad_weights = dot_nt(values, gg)
        delta = jnp.sum(weights * grad_weights, axis=0, keepdims=True)
        grad_scores = (weights * (grad_weights - delta)).astype(BF)
        gq[rows, :] = (own_columns(dot_tn(grad_scores, keys)) * SCALE).astype(BF)
        gk = dot(grad_scores, qq) * SCALE
        gv = dot(weights.astype(BF), gg)
        if layer == 0:
            acc[0, s0] += gk
            acc[1, s0] += gv
        else:
            acc[0, i] = gk
            acc[1, i] = gv
    if layer == 0:
        gkv[...] = acc[...].astype(BF)
    else:
        for side in range(2):
            for t in range(SLOTS):
                total = acc[side, 0] * masks[0][t] + acc[side, 1] * masks[1][t] + acc[side, 2] * masks[2][t]
                gkv[side, t] = total.astype(BF)


def attend_back_kernel(layer, tab, cnt, two, three, q, k, v, gm, e, gq, gkv, vec, got_e, acc, send, recv):
    step = pl.program_id(0)

    def carried():
        return stage_copies("e", 0, e, got_e, send, recv)

    @pl.when(step == 0)
    def _():
        greet(axis_peers((0, 1, 2)))
        begin(carried())

    attend_back_step(layer, tab, cnt, two, three, q, k, v, gm, gq, gkv, acc)
    vec[0:1] = jnp.sum(gq[...].astype(F32), axis=0, keepdims=True)
    total = jnp.zeros((1, 2 * HD), F32)
    for i in range(3):
        _, live = slots_of(0, tab, cnt, two, three, i, 0)
        total += live * jnp.sum(gm[i * PIECE : (i + 1) * PIECE, :].astype(F32), axis=0, keepdims=True)
    vec[1:2] = total

    @pl.when(step == HEADS // 2 - 1)
    def _():
        end(carried())


def attend_back(layer, table, q, kv_all, gm, e):
    tile, keys, values = attend_specs()
    both = pl.BlockSpec((2, SLOTS, BLOCK, 2 * HD), lambda p: (0, 0, 0, p))
    shape, dma = jax.ShapeDtypeStruct, pltpu.SemaphoreType.DMA
    return pl.pallas_call(
        functools.partial(attend_back_kernel, layer),
        grid=(HEADS // 2,),
        out_shape=(shape((ROWS, D), BF), shape((2, SLOTS, BLOCK, D), BF), shape((2, D), F32), landing(0)),
        in_specs=[SMEM] * 4 + [tile, keys, values, tile, ANY],
        out_specs=(tile, both, pl.BlockSpec((2, 2 * HD), lambda p: (0, p)), ANY),
        scratch_shapes=[pltpu.VMEM((2, SLOTS, BLOCK, 2 * HD), F32), dma((3, 3)), dma((3, 3))],
        compiler_params=pltpu.CompilerParams(collective_id=9 + layer, has_side_effects=True, vmem_limit_bytes=60 * MIB),
        name=f"attend_back_{layer}",
    )(*table, q, kv_all, kv_all, gm, e)


STEPS = FF // CHUNK


def tail_kernel(
    layer, mixed, h, wo, bo, g1, s1, we, be, wr, br, g2, s2, r1, r2, out, slope, act_all, low_all, mixed_all,
    first, total, low, act, local, send, recv,
):
    j = pl.program_id(0)
    core = lax.axis_index("blk_1")
    sibling = {"blk_1": 1 - core}

    def both(src, dst, n):
        return [remote(src, dst, send.at[n], recv.at[n], sibling), pltpu.make_async_copy(src, dst, local.at[n])]

    def act_copies(at):
        return both(act.at[at], act_all.at[core, :, columns_at(at * CHUNK, CHUNK)], at)

    early = both(mixed, mixed_all.at[core], STEPS) + both(low, low_all.at[core], STEPS + 1)

    @pl.when(j == 0)
    def _():
        barrier = pltpu.get_barrier_semaphore()
        pl.semaphore_signal(barrier, inc=1, device_id=sibling, device_id_type=MESH)
        residual = h[...].astype(F32) + dot(mixed[...], wo[...]) + row_of(bo, layer)
        r1[...] = residual
        normed, _ = norm_parts(residual)
        first[...] = normed * row_of(g1, layer) + row_of(s1, layer)
        low[...] = first[...].astype(BF)
        total[...] = jnp.zeros_like(total)
        pl.semaphore_wait(barrier, 1)
        for c in early:
            c.start()

    inner = dot(low[...], we[...]) + be[layer : layer + 1, columns_at(j * CHUNK, CHUNK)].astype(F32)
    phi = 0.5 * (1.0 + lax.erf(inner * ROOT_HALF))
    low_act = (inner * phi).astype(BF)
    act[j] = low_act
    for c in act_copies(j):
        c.start()
    slope[...] = (phi + inner * (INV_ROOT_TAU * jnp.exp(-0.5 * inner * inner))).astype(BF)
    total[...] += dot(low_act, wr[...])

    @pl.when(j == STEPS - 1)
    def _():
        residual = first[...] + total[...] + row_of(br, layer)
        r2[...] = residual
        normed, _ = norm_parts(residual)
        out[...] = (normed * row_of(g2, layer) + row_of(s2, layer)).astype(out.dtype)
        for c in early:
            c.wait()
        for at in range(STEPS):
            for c in act_copies(at):
                c.wait()


def tail(layer, mixed, h, w, out_type):
    square = layer_block(layer, (D, D), lambda j: (0, 0))
    wide = layer_block(layer, (D, CHUNK), lambda j: (0, j))
    tall = layer_block(layer, (CHUNK, D), lambda j: (j, 0))
    full = pl.BlockSpec((ROWS, D), lambda j: (0, 0))
    vec, dma = VMEM, pltpu.SemaphoreType.DMA
    shape = jax.ShapeDtypeStruct
    return pl.pallas_call(
        functools.partial(tail_kernel, layer),
        grid=(STEPS,),
        out_shape=(
            shape((ROWS, D), F32), shape((ROWS, D), F32), shape((ROWS, D), out_type), shape((ROWS, FF), BF),
            shape((2, ROWS, FF), BF), shape((2, ROWS, D), BF), shape((2, ROWS, D), BF),
        ),
        in_specs=[full, full, square, vec, vec, vec, wide, vec, tall, vec, vec, vec],
        out_specs=(full, full, full, pl.BlockSpec((ROWS, CHUNK), lambda j: (0, j)), ANY, ANY, ANY),
        scratch_shapes=[
            pltpu.VMEM((ROWS, D), F32), pltpu.VMEM((ROWS, D), F32), pltpu.VMEM((ROWS, D), BF),
            pltpu.VMEM((STEPS, ROWS, CHUNK), BF), dma((STEPS + 2,)), dma((STEPS + 2,)), dma((STEPS + 2,)),
        ],
        compiler_params=pltpu.CompilerParams(collective_id=5 + layer, has_side_effects=True, vmem_limit_bytes=60 * MIB),
        name=f"tail_{layer}",
    )(mixed, h, w["output_weight"], w["output_bias"], w["first_gain"], w["first_shift"], w["expand_weight"], w["expand_bias"],
      w["reduce_weight"], w["reduce_bias"], w["second_gain"], w["second_shift"])


def tail_back_kernel(layer, g, r1, r2, low_all, act_all, slope, mixed_all, wo, we, wr, g1, g2, *refs):
    refs = list(refs)

    def take(count):
        out, refs[:count] = refs[:count], []
        return out

    q_in = take(1) if layer == 0 else []
    dwr, dwe, dwo, gres, gm, vec, vec_e, got_r = take(8)
    got_q = take(1) if layer == 0 else []
    go, ga, gi, total, gocat, gacat, gicat, send, recv, rsend, rrecv = take(11)
    place = chip_place()

    def square_copies():
        return stage_copies("q", 0, q_in[0], got_q[0], *refs) if layer == 0 else []

    def reduce_copies(at):
        out = []
        for d in (2, 1, 3):
            for n, axis in ((0, 2), (1, 1)):
                to = lax.rem(place[axis] + d, 4)
                src = dwr.at[0, at, :, lax.rem(to, 2) * 2 + to // 2] if n == 0 else dwr.at[1, at, to]
                out.append(
                    remote(src, got_r.at[n, d - 1, at], rsend.at[n, d - 1, at], rrecv.at[n, d - 1, at], peer_of(axis, place, d))
                )
        return out

    def reduce_along_z(d):
        to = lax.rem(place[0] + d, 4)
        return remote(dwr.at[2, to], got_r.at[2, d - 1], rsend.at[2, d - 1, 0], rrecv.at[2, d - 1, 0], peer_of(0, place, d))

    j = pl.program_id(0)
    core = lax.axis_index("blk_1")
    sibling = {"blk_1": 1 - core}
    mine, yours = columns_at(core * HALF, HALF), columns_at((1 - core) * HALF, HALF)

    def share_go():
        return remote(go.at[:, yours], gocat.at[core], send.at[STEPS], recv.at[STEPS], sibling)

    def share_ga():
        return remote(ga.at[:, yours], gacat.at[core], send.at[STEPS + 1], recv.at[STEPS + 1], sibling)

    def share_gi(at):
        return remote(gi.at[at, :, yours], gicat.at[at, core], send.at[at], recv.at[at], sibling)

    @pl.when(j == 0)
    def _():
        barrier = pltpu.get_barrier_semaphore()
        peers = [sibling] + axis_peers((0, 1, 2))
        for peer in peers:
            pl.semaphore_signal(barrier, inc=1, device_id=peer, device_id_type=MESH)
        grad = g[...].astype(F32)
        normed, inv_std = norm_parts(r2[...])
        grad_r = norm_backward(grad, row_of(g2, layer), normed, inv_std)
        vec[0:1] = jnp.sum(grad * normed, axis=0, keepdims=True)
        vec[1:2] = jnp.sum(grad, axis=0, keepdims=True)
        total[...] = grad_r
        go[...] = grad_r.astype(BF)
        vec[2:3] = jnp.sum(go[...].astype(F32), axis=0, keepdims=True)
        pl.semaphore_wait(barrier, len(peers))
        share_go().start()
        begin(square_copies())
        gocat[core] = go[:, mine]

    @pl.when(j < STEPS)
    def _():
        grad_inner = (dot_nt(go[...], wr[...]) * slope[...].astype(F32)).astype(BF)
        gi[j] = grad_inner
        share_gi(j).start()
        gicat[j, core] = gi[j, :, mine]
        vec_e[...] = jnp.sum(grad_inner.astype(F32), axis=0, keepdims=True)
        total[...] += dot_nt(grad_inner, we[...])

        @pl.when(j == 0)
        def _():
            share_go().wait()

        grad = dot_tn(act_all[...].reshape(2 * ROWS, CHUNK), gocat[...].reshape(2 * ROWS, HALF)).astype(BF)
        for k, piece in enumerate(pieces_of(grad)):
            dwr[k, j] = piece
        begin(reduce_copies(j))
        for d in (1, 2, 3):

            @pl.when(lax.rem(place[0] + d, 4) == j)
            def _(d=d):
                reduce_along_z(d).start()

    @pl.when(j == STEPS - 1)
    def _():
        grad = total[...]
        normed, inv_std = norm_parts(r1[...])
        grad_r = norm_backward(grad, row_of(g1, layer), normed, inv_std)
        vec[3:4] = jnp.sum(grad * normed, axis=0, keepdims=True)
        vec[4:5] = jnp.sum(grad, axis=0, keepdims=True)
        gres[...] = grad_r
        ga[...] = grad_r.astype(BF)
        vec[5:6] = jnp.sum(ga[...].astype(F32), axis=0, keepdims=True)
        share_ga().start()
        gacat[core] = ga[:, mine]

    @pl.when(j > 0)
    def _():
        share_gi(j - 1).wait()
        grad = dot_tn(low_all[...].reshape(2 * ROWS, D), gicat[j - 1].reshape(2 * ROWS, HALF)).astype(BF)
        for k, piece in enumerate(pieces_of(grad)):
            dwe[k, 0] = piece

    @pl.when(j == STEPS)
    def _():
        gm[...] = dot_nt(ga[...], wo[...]).astype(BF)
        share_ga().wait()
        dwo[...] = dot_tn(mixed_all[...].reshape(2 * ROWS, D), gacat[...].reshape(2 * ROWS, HALF)).astype(BF)
        end(square_copies() + [reduce_along_z(d) for d in (1, 2, 3)])
        for at in range(STEPS):
            end(reduce_copies(at))


def tail_back(layer, g, saved, w, carry=()):
    at = lambda j: jnp.minimum(j, STEPS - 1)
    square = layer_block(layer, (D, D), lambda j: (0, 0))
    wide = layer_block(layer, (D, CHUNK), lambda j: (0, at(j)))
    tall = layer_block(layer, (CHUNK, D), lambda j: (at(j), 0))
    full = pl.BlockSpec((ROWS, D), lambda j: (0, 0))
    pair = pl.BlockSpec((2, ROWS, D), lambda j: (0, 0, 0))
    vec, dma = VMEM, pltpu.SemaphoreType.DMA
    shape = jax.ShapeDtypeStruct
    return pl.pallas_call(
        functools.partial(tail_back_kernel, layer),
        grid=(STEPS + 1,),
        out_shape=(
            shape(WHOLE, BF), shape(WHOLE, BF), shape((D, HALF), BF), shape((ROWS, D), F32), shape((ROWS, D), BF),
            shape((8, D), F32), shape((1, FF), F32), landing(0),
        )
        + ((landing(0),) if carry else ()),
        in_specs=[
            full, full, full, pair, pl.BlockSpec((2, ROWS, CHUNK), lambda j: (0, 0, at(j))),
            pl.BlockSpec((ROWS, CHUNK), lambda j: (0, at(j))), pair, square, wide, tall, vec, vec,
        ]
        + [ANY] * len(carry),
        out_specs=(
            VMEM,
            pl.BlockSpec((3, 1) + LEFT[0], lambda j: (0, jnp.maximum(j - 1, 0), 0, 0, 0, 0)),
            pl.BlockSpec((D, HALF), lambda j: (0, 0)), full, full,
            pl.BlockSpec((8, D), lambda j: (0, 0)), pl.BlockSpec((1, CHUNK), lambda j: (0, at(j))), ANY,
        )
        + ((ANY,) if carry else ()),
        scratch_shapes=[
            pltpu.VMEM((ROWS, D), BF), pltpu.VMEM((ROWS, D), BF), pltpu.VMEM((STEPS, ROWS, CHUNK), BF), pltpu.VMEM((ROWS, D), F32),
            pltpu.VMEM((2, ROWS, HALF), BF), pltpu.VMEM((2, ROWS, HALF), BF), pltpu.VMEM((STEPS, 2, ROWS, HALF), BF),
            dma((STEPS + 2,)), dma((STEPS + 2,)), dma((3, 3, STEPS)), dma((3, 3, STEPS)),
        ]
        + ([dma((3, 3)), dma((3, 3))] if carry else []),
        compiler_params=pltpu.CompilerParams(collective_id=7 + layer, has_side_effects=True, vmem_limit_bytes=60 * MIB),
        name=f"tail_back_{layer}",
    )(g, saved["r1"], saved["r2"], saved["low_all"], saved["act_all"], saved["slope"], saved["mixed_all"],
      w["output_weight"], w["expand_weight"], w["reduce_weight"], w["first_gain"], w["second_gain"], *carry)


VECTORS = 24


def last_kernel(*refs):
    refs = list(refs)

    def take(count):
        out, refs[:count] = refs[:count], []
        return out

    rows, gq, parts, gres, dwo, wq, wk, wv = take(8)
    e0, got_e0, r0, got_r0, q0_two, got_q0_two, e1_two, got_e1_two, r1_two, got_r1_two = take(10)
    vec_p, vec, vec_e, vec_p_two, vec_two, vec_e_two = take(6)
    gh, q_out, r_out, v_out = take(4)
    scratch = take(10)
    p0, got_q0, own_q0, s_q0, got_q1, s_q1, got_q2 = take(7)
    own_e0, held_e0, s_e0, got_e1, s_e1, got_e2 = take(6)
    own_r0, held_r0, s_r0, got_r1, s_r1, got_r2 = take(6)
    own_q0_two, held_q0_two, s_q0_two, got_q1_two, s_q1_two, got_q2_two = take(6)
    own_e1_two, held_e1_two, s_e1_two, got_e2_two = take(4)
    own_r1_two, held_r1_two, s_r1_two, got_r2_two = take(4)
    fix_send, fix_got, rfix_send, rfix_got, vsum, vgot, vtotal, vz, vx = take(9)
    local, send, recv, fsend, frecv, vsend, vrecv = take(7)

    place = chip_place()
    core = lax.axis_index("blk_1")
    pos = lax.axis_index("dp_2") * 4 + lax.axis_index("blk_0") * 2 + core
    other = 1 - core
    sibling = {"blk_1": other}
    loads = [
        begin(own_loads("e", 0, e0, own_e0, got_e0, held_e0, local.at[0])),
        begin(own_loads("r", 0, r0, own_r0, got_r0, held_r0, local.at[1])),
        begin(own_loads("q", 0, q0_two, own_q0_two, got_q0_two, held_q0_two, local.at[2])),
        begin(own_loads("e", 1, e1_two, own_e1_two, got_e1_two, held_e1_two, local.at[3])),
        begin(own_loads("r", 1, r1_two, own_r1_two, got_r1_two, held_r1_two, local.at[4])),
    ]
    vectors = [vec_p[0:1], vec_p[1:2]] + [vec[k : k + 1] for k in range(6)]
    vectors += [vec_p_two[0:1], vec_p_two[1:2]] + [vec_two[k : k + 1] for k in range(6)]
    vectors += [v[:, k * D : (k + 1) * D] for v in (vec_e, vec_e_two) for k in range(4)]
    for k, vector in enumerate(vectors):
        vsum[k // 3, k % 3 : k % 3 + 1] = vector
    for k in range(8):
        vsum[k, 3:8] = jnp.zeros((5, D), F32)
    flights = {}

    def launch(key, group, stage, source, got, n):
        flights[key] = begin(stage_copies(group, stage, source, got, send.at[n], recv.at[n]))

    def to_all(source, dest, at):
        out = []
        for d in range(1, 8):
            t = lax.rem(pos + d, 8)
            out.append(remote(source(t), dest.at[pos], vsend.at[at + d], vrecv.at[at + d], pos_device(t)))
        return begin(out)

    def along(axis, got, at):
        return begin([remote(vtotal, got.at[d - 1], vsend.at[at + d], vrecv.at[at + d], peer_of(axis, place, d)) for d in (1, 2, 3)])

    def carry():
        vc = to_all(lambda t: vsum.at[t], vgot, 0)
        end(loads[0])
        add_held(own_e0, held_e0, s_e0)
        end(vc)
        vgot[pos] = vsum[pos]
        total = vgot[0]
        for k in range(1, 8):
            total = total + vgot[k]
        vtotal[...] = total
        vzs = along(0, vz, 7)
        launch("e1", "e", 1, s_e0, got_e1, 0)
        end(loads[1])
        add_held(own_r0, held_r0, s_r0)
        end(vzs)
        vtotal[...] = vtotal[...] + vz[0] + vz[1] + vz[2]
        flights["vx"] = along(1, vx, 10)
        launch("r1", "r", 1, s_r0, got_r1, 1)
        end(loads[2])
        add_held(own_q0_two, held_q0_two, s_q0_two)
        launch("q1_two", "q", 1, s_q0_two, got_q1_two, 2)
        end(loads[3])
        add_held(own_e1_two, held_e1_two, s_e1_two)
        launch("e2_two", "e", 2, s_e1_two, got_e2_two, 3)
        end(loads[4])
        add_held(own_r1_two, held_r1_two, s_r1_two)
        launch("r2_two", "r", 2, s_r1_two, got_r2_two, 4)

    def squares_done():
        launch("q0", "q", 0, p0, got_q0, 5)

    peers = axis_peers((0, 1)) + [pos_device(lax.rem(pos + d, 8)) for d in range(1, 8)]
    project_back_body(0, rows, gq, parts, gres, dwo, wq, wk, wv, p0, gh, scratch, peers, carry, squares_done)

    def last(group, source, got):
        thirds = []
        for n in range(3):
            total = own_share(group, 2, n, source)[...].astype(F32)
            for d in range(3):
                total += got[n, d].astype(F32)
            thirds.append(total)
        return jnp.concatenate(thirds, axis=1)

    def rows_out(layer, square, expand, reduce):
        for k in range(8):
            fix_send[layer, k, 0, 0:6] = square[6 * k : 6 * k + 6]
            fix_send[layer, k, 1, 0:6] = expand[6 * k : 6 * k + 6]
        rfix_send[layer] = reduce
        out = []
        for d in range(1, 8):
            t = lax.rem(pos + d, 8)
            out.append(
                remote(fix_send.at[layer, t], fix_got.at[layer, pos], fsend.at[layer, d], frecv.at[layer, d], pos_device(t))
            )
        there = pl.ds(pl.multiple_of(other * 24, 8), 24)
        out.append(remote(rfix_send.at[layer, there], rfix_got.at[layer], fsend.at[layer, 0], frecv.at[layer, 0], sibling))
        return begin(out)

    end(flights["vx"])
    vtotal[...] = vtotal[...] + vx[0] + vx[1] + vx[2]
    vc = to_all(lambda t: vtotal, v_out, 13)
    end(flights["q1_two"])
    add_direct("q", 1, s_q0_two, got_q1_two, s_q1_two)
    launch("q2_two", "q", 2, s_q1_two, got_q2_two, 6)
    end(flights["e1"])
    add_direct("e", 1, s_e0, got_e1, s_e1)
    launch("e2", "e", 2, s_e1, got_e2, 7)
    end(flights["r1"])
    add_direct("r", 1, s_r0, got_r1, s_r1)
    launch("r2", "r", 2, s_r1, got_r2, 8)
    for n in range(3):
        own_q0[n] = own_share("q", 0, n, p0)[...]
    end(flights["e2_two"] + flights["r2_two"] + flights["q2_two"])
    fixes = rows_out(
        1, last("q", s_q1_two, got_q2_two), last("e", s_e1_two, got_e2_two), last("r", s_r1_two, got_r2_two)
    )
    end(flights["e2"] + flights["r2"])
    expand, reduce = last("e", s_e1, got_e2), last("r", s_r1, got_r2)
    end(flights["q0"])
    add_held(own_q0, got_q0, s_q0)
    launch("q1", "q", 1, s_q0, got_q1, 9)
    end(vc)
    v_out[pos] = vtotal[...]
    end(flights["q1"])
    add_direct("q", 1, s_q0, got_q1, s_q1)
    launch("q2", "q", 2, s_q1, got_q2, 10)
    end(flights["q2"])
    fixes += rows_out(0, last("q", s_q1, got_q2), expand, reduce)
    end(fixes)
    for layer in range(2):
        fix_got[layer, pos] = fix_send[layer, pos]
        for s in range(8):
            at, c = (s // 2 % 2) * 2 + s // 4, s % 2
            for part in range(2):
                q_out[layer, part, at, :, c * HALF : (c + 1) * HALF] = fix_got[layer, s, part, 0:6]
        here = pl.ds(pl.multiple_of(core * 24, 8), 24)
        r_out[layer, :, columns_at(core * HALF, HALF)] = rfix_send[layer, here]
        r_out[layer, :, columns_at(other * HALF, HALF)] = rfix_got[layer]


def last_step(rows_all, gq, parts, gres, dwo, w, carry, vecs):
    whole = layer_block(0, (D, D), lambda j: (0, 0))
    dma, shape = pltpu.SemaphoreType.DMA, jax.ShapeDtypeStruct
    own, got = own_scratch, got_scratch
    return pl.pallas_call(
        last_kernel,
        grid=(1,),
        out_shape=(shape((ROWS, D), BF), shape((2, 2, 4, 6, D), F32), shape((2, 24, D), F32), shape((8, 8, D), F32)),
        in_specs=[VMEM, VMEM, ANY, VMEM, VMEM] + [whole] * 3 + [ANY] * 10 + [VMEM] * 6,
        out_specs=[VMEM] * 4,
        scratch_shapes=project_back_scratch(0)
        + [pltpu.VMEM(WHOLE, BF), got(0), own(0), own(0), got(1), own(1), got(2)]
        + [own(0), got(0), own(0), got(1), own(1), got(2)] * 3
        + [own(1), got(1), own(1), got(2)] * 2
        + [
            pltpu.VMEM((2, 8, 2, 8, HALF), F32),
            pltpu.VMEM((2, 8, 2, 8, HALF), F32),
            pltpu.VMEM((2, 48, HALF), F32),
            pltpu.VMEM((2, 24, HALF), F32),
            pltpu.VMEM((8, 8, D), F32),
            pltpu.VMEM((8, 8, D), F32),
            pltpu.VMEM((8, D), F32),
            pltpu.VMEM((3, 8, D), F32),
            pltpu.VMEM((3, 8, D), F32),
            dma((5, 4)), dma((11, 3, 3)), dma((11, 3, 3)), dma((2, 8)), dma((2, 8)), dma((21,)), dma((21,)),
        ],
        compiler_params=pltpu.CompilerParams(collective_id=3, has_side_effects=True, vmem_limit_bytes=60 * MIB),
        name="last_step",
    )(rows_all, gq, parts.reshape(2, SLOTS * BLOCK, D), gres, dwo, w["query_weight"], w["key_weight"], w["value_weight"], *carry, *vecs)


def layer_forward(layer, h, table, w, out_type):
    q, kv_all, rows_all = project(layer, h, w)
    mixed = attend(layer, table, q, kv_all)
    r1, r2, out, slope, act_all, low_all, mixed_all = tail(layer, mixed, h, w, out_type)
    return out, dict(
        rows_all=rows_all, q=q, kv_all=kv_all, r1=r1, r2=r2, slope=slope, act_all=act_all, low_all=low_all, mixed_all=mixed_all
    )


def finish_kernel(quads, rows, vecs, final, grad, *outs):
    me = lax.axis_index(DP_BLK)
    wq, wk, wv, wo, we, wr, q_b, v_b, s_g, s_s, r_b, f_g, f_s, o_b, e_b, final_out, grad_out = outs
    final_out[...] = final[...]
    grad_out[...] = grad[...]
    for layer in range(2):
        for y, out in enumerate((wq, wk, wv, wo)):
            out[:, layer] = quads[layer, 0, y]
        for y in range(4):
            we[:, layer, y * D : (y + 1) * D] = quads[layer, 1, y]
    wr[...] = rows[...]
    vectors = [vecs[k // 3, k % 3 : k % 3 + 1] for k in range(VECTORS)]
    turned = pltpu.roll(jnp.concatenate(vectors[0:16], axis=0), lax.rem(D - 6 * me, D), 1)
    for n, out in enumerate((q_b, v_b, s_g, s_s, r_b, f_g, f_s, o_b)):
        for layer in range(2):
            out[layer : layer + 1] = turned[8 * layer + n : 8 * layer + n + 1, 0:6]
    wide = pltpu.roll(jnp.concatenate(vectors[16:24], axis=0), lax.rem(D - 24 * lax.rem(me, 32), D), 1)
    for layer in range(2):
        total = jnp.zeros((1, 24), F32)
        for k in range(4):
            total = total + jnp.where(me // 32 == k, wide[4 * layer + k : 4 * layer + k + 1, 0:24], 0.0)
        e_b[layer : layer + 1] = total


def finish(quads, rows, vecs, final, grad):
    shape = jax.ShapeDtypeStruct
    square, small, hidden = shape((6, 2, D), F32), shape((2, 6), F32), shape((1, ROWS, D), BF)
    outs = pl.pallas_call(
        finish_kernel,
        out_shape=(square,) * 4 + (shape((6, 2, FF), F32), shape((2, 24, D), F32)) + (small,) * 8 + (shape((2, 24), F32),)
        + (hidden, hidden),
        in_specs=[VMEM] * 5,
        out_specs=(VMEM,) * 17,
        name="finish",
    )(quads, rows, vecs, final[None], grad[None])
    wq, wk, wv, wo, we = [o.transpose(1, 0, 2) for o in outs[:5]]
    wr, q_b, v_b, s_g, s_s, r_b, f_g, f_s, o_b, e_b, final, grad = outs[5:]
    return (final, grad, wq, wk, wv, wo, q_b, v_b, o_b, we, e_b, wr, r_b, f_g, f_s, s_g, s_s)


NAMES = (
    "query_weight", "key_weight", "value_weight", "output_weight", "query_bias", "value_bias", "output_bias", "expand_weight",
    "expand_bias", "reduce_weight", "reduce_bias", "first_gain", "first_shift", "second_gain", "second_shift",
)


def local(hidden, output_grad, block_counts, slot_table, block_order_two, block_order_three, *weights):
    w = dict(zip(NAMES, weights))
    table = (slot_table, block_counts, block_order_two, block_order_three)
    middle, saved_one = layer_forward(0, hidden[0], table, w, F32)
    final, saved_two = layer_forward(1, middle, table, w, BF)
    r_two, e_two, dwo, gres, gm, vec_two, vec_e_two, got_r = tail_back(1, output_grad[0], saved_two, w)
    gq, parts, vec_p_two, got_e = attend_back(1, table, saved_two["q"], saved_two["kv_all"], gm, e_two)
    carry = (e_two, got_e, r_two, got_r)
    q_two, grad_middle, e1, got_e, r1, got_r = project_back_two(saved_two["rows_all"], gq, parts, gres, dwo, w, carry)
    r0, e0, dwo, gres, gm, vec, vec_e, got_r0, got_q = tail_back(0, grad_middle, saved_one, w, (q_two,))
    gq, parts, vec_p, got_e0 = attend_back(0, table, saved_one["q"], saved_one["kv_all"], gm, e0)
    carry = (e0, got_e0, r0, got_r0, q_two, got_q, e1, got_e, r1, got_r)
    vecs = (vec_p, vec, vec_e, vec_p_two, vec_two, vec_e_two)
    grad_hidden, *sums = last_step(saved_one["rows_all"], gq, parts, gres, dwo, w, carry, vecs)
    return finish(*sums, final, grad_hidden)


def solution(mesh):
    finer = Mesh(mesh.devices.reshape(4, 4, 2, 2, 2), DP_BLK)
    in_specs = (P(DP, BLK, None), P(DP, BLK, None), P(DP), P(DP, None)) + (P(),) * 17
    wide, flat = P(None, DP_BLK, None), P(None, DP_BLK)
    out_specs = (P(DP, BLK, None), P(DP, BLK, None), wide, wide, wide, wide, flat, flat, flat, wide, flat, wide) + (flat,) * 5
    return jax.shard_map(local, mesh=finer, in_specs=in_specs, out_specs=out_specs, check_vma=False)
```

```python
import functools

import jax
import jax.numpy as jnp
from jax import lax
from jax.experimental import pallas as pl
from jax.experimental.pallas import tpu as pltpu
from jax.sharding import Mesh
from jax.sharding import PartitionSpec as P

D = 768
FF = 3072
HEADS = 12
HD = 64
BLOCK = 512
SLOTS = 3
ROWS = 384
PIECE = 128
CHUNK = 768
HALF = 384
BLK = ("blk_0", "blk_1")
DP_BLK = ("dp_0", "dp_1", "dp_2", "blk_0", "blk_1")
DP = ("dp_0", "dp_1", "dp_2")
EPSILON = 1e-06
ROOT_HALF = 0.7071067811865476
INV_ROOT_TAU = 0.3989422804014327
SCALE = HD ** (-0.5)
MESH = pl.DeviceIdType.MESH
BF = jnp.bfloat16
F32 = jnp.float32
MIB = 1024 * 1024
VMEM = pl.BlockSpec(memory_space=pltpu.VMEM)
SMEM = pl.BlockSpec(memory_space=pltpu.SMEM)
ANY = pl.BlockSpec(memory_space=pl.ANY)


def dot(left, right):
    return jnp.dot(left, right, preferred_element_type=F32)


def dot_nt(left, right):
    return lax.dot_general(left, right, (((1,), (1,)), ((), ())), preferred_element_type=F32)


def dot_tn(left, right):
    return lax.dot_general(left, right, (((0,), (0,)), ((), ())), preferred_element_type=F32)


def params(limit=60):
    return pltpu.CompilerParams(vmem_limit_bytes=limit * MIB)


def row_of(ref, layer):
    return ref[layer : layer + 1, :].astype(F32)


def norm_parts(residual):
    mean = jnp.mean(residual, axis=-1, keepdims=True)
    centred = residual - mean
    inv_std = lax.rsqrt(jnp.mean(centred * centred, axis=-1, keepdims=True) + EPSILON)
    return centred * inv_std, inv_std


def norm_backward(grad, gain, normed, inv_std):
    scaled = grad * gain
    return inv_std * (
        scaled
        - jnp.mean(scaled, axis=-1, keepdims=True)
        - normed * jnp.mean(scaled * normed, axis=-1, keepdims=True)
    )


def layer_block(layer, shape, index):
    return pl.BlockSpec((None,) + shape, lambda j: (layer,) + index(j))


def peer_of(axis, place, offset):
    at = lax.rem(place[axis] + offset, 4)
    if axis == 0:
        return {"dp_0": at}
    if axis == 1:
        return {"dp_1": at}
    return {"dp_2": lax.rem(at, 2), "blk_0": at // 2}


def pos_device(t):
    return {"dp_2": t // 4, "blk_0": lax.rem(t // 2, 2), "blk_1": lax.rem(t, 2)}


def columns_at(start, count):
    return pl.ds(pl.multiple_of(start, 128), count)


STREAM_ORDERS = ((2, 0, 1), (1, 2, 0), (0, 1, 2))
LAYOUT = {"q": (2, 0, 1), "e": (2, 0, 1), "r": (0, 1, 2)}
PIECES = (48, 128)
LEFT = ((4, 4) + PIECES, (4,) + PIECES, PIECES)
WHOLE = (3, 4) + LEFT[0]


def share(group, stage, stream, ref, at):
    order, left = STREAM_ORDERS[stream], list(LAYOUT[group])
    for done in order[:stage]:
        left.remove(done)
    if group == "r" and order[stage] == 2:
        at = lax.rem(at, 2) * 2 + at // 2
    index = [slice(None)] * left.index(order[stage]) + [at]
    return ref.at[(stream, *index)]


def add_up(own, got, out, streams=3):
    count = out.shape[1] * out.shape[2] if len(out.shape) == 5 else out.shape[1]
    for n in range(streams):

        @pl.loop(0, count)
        def _(k, n=n):
            at = (k // 4, lax.rem(k, 4)) if len(out.shape) == 5 else (k,)
            total = own[n](at).astype(F32)
            for d in range(3):
                total += got[(n, d) + at].astype(F32)
            out[(n,) + at] = total.astype(out.dtype)


def chip_place():
    y = lax.axis_index("blk_0") * 2 + lax.axis_index("dp_2")
    return (lax.axis_index("dp_0"), lax.axis_index("dp_1"), y)


def stage_copies(group, stage, source, got, send, recv):
    place = chip_place()
    copies = []
    for d in (2, 1, 3):
        for n in range(3):
            axis = STREAM_ORDERS[n][stage]
            src = share(group, stage, n, source, lax.rem(place[axis] + d, 4))
            copies.append(remote(src, got.at[n, d - 1], send.at[n, d - 1], recv.at[n, d - 1], peer_of(axis, place, d)))
    return copies


def own_share(group, stage, stream, source):
    return share(group, stage, stream, source, chip_place()[STREAM_ORDERS[stream][stage]])


def own_loads(group, stage, source, held, got, got_held, sems):
    out = [pltpu.make_async_copy(own_share(group, stage, n, source), held.at[n], sems.at[n]) for n in range(3)]
    return out + [pltpu.make_async_copy(got, got_held, sems.at[3])]


def add_held(held, got, out):
    add_up([lambda at, n=n: held[(n,) + at] for n in range(3)], got, out)


def add_direct(group, stage, source, got, out):
    views = [own_share(group, stage, n, source) for n in range(3)]
    add_up([lambda at, v=v: v[at] for v in views], got, out)


def axis_peers(axes, offsets=(1, 2, 3)):
    place = chip_place()
    return [peer_of(a, place, d) for a in axes for d in offsets]


def landing(stage):
    return jax.ShapeDtypeStruct((3, 3) + LEFT[stage], BF)


def summed(stage):
    return (3,) + LEFT[stage]


def begin(copies):
    for c in copies:
        c.start()
    return copies


def end(copies):
    for c in copies:
        c.wait()


class Late:
    def __init__(self, source, held, sem):
        self.copy, self.held, self.waited = pltpu.make_async_copy(source, held, sem), held, False
        self.copy.start()

    def __call__(self):
        if not self.waited:
            self.copy.wait()
            self.waited = True
        return self.held


def pieces_of(grad):
    return [grad[:, k * 128 : (k + 1) * 128].reshape(4, 4, 48, 128) for k in range(3)]


def places():
    y_hi, core = lax.axis_index("blk_0"), lax.axis_index("blk_1")
    return y_hi, core, y_hi * 2 + core


def remote(src, dst, send, recv, device):
    return pltpu.make_async_remote_copy(
        src_ref=src, dst_ref=dst, send_sem=send, recv_sem=recv, device_id=device, device_id_type=MESH
    )


def rows_at(start, count):
    return pl.ds(pl.multiple_of(start, PIECE), count)


def greet(devices):
    barrier = pltpu.get_barrier_semaphore()
    for device in devices:
        pl.semaphore_signal(barrier, inc=1, device_id=device, device_id_type=MESH)
    pl.semaphore_wait(barrier, len(devices))


FAR = (256, ROWS)


def far_plan(layer, y_hi, core, block):
    if layer == 0:
        partner = {"blk_0": 1 - y_hi, "blk_1": 1 - core}
        return partner, jnp.where(block == 1, 128, 0), jnp.where(block == 1, 768, 512)
    return {"blk_0": 1 - y_hi}, 0, lax.rem(block + 2, 4) * ROWS


def is_middle(block):
    return jnp.logical_and(block >= 1, block <= 2)


def project_kernel(
    layer, h, wq, wk, wv, bq, bv, q, kv_all, rows_all, low, kv, far, kv_far, held_q, held_k, held_v, late, local, send, recv
):
    wk, wv = Late(wk.at[layer], held_k, late.at[0]), Late(wv.at[layer], held_v, late.at[1])
    wq = Late(wq.at[layer], held_q, late.at[2])
    y_hi, core, block = places()
    far_rows = FAR[layer]
    sibling = {"blk_1": 1 - core}
    partner, give, theirs = far_plan(layer, y_hi, core, block)
    low[...] = h[...].astype(BF)
    greet([sibling, partner])
    hidden = remote(low.at[rows_at(give, far_rows)], far, send.at[0], recv.at[0], partner)

    def talk(step):
        if layer == 0:
            pl.when(is_middle(block))(step)
        else:
            step()

    def both(src, dst, n):
        return [remote(src, dst, send.at[n], recv.at[n], sibling), pltpu.make_async_copy(src, dst, local.at[n])]

    talk(lambda: hidden.start())
    copies = both(low, rows_all.at[core, pl.ds(0, ROWS)], 1)
    kv[0] = dot(low[...], wk()[...]).astype(BF)
    kv[1] = (dot(low[...], wv()[...]) + row_of(bv, layer)).astype(BF)
    copies += both(kv, kv_all.at[:, rows_at(block * ROWS, ROWS)], 2)
    for c in copies:
        c.start()
    q[...] = (dot(low[...], wq()[...]) + row_of(bq, layer)).astype(BF)
    far_place = kv_all.at[:, rows_at(theirs, far_rows)]
    keep_far = pltpu.make_async_copy(kv_far, far_place, local.at[3])

    def far_keys():
        kv_far[0] = dot(far[...], wk()[...]).astype(BF)
        kv_far[1] = (dot(far[...], wv()[...]) + row_of(bv, layer)).astype(BF)
        keep_far.start()

    talk(lambda: hidden.wait())
    if layer == 0:

        @pl.when(jnp.logical_not(is_middle(block)))
        def _():
            far[...] = jnp.zeros_like(far)

    last = both(far, rows_all.at[core, pl.ds(ROWS, far_rows)], 4)
    for c in last:
        c.start()
    talk(far_keys)
    if layer == 1:
        relay = remote(kv_far, far_place, send.at[3], recv.at[3], sibling)
        relay.start()
        relay.wait()
    talk(lambda: keep_far.wait())
    for c in copies + last:
        c.wait()


def project(layer, h, w):
    shape, dma, far_rows = jax.ShapeDtypeStruct, pltpu.SemaphoreType.DMA, FAR[layer]
    q, kv_all, rows_all = pl.pallas_call(
        functools.partial(project_kernel, layer),
        out_shape=(shape((ROWS, D), BF), shape((2, SLOTS * BLOCK, D), BF), shape((2, ROWS + far_rows, D), BF)),
        in_specs=[VMEM, ANY, ANY, ANY, VMEM, VMEM],
        out_specs=(VMEM, ANY, ANY),
        scratch_shapes=[
            pltpu.VMEM((ROWS, D), BF), pltpu.VMEM((2, ROWS, D), BF), pltpu.VMEM((far_rows, D), BF),
            pltpu.VMEM((2, far_rows, D), BF), pltpu.VMEM((D, D), BF), pltpu.VMEM((D, D), BF), pltpu.VMEM((D, D), BF), dma((3,)),
            dma((5,)), dma((5,)), dma((5,)),
        ],
        compiler_params=pltpu.CompilerParams(collective_id=1 + layer, has_side_effects=True, vmem_limit_bytes=60 * MIB),
        name=f"project_{layer}",
    )(h, w["query_weight"], w["key_weight"], w["value_weight"], w["query_bias"], w["value_bias"])
    return q, kv_all.reshape(2, SLOTS, BLOCK, D), rows_all


def project_back_body(layer, rows, gq, parts, gres, dwo, wq, wk, wv, p0, gh, scratch, peers, hooks):
    (
        grads, near, far_near, gh_send, gh_got, qcat, kvcat, local, send, recv,
        held_rows, held_gq, held_gres, held_dwo, held_q, held_k, held_v, late,
    ) = scratch
    y_hi, core, block = places()
    far_rows = FAR[layer]
    sibling = {"blk_1": 1 - core}
    partner, give, theirs = far_plan(layer, y_hi, core, block)
    mine = columns_at(core * HALF, HALF)
    yours = columns_at((1 - core) * HALF, HALF)

    def hook(name):
        if name in hooks:
            hooks[name]()

    def talk(step):
        if layer == 0:
            pl.when(is_middle(block))(step)
        else:
            step()

    own = begin(
        [
            pltpu.make_async_copy(parts.at[:, rows_at(theirs, far_rows)], grads.at[:, pl.ds(ROWS, far_rows)], local.at[0]),
            pltpu.make_async_copy(parts.at[:, rows_at(block * ROWS, ROWS)], grads.at[:, pl.ds(0, ROWS)], local.at[1]),
            pltpu.make_async_copy(gq.at[:, mine], qcat.at[core], local.at[2]),
        ]
    )
    wk, wv = Late(wk.at[layer], held_k, late.at[0]), Late(wv.at[layer], held_v, late.at[1])
    dwo, rows = Late(dwo, held_dwo, late.at[2]), Late(rows, held_rows, late.at[3])
    gq_held, wq = Late(gq, held_gq, late.at[4]), Late(wq.at[layer], held_q, late.at[5])
    gres = Late(gres, held_gres, late.at[6])
    hook("loads")
    greet(peers or [sibling, partner] + axis_peers((0, 1, 2), (1, 2, 3)))
    beside = y_hi * 2 + 1 - core
    copies = []
    if layer == 1:
        at = (1 - y_hi) * 2 + 1 - core
        copies.append(remote(parts.at[:, rows_at(at * ROWS, ROWS)], far_near, send.at[0], recv.at[0], sibling))
    copies.append(remote(parts.at[:, rows_at(beside * ROWS, ROWS)], near, send.at[1], recv.at[1], sibling))
    half_q = remote(gq.at[:, yours], qcat.at[core], send.at[3], recv.at[3], sibling)
    begin(copies + [half_q])
    hook("greeted")

    def place_square(y, grad):
        for k, piece in enumerate(pieces_of(grad)):
            p0[k, y] = piece

    own[0].wait()
    wk(), wv()
    if layer == 1:
        copies[0].wait()
        grads[:, ROWS:] = (grads[:, ROWS:].astype(F32) + far_near[...].astype(F32)).astype(BF)
    hidden = remote(gh_send, gh_got, send.at[2], recv.at[2], partner)

    def far_part():
        gh_send[...] = (dot_nt(grads[0, ROWS:], wk()[...]) + dot_nt(grads[1, ROWS:], wv()[...])).astype(BF)
        hidden.start()

    talk(far_part)
    hook("far")
    own[1].wait()
    copies[-1].wait()
    grads[:, 0:ROWS] = (grads[:, 0:ROWS].astype(F32) + near[...].astype(F32)).astype(BF)
    half_kv = remote(grads.at[:, :, yours], kvcat.at[:, core], send.at[4], recv.at[4], sibling)
    half_kv.start()
    kvcat[:, core] = grads[:, :, mine]
    hook("near")
    place_square(1, dwo()[...])
    own[2].wait()
    half_q.wait()
    rows = rows()
    place_square(0, (dot_tn(rows[0, 0:ROWS], qcat[0]) + dot_tn(rows[1, 0:ROWS], qcat[1])).astype(BF))
    hook("two_squares")
    half_kv.wait()
    for side in (0, 1):
        cat = kvcat[side].reshape(2 * (ROWS + far_rows), HALF)
        place_square(2 + side, dot_tn(rows[...].reshape(2 * (ROWS + far_rows), D), cat).astype(BF))
    hook("squares")
    total = gres()[...] + dot_nt(gq_held()[...], wq()[...])
    total += dot_nt(grads[0, 0:ROWS], wk()[...]) + dot_nt(grads[1, 0:ROWS], wv()[...])
    if layer == 1:
        hidden.wait()
        gh[...] = (total + gh_got[...].astype(F32)).astype(gh.dtype)
    else:
        gh[...] = total.astype(gh.dtype)

        @pl.when(is_middle(block))
        def _():
            hidden.wait()
            here = rows_at(give, far_rows)
            gh[here, :] = (gh[here, :].astype(F32) + gh_got[...].astype(F32)).astype(gh.dtype)


def project_back_scratch(layer):
    far_rows, dma = FAR[layer], pltpu.SemaphoreType.DMA
    return [
        pltpu.VMEM((2, ROWS + far_rows, D), BF), pltpu.VMEM((2, ROWS, D), BF),
        pltpu.VMEM((2, far_rows, D), BF), pltpu.VMEM((far_rows, D), BF), pltpu.VMEM((far_rows, D), BF),
        pltpu.VMEM((2, ROWS, HALF), BF), pltpu.VMEM((2, 2, ROWS + far_rows, HALF), BF),
        dma((3,)), dma((5,)), dma((5,)),
        pltpu.VMEM((2, ROWS + far_rows, D), BF), pltpu.VMEM((ROWS, D), BF), pltpu.VMEM((ROWS, D), F32), pltpu.VMEM((D, HALF), BF),
        pltpu.VMEM((D, D), BF), pltpu.VMEM((D, D), BF), pltpu.VMEM((D, D), BF), dma((7,)),
    ]


def own_scratch(stage):
    return pltpu.VMEM(summed(stage), BF)


def got_scratch(stage):
    return pltpu.VMEM((3, 3) + LEFT[stage], BF)


def project_back_two_kernel(
    rows, gq, parts, gres, dwo, wq, wk, wv, low_all, gi, gi_other, r0, got_r0, p0_out, gh, e_out, s_r, got_r, *refs
):
    scratch, (p0, e, gicat, held_low, own_r, held_r, csems, gsems, osems, csend, crecv) = refs[:18], refs[18:]
    core = lax.axis_index("blk_1")
    loads_g, loads_r, carried = [], [], []

    def loads():
        loads_r.extend(begin(own_loads("r", 0, r0, own_r, got_r0, held_r, csems)))
        loads_g.extend(
            begin(
                [
                    pltpu.make_async_copy(gi.at[core], gicat.at[core], gsems.at[0]),
                    pltpu.make_async_copy(gi_other, gicat.at[1 - core], gsems.at[1]),
                    pltpu.make_async_copy(low_all, held_low, gsems.at[2]),
                ]
            )
        )

    def two_squares():
        end(loads_r)
        add_held(own_r, held_r, s_r)
        carried.extend(begin(stage_copies("r", 1, s_r, got_r, csend, crecv)))
        end(loads_g)
        for y in (0, 2):
            both = gicat[:, :, y * HALF : (y + 2) * HALF].reshape(2 * ROWS, 2 * HALF)
            grad = dot_tn(held_low[...].reshape(2 * ROWS, D), both).astype(BF)
            for k, piece in enumerate(pieces_of(grad[:, :HALF])):
                e[k, y] = piece
            for k, piece in enumerate(pieces_of(grad[:, HALF:])):
                e[k, y + 1] = piece
        carried.extend(begin([pltpu.make_async_copy(e, e_out, osems.at[0])]))

    def squares():
        carried.extend(begin([pltpu.make_async_copy(p0, p0_out, osems.at[1])]))

    hooks = dict(loads=loads, two_squares=two_squares, squares=squares)
    project_back_body(1, rows, gq, parts, gres, dwo, wq, wk, wv, p0, gh, scratch, None, hooks)
    end(carried)


def project_back_two(rows_all, gq, parts, gres, dwo, w, low_all, carry):
    shape, dma = jax.ShapeDtypeStruct, pltpu.SemaphoreType.DMA
    return pl.pallas_call(
        project_back_two_kernel,
        out_shape=(shape(WHOLE, BF), shape((ROWS, D), F32), shape(WHOLE, BF), shape(summed(0), BF), landing(1)),
        in_specs=[ANY] * 13,
        out_specs=(ANY, VMEM, ANY, VMEM, ANY),
        scratch_shapes=project_back_scratch(1)
        + [pltpu.VMEM(WHOLE, BF), pltpu.VMEM(WHOLE, BF), pltpu.VMEM((2, ROWS, STEPS * HALF), BF), pltpu.VMEM((2, ROWS, D), BF)]
        + [own_scratch(0), got_scratch(0), dma((4,)), dma((3,)), dma((2,)), dma((3, 3)), dma((3, 3))],
        compiler_params=pltpu.CompilerParams(collective_id=4, has_side_effects=True, vmem_limit_bytes=60 * MIB),
        name="project_back_1",
    )(rows_all, gq, parts.reshape(2, SLOTS * BLOCK, D), gres, dwo, w["query_weight"], w["key_weight"], w["value_weight"],
      low_all, *carry)


def slots_of(layer, tab, cnt, two, three, piece, head):
    block = lax.axis_index("blk_0") * 2 + lax.axis_index("blk_1")
    t = (3 * block + piece) // 4
    j = jnp.where(tab[0, 1] == t, 1, jnp.where(tab[0, 2] == t, 2, 0))
    live = jnp.where(j < cnt[0], 1.0, 0.0)
    if layer == 0:
        return t, live
    from_two = jnp.where(j < 2, two[head, jnp.minimum(j, 1)], j)
    chosen = jnp.where(cnt[0] == SLOTS, three[head, j], from_two)
    return tab[0, chosen], live


def left_lanes(rows=1):
    return lax.broadcasted_iota(jnp.int32, (rows, 2 * HD), 1) < HD


def two_heads(tile):
    left, none = left_lanes(PIECE), jnp.zeros_like(tile)
    return jnp.concatenate([jnp.where(left, tile, none), jnp.where(left, none, tile)], axis=0)


def own_columns(both):
    return jnp.where(left_lanes(PIECE), both[:PIECE], both[PIECE:])


def slot_mask(s0, s1, t, kind):
    first, second = jnp.where(s0 == t, 1.0, 0.0), jnp.where(s1 == t, 1.0, 0.0)
    return jnp.where(left_lanes(), first, second).astype(kind)


def soft(scores):
    top = jnp.max(scores, axis=0, keepdims=True)
    e = jnp.exp((scores - top) * SCALE)
    return e * (1.0 / jnp.sum(e, axis=0, keepdims=True))


def attend_kernel(layer, tab, cnt, two, three, q, k, v, mixed):
    pair = pl.program_id(0)
    left = left_lanes(BLOCK)
    for i in range(3):
        rows = pl.ds(i * PIECE, PIECE)
        s0, live = slots_of(layer, tab, cnt, two, three, i, 2 * pair)
        if layer == 0:
            keys, values = k[s0], v[s0]
        else:
            s1, _ = slots_of(layer, tab, cnt, two, three, i, 2 * pair + 1)
            keys, values = jnp.where(left, k[s0], k[s1]), jnp.where(left, v[s0], v[s1])
        weights = soft(dot_nt(keys, two_heads(q[rows, :]))).astype(BF)
        mixed[rows, :] = (own_columns(dot_tn(weights, values)) * live).astype(BF)


def attend_specs():
    tile = pl.BlockSpec((ROWS, 2 * HD), lambda p: (0, p))
    keys = pl.BlockSpec((None, SLOTS, BLOCK, 2 * HD), lambda p: (0, 0, 0, p))
    values = pl.BlockSpec((None, SLOTS, BLOCK, 2 * HD), lambda p: (1, 0, 0, p))
    return tile, keys, values


def attend(layer, table, q, kv_all):
    tile, keys, values = attend_specs()
    return pl.pallas_call(
        functools.partial(attend_kernel, layer),
        grid=(HEADS // 2,),
        out_shape=jax.ShapeDtypeStruct((ROWS, D), BF),
        in_specs=[SMEM] * 4 + [tile, keys, values],
        out_specs=tile,
        compiler_params=params(),
        name=f"attend_{layer}",
    )(*table, q, kv_all, kv_all)


def attend_back_step(layer, tab, cnt, two, three, q, k, v, gm, gq, gkv, acc):
    pair = pl.program_id(0)
    masks = []
    if layer == 0:
        acc[...] = jnp.zeros_like(acc)
    for i in range(3):
        rows = pl.ds(i * PIECE, PIECE)
        s0, live = slots_of(layer, tab, cnt, two, three, i, 2 * pair)
        if layer == 0:
            keys, values = k[s0], v[s0]
        else:
            s1, _ = slots_of(layer, tab, cnt, two, three, i, 2 * pair + 1)
            low = [slot_mask(s0, s1, t, BF) for t in range(SLOTS)]
            masks.append([slot_mask(s0, s1, t, F32) for t in range(SLOTS)])
            keys = k[0] * low[0] + k[1] * low[1] + k[2] * low[2]
            values = v[0] * low[0] + v[1] * low[1] + v[2] * low[2]
        qq = two_heads(q[rows, :])
        gg = two_heads((gm[rows, :].astype(F32) * live).astype(BF))
        weights = soft(dot_nt(keys, qq))
        grad_weights = dot_nt(values, gg)
        delta = jnp.sum(weights * grad_weights, axis=0, keepdims=True)
        grad_scores = (weights * (grad_weights - delta)).astype(BF)
        gq[rows, :] = (own_columns(dot_tn(grad_scores, keys)) * SCALE).astype(BF)
        gk = dot(grad_scores, qq) * SCALE
        gv = dot(weights.astype(BF), gg)
        if layer == 0:
            acc[0, s0] += gk
            acc[1, s0] += gv
        else:
            acc[0, i] = gk
            acc[1, i] = gv
    if layer == 0:
        gkv[...] = acc[...].astype(BF)
    else:
        for side in range(2):
            for t in range(SLOTS):
                total = acc[side, 0] * masks[0][t] + acc[side, 1] * masks[1][t] + acc[side, 2] * masks[2][t]
                gkv[side, t] = total.astype(BF)


def attend_back_kernel(layer, tab, cnt, two, three, q, k, v, gm, e, r, gq, gkv, vec, got_e, got_r, acc, send, recv):
    step = pl.program_id(0)
    core = lax.axis_index("blk_1")

    def carried():
        copies = stage_copies("r", 0, r, got_r, send.at[0], recv.at[0])
        if layer == 0:
            return copies + stage_copies("e", 0, e, got_e, send.at[1], recv.at[1])
        return copies + [remote(e.at[1 - core], got_e, send.at[1, 0, 0], recv.at[1, 0, 0], {"blk_1": 1 - core})]

    peers = axis_peers((0, 1, 2)) + ([{"blk_1": 1 - core}] if layer == 1 else [])

    @pl.when(step == 0)
    def _():
        barrier = pltpu.get_barrier_semaphore()
        for peer in peers:
            pl.semaphore_signal(barrier, inc=1, device_id=peer, device_id_type=MESH)

    attend_back_step(layer, tab, cnt, two, three, q, k, v, gm, gq, gkv, acc)
    vec[0:1] = jnp.sum(gq[...].astype(F32), axis=0, keepdims=True)
    total = jnp.zeros((1, 2 * HD), F32)
    for i in range(3):
        _, live = slots_of(0, tab, cnt, two, three, i, 0)
        total += live * jnp.sum(gm[i * PIECE : (i + 1) * PIECE, :].astype(F32), axis=0, keepdims=True)
    vec[1:2] = total

    @pl.when(step == 0)
    def _():
        pl.semaphore_wait(pltpu.get_barrier_semaphore(), len(peers))
        begin(carried())

    @pl.when(step == HEADS // 2 - 1)
    def _():
        end(carried())


def attend_back(layer, table, q, kv_all, gm, e, r):
    tile, keys, values = attend_specs()
    both = pl.BlockSpec((2, SLOTS, BLOCK, 2 * HD), lambda p: (0, 0, 0, p))
    shape, dma = jax.ShapeDtypeStruct, pltpu.SemaphoreType.DMA
    landed = landing(0) if layer == 0 else shape((ROWS, STEPS * HALF), BF)
    return pl.pallas_call(
        functools.partial(attend_back_kernel, layer),
        grid=(HEADS // 2,),
        out_shape=(shape((ROWS, D), BF), shape((2, SLOTS, BLOCK, D), BF), shape((2, D), F32), landed, landing(0)),
        in_specs=[SMEM] * 4 + [tile, keys, values, tile, ANY, ANY],
        out_specs=(tile, both, pl.BlockSpec((2, 2 * HD), lambda p: (0, p)), ANY, ANY),
        scratch_shapes=[pltpu.VMEM((2, SLOTS, BLOCK, 2 * HD), F32), dma((2, 3, 3)), dma((2, 3, 3))],
        compiler_params=pltpu.CompilerParams(collective_id=9 + layer, has_side_effects=True, vmem_limit_bytes=60 * MIB),
        name=f"attend_back_{layer}",
    )(*table, q, kv_all, kv_all, gm, e, r)


STEPS = FF // CHUNK


def tail_kernel(
    layer, mixed, h, wo, bo, g1, s1, we, be, wr, br, g2, s2, r1, r2, out, slope, act_all, low_all, mixed_all,
    first, total, low, act, local, send, recv,
):
    j = pl.program_id(0)
    core = lax.axis_index("blk_1")
    sibling = {"blk_1": 1 - core}

    def both(src, dst, n):
        return [remote(src, dst, send.at[n], recv.at[n], sibling), pltpu.make_async_copy(src, dst, local.at[n])]

    def act_copies(at):
        return both(act.at[at], act_all.at[core, :, columns_at(at * CHUNK, CHUNK)], at)

    early = both(mixed, mixed_all.at[core], STEPS) + both(low, low_all.at[core], STEPS + 1)

    @pl.when(j == 0)
    def _():
        barrier = pltpu.get_barrier_semaphore()
        pl.semaphore_signal(barrier, inc=1, device_id=sibling, device_id_type=MESH)
        residual = h[...].astype(F32) + dot(mixed[...], wo[...]) + row_of(bo, layer)
        r1[...] = residual
        normed, _ = norm_parts(residual)
        first[...] = normed * row_of(g1, layer) + row_of(s1, layer)
        low[...] = first[...].astype(BF)
        total[...] = jnp.zeros_like(total)
        pl.semaphore_wait(barrier, 1)
        for c in early:
            c.start()

    inner = dot(low[...], we[...]) + be[layer : layer + 1, columns_at(j * CHUNK, CHUNK)].astype(F32)
    phi = 0.5 * (1.0 + lax.erf(inner * ROOT_HALF))
    low_act = (inner * phi).astype(BF)
    act[j] = low_act
    for c in act_copies(j):
        c.start()
    slope[...] = (phi + inner * (INV_ROOT_TAU * jnp.exp(-0.5 * inner * inner))).astype(BF)
    total[...] += dot(low_act, wr[...])

    @pl.when(j == STEPS - 1)
    def _():
        residual = first[...] + total[...] + row_of(br, layer)
        r2[...] = residual
        normed, _ = norm_parts(residual)
        out[...] = (normed * row_of(g2, layer) + row_of(s2, layer)).astype(out.dtype)
        for c in early:
            c.wait()
        for at in range(STEPS):
            for c in act_copies(at):
                c.wait()


def tail(layer, mixed, h, w, out_type):
    square = layer_block(layer, (D, D), lambda j: (0, 0))
    wide = layer_block(layer, (D, CHUNK), lambda j: (0, j))
    tall = layer_block(layer, (CHUNK, D), lambda j: (j, 0))
    full = pl.BlockSpec((ROWS, D), lambda j: (0, 0))
    vec, dma = VMEM, pltpu.SemaphoreType.DMA
    shape = jax.ShapeDtypeStruct
    return pl.pallas_call(
        functools.partial(tail_kernel, layer),
        grid=(STEPS,),
        out_shape=(
            shape((ROWS, D), F32), shape((ROWS, D), F32), shape((ROWS, D), out_type), shape((ROWS, FF), BF),
            shape((2, ROWS, FF), BF), shape((2, ROWS, D), BF), shape((2, ROWS, D), BF),
        ),
        in_specs=[full, full, square, vec, vec, vec, wide, vec, tall, vec, vec, vec],
        out_specs=(full, full, full, pl.BlockSpec((ROWS, CHUNK), lambda j: (0, j)), ANY, ANY, ANY),
        scratch_shapes=[
            pltpu.VMEM((ROWS, D), F32), pltpu.VMEM((ROWS, D), F32), pltpu.VMEM((ROWS, D), BF),
            pltpu.VMEM((STEPS, ROWS, CHUNK), BF), dma((STEPS + 2,)), dma((STEPS + 2,)), dma((STEPS + 2,)),
        ],
        compiler_params=pltpu.CompilerParams(collective_id=5 + layer, has_side_effects=True, vmem_limit_bytes=60 * MIB),
        name=f"tail_{layer}",
    )(mixed, h, w["output_weight"], w["output_bias"], w["first_gain"], w["first_shift"], w["expand_weight"], w["expand_bias"],
      w["reduce_weight"], w["reduce_bias"], w["second_gain"], w["second_shift"])


def tail_back_kernel(layer, g, r1, r2, low_all, act_all, slope, mixed_all, wo, we, wr, g1, g2, *refs):
    refs = list(refs)

    def take(count):
        out, refs[:count] = refs[:count], []
        return out

    q_in, e_in = take(2) if layer == 0 else (None, None)
    dwr, dwe, dwo, gres, gm, vec, vec_e = take(7)
    got_q, got_e = take(2) if layer == 0 else (None, None)
    go, ga, gi, total, gocat, gacat, gicat, send, recv = take(9)
    last = STEPS if layer == 0 else STEPS - 1

    def carried():
        if layer == 1:
            return []
        csend, crecv = refs
        return stage_copies("q", 0, q_in, got_q, csend.at[0], crecv.at[0]) + stage_copies(
            "e", 0, e_in, got_e, csend.at[1], crecv.at[1]
        )

    j = pl.program_id(0)
    core = lax.axis_index("blk_1")
    sibling = {"blk_1": 1 - core}
    mine, yours = columns_at(core * HALF, HALF), columns_at((1 - core) * HALF, HALF)

    def share_go():
        return remote(go.at[:, yours], gocat.at[core], send.at[STEPS], recv.at[STEPS], sibling)

    def share_ga():
        return remote(ga.at[:, yours], gacat.at[core], send.at[STEPS + 1], recv.at[STEPS + 1], sibling)

    def share_gi(at):
        return remote(gi.at[at, :, yours], gicat.at[at, core], send.at[at], recv.at[at], sibling)

    @pl.when(j == 0)
    def _():
        barrier = pltpu.get_barrier_semaphore()
        peers = [sibling] + (axis_peers((0, 1, 2)) if layer == 0 else [])
        for peer in peers:
            pl.semaphore_signal(barrier, inc=1, device_id=peer, device_id_type=MESH)
        grad = g[...].astype(F32)
        normed, inv_std = norm_parts(r2[...])
        grad_r = norm_backward(grad, row_of(g2, layer), normed, inv_std)
        vec[0:1] = jnp.sum(grad * normed, axis=0, keepdims=True)
        vec[1:2] = jnp.sum(grad, axis=0, keepdims=True)
        total[...] = grad_r
        go[...] = grad_r.astype(BF)
        vec[2:3] = jnp.sum(go[...].astype(F32), axis=0, keepdims=True)
        pl.semaphore_wait(barrier, len(peers))
        share_go().start()
        begin(carried())
        gocat[core] = go[:, mine]

    @pl.when(j < STEPS)
    def _():
        grad_inner = (dot_nt(go[...], wr[...]) * slope[...].astype(F32)).astype(BF)
        if layer == 0:
            gi[j] = grad_inner
            share_gi(j).start()
            gicat[j, core] = gi[j, :, mine]
        else:
            dwe[0], dwe[1] = grad_inner[:, :HALF], grad_inner[:, HALF:]
        vec_e[...] = jnp.sum(grad_inner.astype(F32), axis=0, keepdims=True)
        total[...] += dot_nt(grad_inner, we[...])

        @pl.when(j == 0)
        def _():
            share_go().wait()

        grad = dot_tn(act_all[...].reshape(2 * ROWS, CHUNK), gocat[...].reshape(2 * ROWS, HALF)).astype(BF)
        for k, piece in enumerate(pieces_of(grad)):
            dwr[k, 0] = piece

    @pl.when(j == STEPS - 1)
    def _():
        grad = total[...]
        normed, inv_std = norm_parts(r1[...])
        grad_r = norm_backward(grad, row_of(g1, layer), normed, inv_std)
        vec[3:4] = jnp.sum(grad * normed, axis=0, keepdims=True)
        vec[4:5] = jnp.sum(grad, axis=0, keepdims=True)
        gres[...] = grad_r
        ga[...] = grad_r.astype(BF)
        vec[5:6] = jnp.sum(ga[...].astype(F32), axis=0, keepdims=True)
        share_ga().start()
        gacat[core] = ga[:, mine]

    if layer == 0:

        @pl.when(j > 0)
        def _():
            share_gi(j - 1).wait()
            grad = dot_tn(low_all[...].reshape(2 * ROWS, D), gicat[j - 1].reshape(2 * ROWS, HALF)).astype(BF)
            for k, piece in enumerate(pieces_of(grad)):
                dwe[k, 0] = piece

    @pl.when(j == last)
    def _():
        gm[...] = dot_nt(ga[...], wo[...]).astype(BF)
        share_ga().wait()
        dwo[...] = dot_tn(mixed_all[...].reshape(2 * ROWS, D), gacat[...].reshape(2 * ROWS, HALF)).astype(BF)
        end(carried())


def tail_back(layer, g, saved, w, carry=()):
    at = lambda j: jnp.minimum(j, STEPS - 1)
    square = layer_block(layer, (D, D), lambda j: (0, 0))
    wide = layer_block(layer, (D, CHUNK), lambda j: (0, at(j)))
    tall = layer_block(layer, (CHUNK, D), lambda j: (at(j), 0))
    full = pl.BlockSpec((ROWS, D), lambda j: (0, 0))
    pair = pl.BlockSpec((2, ROWS, D), lambda j: (0, 0, 0))
    vec, dma = VMEM, pltpu.SemaphoreType.DMA
    shape = jax.ShapeDtypeStruct
    chunk = pl.BlockSpec((3, 1) + LEFT[0], lambda j: (0, at(j), 0, 0, 0, 0))
    if layer == 0:
        expand, expand_spec = shape(WHOLE, BF), pl.BlockSpec((3, 1) + LEFT[0], lambda j: (0, jnp.maximum(j - 1, 0), 0, 0, 0, 0))
    else:
        expand, expand_spec = shape((2, ROWS, STEPS * HALF), BF), pl.BlockSpec((2, ROWS, HALF), lambda j: (0, 0, j))
    return pl.pallas_call(
        functools.partial(tail_back_kernel, layer),
        grid=(STEPS + 1 if layer == 0 else STEPS,),
        out_shape=(
            shape(WHOLE, BF), expand, shape((D, HALF), BF), shape((ROWS, D), F32), shape((ROWS, D), BF),
            shape((8, D), F32), shape((1, FF), F32),
        )
        + ((landing(0),) * 2 if carry else ()),
        in_specs=[
            full, full, full, pair if layer == 0 else ANY, pl.BlockSpec((2, ROWS, CHUNK), lambda j: (0, 0, at(j))),
            pl.BlockSpec((ROWS, CHUNK), lambda j: (0, at(j))), pair, square, wide, tall, vec, vec,
        ]
        + [ANY] * len(carry),
        out_specs=(
            chunk, expand_spec, pl.BlockSpec((D, HALF), lambda j: (0, 0)), full, full,
            pl.BlockSpec((8, D), lambda j: (0, 0)), pl.BlockSpec((1, CHUNK), lambda j: (0, at(j))),
        )
        + ((ANY,) * 2 if carry else ()),
        scratch_shapes=[
            pltpu.VMEM((ROWS, D), BF), pltpu.VMEM((ROWS, D), BF), pltpu.VMEM((STEPS, ROWS, CHUNK), BF), pltpu.VMEM((ROWS, D), F32),
            pltpu.VMEM((2, ROWS, HALF), BF), pltpu.VMEM((2, ROWS, HALF), BF), pltpu.VMEM((STEPS, 2, ROWS, HALF), BF),
            dma((STEPS + 2,)), dma((STEPS + 2,)),
        ]
        + ([dma((2, 3, 3)), dma((2, 3, 3))] if carry else []),
        compiler_params=pltpu.CompilerParams(collective_id=7 + layer, has_side_effects=True, vmem_limit_bytes=60 * MIB),
        name=f"tail_back_{layer}",
    )(g, saved["r1"], saved["r2"], saved["low_all"], saved["act_all"], saved["slope"], saved["mixed_all"],
      w["output_weight"], w["expand_weight"], w["reduce_weight"], w["first_gain"], w["second_gain"], *carry)


VECTORS = 24


def last_kernel(*refs):
    refs = list(refs)

    def take(count):
        out, refs[:count] = refs[:count], []
        return out

    rows, gq, parts, gres, dwo, wq, wk, wv = take(8)
    e0, got_e0, r0, got_r0, q0_two, got_q0_two, e0_two, got_e0_two, r1_two, got_r1_two = take(10)
    vec_p, vec, vec_e, vec_p_two, vec_two, vec_e_two = take(6)
    gh, fix_got, rfix_got, v_out = take(4)
    scratch = take(18)
    p0, got_q0, own_q0, s_q0, got_q1, s_q1, got_q2 = take(7)
    own_e0, held_e0, s_e0, got_e1, s_e1, got_e2 = take(6)
    own_r0, held_r0, s_r0, got_r1, s_r1, got_r2 = take(6)
    own_q0_two, held_q0_two, s_q0_two, got_q1_two, s_q1_two, got_q2_two = take(6)
    own_e0_two, held_e0_two, s_e0_two, got_e1_two, s_e1_two, got_e2_two = take(6)
    own_r1_two, held_r1_two, s_r1_two, got_r2_two = take(4)
    fix_send, rfix_send, vsum, vgot, vtotal, vz, vx = take(7)
    local, send, recv, fsend, frecv, vsend, vrecv = take(7)

    place = chip_place()
    core = lax.axis_index("blk_1")
    pos = lax.axis_index("dp_2") * 4 + lax.axis_index("blk_0") * 2 + core
    other = 1 - core
    sibling = {"blk_1": other}
    loads, flights = [], {}

    def start_loads():
        loads.extend(
            [
                begin(own_loads("e", 0, e0, own_e0, got_e0, held_e0, local.at[0])),
                begin(own_loads("r", 0, r0, own_r0, got_r0, held_r0, local.at[1])),
                begin(own_loads("q", 0, q0_two, own_q0_two, got_q0_two, held_q0_two, local.at[2])),
                begin(own_loads("e", 0, e0_two, own_e0_two, got_e0_two, held_e0_two, local.at[3])),
                begin(own_loads("r", 1, r1_two, own_r1_two, got_r1_two, held_r1_two, local.at[4])),
            ]
        )
        vectors = [vec_p[0:1], vec_p[1:2]] + [vec[k : k + 1] for k in range(6)]
        vectors += [vec_p_two[0:1], vec_p_two[1:2]] + [vec_two[k : k + 1] for k in range(6)]
        vectors += [v[:, k * D : (k + 1) * D] for v in (vec_e, vec_e_two) for k in range(4)]
        for k, vector in enumerate(vectors):
            vsum[k // 3, k % 3 : k % 3 + 1] = vector
        for k in range(8):
            vsum[k, 3:8] = jnp.zeros((5, D), F32)

    def launch(key, group, stage, source, got, n):
        flights[key] = begin(stage_copies(group, stage, source, got, send.at[n], recv.at[n]))

    def to_all(source, dest, at):
        out = []
        for d in range(1, 8):
            t = lax.rem(pos + d, 8)
            out.append(remote(source(t), dest.at[pos], vsend.at[at + d], vrecv.at[at + d], pos_device(t)))
        return begin(out)

    def along(axis, got, at):
        return begin([remote(vtotal, got.at[d - 1], vsend.at[at + d], vrecv.at[at + d], peer_of(axis, place, d)) for d in (1, 2, 3)])

    def greeted():
        flights["vc"] = to_all(lambda t: vsum.at[t], vgot, 0)
        end(loads[0])
        add_held(own_e0, held_e0, s_e0)
        launch("e1", "e", 1, s_e0, got_e1, 0)
        end(loads[1])
        add_held(own_r0, held_r0, s_r0)
        launch("r1", "r", 1, s_r0, got_r1, 1)
        end(loads[2])
        add_held(own_q0_two, held_q0_two, s_q0_two)
        launch("q1_two", "q", 1, s_q0_two, got_q1_two, 2)
        end(loads[3])
        add_held(own_e0_two, held_e0_two, s_e0_two)
        launch("e1_two", "e", 1, s_e0_two, got_e1_two, 3)
        end(loads[4])
        add_held(own_r1_two, held_r1_two, s_r1_two)
        launch("r2_two", "r", 2, s_r1_two, got_r2_two, 4)

    def far_done():
        end(flights["vc"])
        vgot[pos] = vsum[pos]
        total = vgot[0]
        for k in range(1, 8):
            total = total + vgot[k]
        vtotal[...] = total
        flights["vz"] = along(0, vz, 7)

    def square_flights(half):
        out = []
        for d in (2, 1, 3):
            for n, axis in ((1, 1), (2, 0)):
                at, two = lax.rem(place[axis] + d, 4), pl.ds(2 * half, 2)
                src = p0.at[1, two, :, at] if n == 1 else p0.at[2, two, at]
                sems = send.at[12 + half, n, d - 1], recv.at[12 + half, n, d - 1]
                out.append(remote(src, got_q0.at[n, d - 1, two], *sems, peer_of(axis, place, d)))
        return out

    def square_along_y(d):
        to = lax.rem(place[2] + d, 4)
        return remote(p0.at[0, to], got_q0.at[0, d - 1], send.at[5, 0, d - 1], recv.at[5, 0, d - 1], peer_of(2, place, d))

    def launch_squares(half):
        for d in (2, 1, 3):
            pl.when(lax.rem(place[2] + d, 4) // 2 == half)(lambda d=d: square_along_y(d).start())
        begin(square_flights(half))

    def two_squares():
        launch_squares(0)

    def squares():
        launch_squares(1)
        end(flights["vz"])
        vtotal[...] = vtotal[...] + vz[0] + vz[1] + vz[2]
        flights["vx"] = along(1, vx, 10)
        end(flights["e1"])
        add_direct("e", 1, s_e0, got_e1, s_e1)
        launch("e2", "e", 2, s_e1, got_e2, 7)
        end(flights["r1"])
        add_direct("r", 1, s_r0, got_r1, s_r1)
        launch("r2", "r", 2, s_r1, got_r2, 8)
        end(flights["q1_two"])
        add_direct("q", 1, s_q0_two, got_q1_two, s_q1_two)
        launch("q2_two", "q", 2, s_q1_two, got_q2_two, 6)
        end(flights["e1_two"])
        add_direct("e", 1, s_e0_two, got_e1_two, s_e1_two)
        launch("e2_two", "e", 2, s_e1_two, got_e2_two, 11)

    peers = axis_peers((0, 1)) + [pos_device(lax.rem(pos + d, 8)) for d in range(1, 8)]
    hooks = dict(loads=start_loads, greeted=greeted, far=far_done, two_squares=two_squares, squares=squares)
    project_back_body(0, rows, gq, parts, gres, dwo, wq, wk, wv, p0, gh, scratch, peers, hooks)

    def last(group, source, got):
        thirds = []
        for n in range(3):
            total = own_share(group, 2, n, source)[...].astype(F32)
            for d in range(3):
                total += got[n, d].astype(F32)
            thirds.append(total)
        return jnp.concatenate(thirds, axis=1)

    def rows_out(layer, part, total):
        for k in range(8):
            fix_send[layer, part, k, 0:6] = total[6 * k : 6 * k + 6]
        out = []
        for d in range(1, 8):
            t = lax.rem(pos + d, 8)
            sems = fsend.at[layer, part, d], frecv.at[layer, part, d]
            out.append(remote(fix_send.at[layer, part, t], fix_got.at[layer, part, pos], *sems, pos_device(t)))
        return begin(out)

    def reduce_out(layer, total):
        rfix_send[layer] = total
        there, here = [pl.ds(pl.multiple_of(c * 24, 8), 24) for c in (other, core)]
        rfix_got[layer, core] = rfix_send[layer, here]
        sems = fsend.at[layer, 0, 0], frecv.at[layer, 0, 0]
        return begin([remote(rfix_send.at[layer, there], rfix_got.at[layer, core], *sems, sibling)])

    end(flights["vx"])
    vtotal[...] = vtotal[...] + vx[0] + vx[1] + vx[2]
    fixes = to_all(lambda t: vtotal, v_out, 13)
    v_out[pos] = vtotal[...]
    end(flights["r2_two"])
    fixes += reduce_out(1, last("r", s_r1_two, got_r2_two))
    end(flights["e2"])
    fixes += rows_out(0, 1, last("e", s_e1, got_e2))
    end(flights["r2"])
    fixes += reduce_out(0, last("r", s_r1, got_r2))
    end(flights["q2_two"])
    fixes += rows_out(1, 0, last("q", s_q1_two, got_q2_two))
    end(flights["e2_two"])
    fixes += rows_out(1, 1, last("e", s_e1_two, got_e2_two))
    for n in range(3):
        own_q0[n] = own_share("q", 0, n, p0)[...]
    end([square_along_y(d) for d in (1, 2, 3)] + square_flights(0) + square_flights(1))
    add_held(own_q0, got_q0, s_q0)
    launch("q1", "q", 1, s_q0, got_q1, 9)
    end(flights["q1"])
    add_direct("q", 1, s_q0, got_q1, s_q1)
    launch("q2", "q", 2, s_q1, got_q2, 10)
    end(flights["q2"])
    fixes += rows_out(0, 0, last("q", s_q1, got_q2))
    for layer in range(2):
        for part in range(2):
            fix_got[layer, part, pos] = fix_send[layer, part, pos]
    end(fixes)


def last_step(rows_all, gq, parts, gres, dwo, w, carry, vecs):
    dma, shape = pltpu.SemaphoreType.DMA, jax.ShapeDtypeStruct
    own, got = own_scratch, got_scratch
    return pl.pallas_call(
        last_kernel,
        out_shape=(shape((ROWS, D), BF), shape((2, 2, 8, 8, HALF), F32), shape((2, 2, 24, HALF), F32), shape((8, 8, D), F32)),
        in_specs=[ANY] * 18 + [VMEM] * 6,
        out_specs=[VMEM] * 4,
        scratch_shapes=project_back_scratch(0)
        + [pltpu.VMEM(WHOLE, BF), got(0), own(0), own(0), got(1), own(1), got(2)]
        + [own(0), got(0), own(0), got(1), own(1), got(2)] * 4
        + [own(1), got(1), own(1), got(2)]
        + [
            pltpu.VMEM((2, 2, 8, 8, HALF), F32),
            pltpu.VMEM((2, 48, HALF), F32),
            pltpu.VMEM((8, 8, D), F32),
            pltpu.VMEM((8, 8, D), F32),
            pltpu.VMEM((8, D), F32),
            pltpu.VMEM((3, 8, D), F32),
            pltpu.VMEM((3, 8, D), F32),
            dma((5, 4)), dma((14, 3, 3)), dma((14, 3, 3)), dma((2, 2, 8)), dma((2, 2, 8)), dma((21,)), dma((21,)),
        ],
        compiler_params=pltpu.CompilerParams(collective_id=3, has_side_effects=True, vmem_limit_bytes=60 * MIB),
        name="last_step",
    )(rows_all, gq, parts.reshape(2, SLOTS * BLOCK, D), gres, dwo, w["query_weight"], w["key_weight"], w["value_weight"], *carry, *vecs)


def layer_forward(layer, h, table, w, out_type):
    q, kv_all, rows_all = project(layer, h, w)
    mixed = attend(layer, table, q, kv_all)
    r1, r2, out, slope, act_all, low_all, mixed_all = tail(layer, mixed, h, w, out_type)
    return out, dict(
        rows_all=rows_all, q=q, kv_all=kv_all, r1=r1, r2=r2, slope=slope, act_all=act_all, low_all=low_all, mixed_all=mixed_all
    )


def finish_kernel(quads, rows, vecs, final, grad, *outs):
    me = lax.axis_index(DP_BLK)
    wq, wk, wv, wo, we, wr, q_b, v_b, s_g, s_s, r_b, f_g, f_s, o_b, e_b, final_out, grad_out = outs
    final_out[...] = final[...]
    grad_out[...] = grad[...]
    for layer in range(2):
        for s in range(8):
            y, c = (s // 2 % 2) * 2 + s // 4, s % 2
            (wq, wo, wk, wv)[y][:, layer, c * HALF : (c + 1) * HALF] = quads[layer, 0, s, 0:6]
            we[:, layer, y * D + c * HALF : y * D + (c + 1) * HALF] = quads[layer, 1, s, 0:6]
        for c in range(2):
            wr[layer, :, c * HALF : (c + 1) * HALF] = rows[layer, c]
    vectors = [vecs[k // 3, k % 3 : k % 3 + 1] for k in range(VECTORS)]
    turned = pltpu.roll(jnp.concatenate(vectors[0:16], axis=0), lax.rem(D - 6 * me, D), 1)
    for n, out in enumerate((q_b, v_b, s_g, s_s, r_b, f_g, f_s, o_b)):
        for layer in range(2):
            out[layer : layer + 1] = turned[8 * layer + n : 8 * layer + n + 1, 0:6]
    wide = pltpu.roll(jnp.concatenate(vectors[16:24], axis=0), lax.rem(D - 24 * lax.rem(me, 32), D), 1)
    for layer in range(2):
        total = jnp.zeros((1, 24), F32)
        for k in range(4):
            total = total + jnp.where(me // 32 == k, wide[4 * layer + k : 4 * layer + k + 1, 0:24], 0.0)
        e_b[layer : layer + 1] = total


def finish(quads, rows, vecs, final, grad):
    shape = jax.ShapeDtypeStruct
    square, small, hidden = shape((6, 2, D), F32), shape((2, 6), F32), shape((1, ROWS, D), BF)
    outs = pl.pallas_call(
        finish_kernel,
        out_shape=(square,) * 4 + (shape((6, 2, FF), F32), shape((2, 24, D), F32)) + (small,) * 8 + (shape((2, 24), F32),)
        + (hidden, hidden),
        in_specs=[VMEM] * 5,
        out_specs=(VMEM,) * 17,
        name="finish",
    )(quads, rows, vecs, final[None], grad[None])
    wq, wk, wv, wo, we = [o.transpose(1, 0, 2) for o in outs[:5]]
    wr, q_b, v_b, s_g, s_s, r_b, f_g, f_s, o_b, e_b, final, grad = outs[5:]
    return (final, grad, wq, wk, wv, wo, q_b, v_b, o_b, we, e_b, wr, r_b, f_g, f_s, s_g, s_s)


NAMES = (
    "query_weight", "key_weight", "value_weight", "output_weight", "query_bias", "value_bias", "output_bias", "expand_weight",
    "expand_bias", "reduce_weight", "reduce_bias", "first_gain", "first_shift", "second_gain", "second_shift",
)


def local(hidden, output_grad, block_counts, slot_table, block_order_two, block_order_three, *weights):
    w = dict(zip(NAMES, weights))
    table = (slot_table, block_counts, block_order_two, block_order_three)
    middle, saved_one = layer_forward(0, hidden[0], table, w, F32)
    final, saved_two = layer_forward(1, middle, table, w, BF)
    r_two, gi, dwo, gres, gm, vec_two, vec_e_two = tail_back(1, output_grad[0], saved_two, w)
    gq, parts, vec_p_two, gi_other, got_r = attend_back(1, table, saved_two["q"], saved_two["kv_all"], gm, gi, r_two)
    carry = (gi, gi_other, r_two, got_r)
    q_two, grad_middle, e_two, r1, got_r = project_back_two(
        saved_two["rows_all"], gq, parts, gres, dwo, w, saved_two["low_all"], carry
    )
    r0, e0, dwo, gres, gm, vec, vec_e, got_q, got_e = tail_back(0, grad_middle, saved_one, w, (q_two, e_two))
    gq, parts, vec_p, got_e0, got_r0 = attend_back(0, table, saved_one["q"], saved_one["kv_all"], gm, e0, r0)
    carry = (e0, got_e0, r0, got_r0, q_two, got_q, e_two, got_e, r1, got_r)
    vecs = (vec_p, vec, vec_e, vec_p_two, vec_two, vec_e_two)
    grad_hidden, *sums = last_step(saved_one["rows_all"], gq, parts, gres, dwo, w, carry, vecs)
    return finish(*sums, final, grad_hidden)


def solution(mesh):
    finer = Mesh(mesh.devices.reshape(4, 4, 2, 2, 2), DP_BLK)
    in_specs = (P(DP, BLK, None), P(DP, BLK, None), P(DP), P(DP, None)) + (P(),) * 17
    wide, flat = P(None, DP_BLK, None), P(None, DP_BLK)
    out_specs = (P(DP, BLK, None), P(DP, BLK, None), wide, wide, wide, wide, flat, flat, flat, wide, flat, wide) + (flat,) * 5
    return jax.shard_map(local, mesh=finer, in_specs=in_specs, out_specs=out_specs, check_vma=False)
```

```python
import functools

import jax
import jax.numpy as jnp
from jax import lax
from jax.experimental import pallas as pl
from jax.experimental.pallas import tpu as pltpu
from jax.sharding import Mesh
from jax.sharding import PartitionSpec as P

D = 768
FF = 3072
HEADS = 12
HD = 64
BLOCK = 512
SLOTS = 3
ROWS = 384
PIECE = 128
CHUNK = 768
HALF = 384
BLK = ("blk_0", "blk_1")
DP_BLK = ("dp_0", "dp_1", "dp_2", "blk_0", "blk_1")
DP = ("dp_0", "dp_1", "dp_2")
EPSILON = 1e-06
ROOT_HALF = 0.7071067811865476
INV_ROOT_TAU = 0.3989422804014327
SCALE = HD ** (-0.5)
MESH = pl.DeviceIdType.MESH
BF = jnp.bfloat16
F32 = jnp.float32
MIB = 1024 * 1024
VMEM = pl.BlockSpec(memory_space=pltpu.VMEM)
SMEM = pl.BlockSpec(memory_space=pltpu.SMEM)
ANY = pl.BlockSpec(memory_space=pl.ANY)


def dot(left, right):
    return jnp.dot(left, right, preferred_element_type=F32)


def dot_nt(left, right):
    return lax.dot_general(left, right, (((1,), (1,)), ((), ())), preferred_element_type=F32)


def dot_tn(left, right):
    return lax.dot_general(left, right, (((0,), (0,)), ((), ())), preferred_element_type=F32)


def params(limit=60):
    return pltpu.CompilerParams(vmem_limit_bytes=limit * MIB)


def row_of(ref, layer):
    return ref[layer : layer + 1, :].astype(F32)


def norm_parts(residual):
    mean = jnp.mean(residual, axis=-1, keepdims=True)
    centred = residual - mean
    inv_std = lax.rsqrt(jnp.mean(centred * centred, axis=-1, keepdims=True) + EPSILON)
    return centred * inv_std, inv_std


def norm_backward(grad, gain, normed, inv_std):
    scaled = grad * gain
    return inv_std * (
        scaled
        - jnp.mean(scaled, axis=-1, keepdims=True)
        - normed * jnp.mean(scaled * normed, axis=-1, keepdims=True)
    )


def layer_block(layer, shape, index):
    return pl.BlockSpec((None,) + shape, lambda j: (layer,) + index(j))


def peer_of(axis, place, offset):
    at = lax.rem(place[axis] + offset, 4)
    if axis == 0:
        return {"dp_0": at}
    if axis == 1:
        return {"dp_1": at}
    return {"dp_2": lax.rem(at, 2), "blk_0": at // 2}


def pos_device(t):
    return {"dp_2": t // 4, "blk_0": lax.rem(t // 2, 2), "blk_1": lax.rem(t, 2)}


def columns_at(start, count):
    return pl.ds(pl.multiple_of(start, 128), count)


STREAM_ORDERS = ((2, 0, 1), (1, 2, 0), (0, 1, 2))
LAYOUT = {"q": (2, 0, 1), "e": (2, 0, 1), "r": (0, 1, 2)}
PIECES = (48, 128)
LEFT = ((4, 4) + PIECES, (4,) + PIECES, PIECES)
WHOLE = (3, 4) + LEFT[0]


def share(group, stage, stream, ref, at):
    order, left = STREAM_ORDERS[stream], list(LAYOUT[group])
    for done in order[:stage]:
        left.remove(done)
    if group == "r" and order[stage] == 2:
        at = lax.rem(at, 2) * 2 + at // 2
    index = [slice(None)] * left.index(order[stage]) + [at]
    return ref.at[(stream, *index)]


def add_up(own, got, out, streams=3):
    count = out.shape[1] * out.shape[2] if len(out.shape) == 5 else out.shape[1]
    for n in range(streams):

        @pl.loop(0, count)
        def _(k, n=n):
            at = (k // 4, lax.rem(k, 4)) if len(out.shape) == 5 else (k,)
            total = own[n](at).astype(F32)
            for d in range(3):
                total += got[(n, d) + at].astype(F32)
            out[(n,) + at] = total.astype(out.dtype)


def chip_place():
    y = lax.axis_index("blk_0") * 2 + lax.axis_index("dp_2")
    return (lax.axis_index("dp_0"), lax.axis_index("dp_1"), y)


def stage_copies(group, stage, source, got, send, recv):
    place = chip_place()
    copies = []
    for d in (2, 1, 3):
        for n in range(3):
            axis = STREAM_ORDERS[n][stage]
            src = share(group, stage, n, source, lax.rem(place[axis] + d, 4))
            copies.append(remote(src, got.at[n, d - 1], send.at[n, d - 1], recv.at[n, d - 1], peer_of(axis, place, d)))
    return copies


def own_share(group, stage, stream, source):
    return share(group, stage, stream, source, chip_place()[STREAM_ORDERS[stream][stage]])


def own_loads(group, stage, source, held, got, got_held, sems):
    out = [pltpu.make_async_copy(own_share(group, stage, n, source), held.at[n], sems.at[n]) for n in range(3)]
    return out + [pltpu.make_async_copy(got, got_held, sems.at[3])]


def add_held(held, got, out):
    add_up([lambda at, n=n: held[(n,) + at] for n in range(3)], got, out)


def add_direct(group, stage, source, got, out):
    views = [own_share(group, stage, n, source) for n in range(3)]
    add_up([lambda at, v=v: v[at] for v in views], got, out)


def axis_peers(axes, offsets=(1, 2, 3)):
    place = chip_place()
    return [peer_of(a, place, d) for a in axes for d in offsets]


def landing(stage):
    return jax.ShapeDtypeStruct((3, 3) + LEFT[stage], BF)


def summed(stage):
    return (3,) + LEFT[stage]


def begin(copies):
    for c in copies:
        c.start()
    return copies


def end(copies):
    for c in copies:
        c.wait()


class Late:
    def __init__(self, source, held, sem):
        self.copy, self.held, self.waited = pltpu.make_async_copy(source, held, sem), held, False
        self.copy.start()

    def __call__(self):
        if not self.waited:
            self.copy.wait()
            self.waited = True
        return self.held


def pieces_of(grad):
    return [grad[:, k * 128 : (k + 1) * 128].reshape(4, 4, 48, 128) for k in range(3)]


def places():
    y_hi, core = lax.axis_index("blk_0"), lax.axis_index("blk_1")
    return y_hi, core, y_hi * 2 + core


def remote(src, dst, send, recv, device):
    return pltpu.make_async_remote_copy(
        src_ref=src, dst_ref=dst, send_sem=send, recv_sem=recv, device_id=device, device_id_type=MESH
    )


def rows_at(start, count):
    return pl.ds(pl.multiple_of(start, PIECE), count)


def greet(devices):
    barrier = pltpu.get_barrier_semaphore()
    for device in devices:
        pl.semaphore_signal(barrier, inc=1, device_id=device, device_id_type=MESH)
    pl.semaphore_wait(barrier, len(devices))


FAR = (256, ROWS)
EARLY = 192


def far_plan(layer, y_hi, core, block):
    if layer == 0:
        partner = {"blk_0": 1 - y_hi, "blk_1": 1 - core}
        return partner, jnp.where(block == 1, 128, 0), jnp.where(block == 1, 768, 512)
    return {"blk_0": 1 - y_hi}, 0, lax.rem(block + 2, 4) * ROWS


def is_middle(block):
    return jnp.logical_and(block >= 1, block <= 2)


def project_back_body(layer, rows, gq, parts, gres, dwo, wq, wk, wv, p0, gh, scratch, peers, hooks):
    (
        grads, near, far_near, gh_send, gh_got, qcat, kvcat, local, send, recv,
        held_rows, held_gq, held_gres, held_dwo, held_q, held_k, held_v, late,
    ) = scratch
    y_hi, core, block = places()
    far_rows = FAR[layer]
    sibling = {"blk_1": 1 - core}
    partner, give, theirs = far_plan(layer, y_hi, core, block)
    mine = columns_at(core * HALF, HALF)
    yours = columns_at((1 - core) * HALF, HALF)

    def hook(name):
        if name in hooks:
            hooks[name]()

    def talk(step):
        if layer == 0:
            pl.when(is_middle(block))(step)
        else:
            step()

    own = begin(
        [
            pltpu.make_async_copy(parts.at[:, rows_at(theirs, far_rows)], grads.at[:, pl.ds(ROWS, far_rows)], local.at[0]),
            pltpu.make_async_copy(parts.at[:, rows_at(block * ROWS, ROWS)], grads.at[:, pl.ds(0, ROWS)], local.at[1]),
            pltpu.make_async_copy(gq.at[:, mine], qcat.at[core], local.at[2]),
        ]
    )
    wk, wv = Late(wk.at[layer], held_k, late.at[0]), Late(wv.at[layer], held_v, late.at[1])
    dwo, rows = Late(dwo, held_dwo, late.at[2]), Late(rows, held_rows, late.at[3])
    gq_held, wq = Late(gq, held_gq, late.at[4]), Late(wq.at[layer], held_q, late.at[5])
    gres = Late(gres, held_gres, late.at[6])
    hook("loads")
    greet(peers or [sibling, partner] + axis_peers((0, 1, 2), (1, 2, 3)))
    beside = y_hi * 2 + 1 - core
    copies = []
    if layer == 1:
        at = (1 - y_hi) * 2 + 1 - core
        copies.append(remote(parts.at[:, rows_at(at * ROWS, ROWS)], far_near, send.at[0], recv.at[0], sibling))
    copies.append(remote(parts.at[:, rows_at(beside * ROWS, ROWS)], near, send.at[1], recv.at[1], sibling))
    half_q = remote(gq.at[:, yours], qcat.at[core], send.at[3], recv.at[3], sibling)
    begin(copies + [half_q])
    hook("greeted")

    def place_square(y, grad):
        for k, piece in enumerate(pieces_of(grad)):
            p0[k, y] = piece

    own[0].wait()
    wk(), wv()
    if layer == 1:
        copies[0].wait()
        grads[:, ROWS:] = (grads[:, ROWS:].astype(F32) + far_near[...].astype(F32)).astype(BF)
    hidden = remote(gh_send, gh_got, send.at[2], recv.at[2], partner)

    def far_part():
        gh_send[...] = (dot_nt(grads[0, ROWS:], wk()[...]) + dot_nt(grads[1, ROWS:], wv()[...])).astype(BF)
        hidden.start()

    talk(far_part)
    hook("far")
    own[1].wait()
    copies[-1].wait()
    grads[:, 0:ROWS] = (grads[:, 0:ROWS].astype(F32) + near[...].astype(F32)).astype(BF)
    half_kv = remote(grads.at[:, :, yours], kvcat.at[:, core], send.at[4], recv.at[4], sibling)
    half_kv.start()
    kvcat[:, core] = grads[:, :, mine]
    hook("near")
    place_square(1, dwo()[...])
    own[2].wait()
    half_q.wait()
    rows = rows()
    place_square(0, (dot_tn(rows[0, 0:ROWS], qcat[0]) + dot_tn(rows[1, 0:ROWS], qcat[1])).astype(BF))
    hook("two_squares")
    half_kv.wait()
    for side in (0, 1):
        cat = kvcat[side].reshape(2 * (ROWS + far_rows), HALF)
        place_square(2 + side, dot_tn(rows[...].reshape(2 * (ROWS + far_rows), D), cat).astype(BF))
    hook("squares")
    total = gres()[...] + dot_nt(gq_held()[...], wq()[...])
    total += dot_nt(grads[0, 0:ROWS], wk()[...]) + dot_nt(grads[1, 0:ROWS], wv()[...])
    if layer == 1:
        hidden.wait()
        gh[...] = (total + gh_got[...].astype(F32)).astype(gh.dtype)
    else:
        gh[...] = total.astype(gh.dtype)

        @pl.when(is_middle(block))
        def _():
            hidden.wait()
            here = rows_at(give, far_rows)
            gh[here, :] = (gh[here, :].astype(F32) + gh_got[...].astype(F32)).astype(gh.dtype)


def project_back_scratch(layer):
    far_rows, dma = FAR[layer], pltpu.SemaphoreType.DMA
    return [
        pltpu.VMEM((2, ROWS + far_rows, D), BF), pltpu.VMEM((2, ROWS, D), BF),
        pltpu.VMEM((2, far_rows, D), BF), pltpu.VMEM((far_rows, D), BF), pltpu.VMEM((far_rows, D), BF),
        pltpu.VMEM((2, ROWS, HALF), BF), pltpu.VMEM((2, 2, ROWS + far_rows, HALF), BF),
        dma((3,)), dma((5,)), dma((5,)),
        pltpu.VMEM((2, ROWS + far_rows, D), BF), pltpu.VMEM((ROWS, D), BF), pltpu.VMEM((ROWS, D), F32), pltpu.VMEM((D, HALF), BF),
        pltpu.VMEM((D, D), BF), pltpu.VMEM((D, D), BF), pltpu.VMEM((D, D), BF), dma((7,)),
    ]


def own_scratch(stage):
    return pltpu.VMEM(summed(stage), BF)


def got_scratch(stage):
    return pltpu.VMEM((3, 3) + LEFT[stage], BF)


def project_back_two_kernel(
    rows, gq, parts, gres, dwo, wq, wk, wv, low_all, gi, gi_other, r0, got_r0, p0_out, gh, e_out, s_r, got_r, *refs
):
    scratch, (p0, e, gicat, held_low, own_r, held_r, csems, gsems, osems, csend, crecv) = refs[:18], refs[18:]
    core = lax.axis_index("blk_1")
    loads_g, loads_r, carried = [], [], []

    def loads():
        loads_r.extend(begin(own_loads("r", 0, r0, own_r, got_r0, held_r, csems)))
        loads_g.extend(
            begin(
                [
                    pltpu.make_async_copy(gi.at[core], gicat.at[core], gsems.at[0]),
                    pltpu.make_async_copy(gi_other, gicat.at[1 - core], gsems.at[1]),
                    pltpu.make_async_copy(low_all, held_low, gsems.at[2]),
                ]
            )
        )

    def two_squares():
        end(loads_r)
        add_held(own_r, held_r, s_r)
        carried.extend(begin(stage_copies("r", 1, s_r, got_r, csend, crecv)))
        end(loads_g)
        for y in (0, 2):
            both = gicat[:, :, y * HALF : (y + 2) * HALF].reshape(2 * ROWS, 2 * HALF)
            grad = dot_tn(held_low[...].reshape(2 * ROWS, D), both).astype(BF)
            for k, piece in enumerate(pieces_of(grad[:, :HALF])):
                e[k, y] = piece
            for k, piece in enumerate(pieces_of(grad[:, HALF:])):
                e[k, y + 1] = piece
        carried.extend(begin([pltpu.make_async_copy(e, e_out, osems.at[0])]))

    def squares():
        carried.extend(begin([pltpu.make_async_copy(p0, p0_out, osems.at[1])]))

    hooks = dict(loads=loads, two_squares=two_squares, squares=squares)
    project_back_body(1, rows, gq, parts, gres, dwo, wq, wk, wv, p0, gh, scratch, None, hooks)
    end(carried)


def project_back_two(rows_all, gq, parts, gres, dwo, w, low_all, carry):
    shape, dma = jax.ShapeDtypeStruct, pltpu.SemaphoreType.DMA
    return pl.pallas_call(
        project_back_two_kernel,
        out_shape=(shape(WHOLE, BF), shape((ROWS, D), F32), shape(WHOLE, BF), shape(summed(0), BF), landing(1)),
        in_specs=[ANY] * 13,
        out_specs=(ANY, VMEM, ANY, VMEM, ANY),
        scratch_shapes=project_back_scratch(1)
        + [pltpu.VMEM(WHOLE, BF), pltpu.VMEM(WHOLE, BF), pltpu.VMEM((2, ROWS, STEPS * HALF), BF), pltpu.VMEM((2, ROWS, D), BF)]
        + [own_scratch(0), got_scratch(0), dma((4,)), dma((3,)), dma((2,)), dma((3, 3)), dma((3, 3))],
        compiler_params=pltpu.CompilerParams(collective_id=4, has_side_effects=True, vmem_limit_bytes=60 * MIB),
        name="project_back_1",
    )(rows_all, gq, parts.reshape(2, SLOTS * BLOCK, D), gres, dwo, w["query_weight"], w["key_weight"], w["value_weight"],
      low_all, *carry)


def slots_of(layer, tab, cnt, two, three, piece, head):
    block = lax.axis_index("blk_0") * 2 + lax.axis_index("blk_1")
    t = (3 * block + piece) // 4
    j = jnp.where(tab[0, 1] == t, 1, jnp.where(tab[0, 2] == t, 2, 0))
    live = jnp.where(j < cnt[0], 1.0, 0.0)
    if layer == 0:
        return t, live
    from_two = jnp.where(j < 2, two[head, jnp.minimum(j, 1)], j)
    chosen = jnp.where(cnt[0] == SLOTS, three[head, j], from_two)
    return tab[0, chosen], live


def left_lanes(rows=1):
    return lax.broadcasted_iota(jnp.int32, (rows, 2 * HD), 1) < HD


def two_heads(tile):
    left, none = left_lanes(PIECE), jnp.zeros_like(tile)
    return jnp.concatenate([jnp.where(left, tile, none), jnp.where(left, none, tile)], axis=0)


def own_columns(both):
    return jnp.where(left_lanes(PIECE), both[:PIECE], both[PIECE:])


def own_rows(both):
    top = lax.broadcasted_iota(jnp.int32, (2 * HD, PIECE), 0) < HD
    return jnp.where(top, both[:, :PIECE], both[:, PIECE:]).T


def slot_mask(s0, s1, t, kind):
    first, second = jnp.where(s0 == t, 1.0, 0.0), jnp.where(s1 == t, 1.0, 0.0)
    return jnp.where(left_lanes(), first, second).astype(kind)


def attend_specs():
    tile = pl.BlockSpec((ROWS, 2 * HD), lambda p: (0, p))
    keys = pl.BlockSpec((None, SLOTS, BLOCK, 2 * HD), lambda p: (0, 0, 0, p))
    values = pl.BlockSpec((None, SLOTS, BLOCK, 2 * HD), lambda p: (1, 0, 0, p))
    return tile, keys, values


def attend_back_step(layer, tab, cnt, two, three, q, k, v, gm, gq, gkv, acc):
    pair = pl.program_id(0)
    masks = []
    if layer == 0:
        acc[...] = jnp.zeros_like(acc)
    for i in range(3):
        rows = pl.ds(i * PIECE, PIECE)
        s0, live = slots_of(layer, tab, cnt, two, three, i, 2 * pair)
        if layer == 0:
            keys, values = k[s0], v[s0]
        else:
            s1, _ = slots_of(layer, tab, cnt, two, three, i, 2 * pair + 1)
            low = [slot_mask(s0, s1, t, BF) for t in range(SLOTS)]
            masks.append([slot_mask(s0, s1, t, F32) for t in range(SLOTS)])
            keys = k[0] * low[0] + k[1] * low[1] + k[2] * low[2]
            values = v[0] * low[0] + v[1] * low[1] + v[2] * low[2]
        qq = two_heads(q[rows, :] * jnp.asarray(SCALE, BF))
        gg = two_heads((gm[rows, :].astype(F32) * live).astype(BF))
        scores = dot_nt(keys, qq)
        exps = jnp.exp(scores - jnp.max(scores, axis=0, keepdims=True))
        factor = 1.0 / jnp.sum(exps, axis=0, keepdims=True)
        grad_weights = dot_nt(values, gg)
        delta = jnp.sum(exps * grad_weights, axis=0, keepdims=True) * factor
        weights = exps * factor
        grad_scores = (weights * (grad_weights - delta)).astype(BF)
        gq[rows, :] = (own_rows(dot_tn(keys, grad_scores)) * SCALE).astype(BF)
        gk = dot(grad_scores, qq)
        gv = dot(weights.astype(BF), gg)
        if layer == 0:
            acc[0, s0] += gk
            acc[1, s0] += gv
        else:
            acc[0, i] = gk
            acc[1, i] = gv
    if layer == 0:
        gkv[...] = acc[...].astype(BF)
    else:
        for side in range(2):
            for t in range(SLOTS):
                total = acc[side, 0] * masks[0][t] + acc[side, 1] * masks[1][t] + acc[side, 2] * masks[2][t]
                gkv[side, t] = total.astype(BF)


def attend_back_kernel(layer, tab, cnt, two, three, q, k, v, gm, e, r, gq, gkv, vec, got_e, got_r, acc, send, recv):
    step = pl.program_id(0)
    core = lax.axis_index("blk_1")

    def carried():
        copies = stage_copies("r", 0, r, got_r, send.at[0], recv.at[0])
        if layer == 0:
            return copies + stage_copies("e", 0, e, got_e, send.at[1], recv.at[1])
        return copies + [remote(e.at[1 - core], got_e, send.at[1, 0, 0], recv.at[1, 0, 0], {"blk_1": 1 - core})]

    peers = axis_peers((0, 1, 2)) + ([{"blk_1": 1 - core}] if layer == 1 else [])

    @pl.when(step == 0)
    def _():
        barrier = pltpu.get_barrier_semaphore()
        for peer in peers:
            pl.semaphore_signal(barrier, inc=1, device_id=peer, device_id_type=MESH)
        if layer == 0:
            pl.semaphore_wait(barrier, len(peers))
            begin(carried())

    attend_back_step(layer, tab, cnt, two, three, q, k, v, gm, gq, gkv, acc)
    vec[0:1] = jnp.sum(gq[...].astype(F32), axis=0, keepdims=True)
    total = jnp.zeros((1, 2 * HD), F32)
    for i in range(3):
        _, live = slots_of(0, tab, cnt, two, three, i, 0)
        total += live * jnp.sum(gm[i * PIECE : (i + 1) * PIECE, :].astype(F32), axis=0, keepdims=True)
    vec[1:2] = total

    if layer == 1:

        @pl.when(step == 0)
        def _():
            pl.semaphore_wait(pltpu.get_barrier_semaphore(), len(peers))
            begin(carried())

    @pl.when(step == HEADS // 2 - 1)
    def _():
        end(carried())


def attend_back(layer, table, q, kv_all, gm, e, r):
    tile, keys, values = attend_specs()
    both = pl.BlockSpec((2, SLOTS, BLOCK, 2 * HD), lambda p: (0, 0, 0, p))
    shape, dma = jax.ShapeDtypeStruct, pltpu.SemaphoreType.DMA
    landed = landing(0) if layer == 0 else shape((ROWS, STEPS * HALF), BF)
    return pl.pallas_call(
        functools.partial(attend_back_kernel, layer),
        grid=(HEADS // 2,),
        out_shape=(shape((ROWS, D), BF), shape((2, SLOTS, BLOCK, D), BF), shape((2, D), F32), landed, landing(0)),
        in_specs=[SMEM] * 4 + [tile, keys, values, tile, ANY, ANY],
        out_specs=(tile, both, pl.BlockSpec((2, 2 * HD), lambda p: (0, p)), ANY, ANY),
        scratch_shapes=[pltpu.VMEM((2, SLOTS, BLOCK, 2 * HD), F32), dma((2, 3, 3)), dma((2, 3, 3))],
        compiler_params=pltpu.CompilerParams(collective_id=9 + layer, has_side_effects=True, vmem_limit_bytes=60 * MIB),
        name=f"attend_back_{layer}",
    )(*table, q, kv_all, kv_all, gm, e, r)


STEPS = FF // CHUNK


def chunk_columns(j):
    return pl.ds(j * CHUNK, CHUNK)


def project_part(layer, h, early, wq, wk, wv, bq, bv, q, kv_all, rows_all, low, far, local, send, recv):
    y_hi, core, block = places()
    far_rows = FAR[layer]
    sibling = {"blk_1": 1 - core}
    partner, give, theirs = far_plan(layer, y_hi, core, block)
    low[...] = h[...].astype(BF)
    first = 0 if layer == 0 else EARLY
    rest = far.at[pl.ds(first, far_rows - first)]
    hidden = remote(low.at[pl.ds(pl.multiple_of(give + first, 64), far_rows - first)], rest, send.at[0], recv.at[0], partner)

    def talk(step):
        if layer == 0:
            pl.when(is_middle(block))(step)
        else:
            step()

    talk(lambda: hidden.start())
    if layer == 1:
        there = pltpu.make_async_copy(early, far.at[pl.ds(0, EARLY)], local.at[0])
        there.start()
    own_dst = rows_all.at[core, pl.ds(0, ROWS)]
    copies = begin([remote(low, own_dst, send.at[1], recv.at[1], sibling), pltpu.make_async_copy(low, own_dst, local.at[1])])

    def keys_of(source, count, start):
        at = rows_at(start, count) if count % PIECE == 0 else pl.ds(pl.multiple_of(start, 64), count)
        kv_all[0, at] = dot(source, wk()[...]).astype(BF)
        kv_all[1, at] = (dot(source, wv()[...]) + row_of(bv, layer)).astype(BF)
        return kv_all.at[:, at]

    mine = keys_of(low[...], ROWS, block * ROWS)
    copies += begin([remote(mine, mine, send.at[2], recv.at[2], sibling)])
    q[...] = (dot(low[...], wq()[...]) + row_of(bq, layer)).astype(BF)
    if layer == 1:
        there.wait()
        part = keys_of(far[0:EARLY], EARLY, theirs)
        copies += begin([remote(part, part, send.at[3], recv.at[3], sibling)])
    talk(lambda: hidden.wait())
    if layer == 0:

        @pl.when(jnp.logical_not(is_middle(block)))
        def _():
            far[...] = jnp.zeros_like(far)

    far_dst = rows_all.at[core, pl.ds(ROWS, far_rows)]
    copies += begin([remote(far, far_dst, send.at[4], recv.at[4], sibling), pltpu.make_async_copy(far, far_dst, local.at[2])])
    if layer == 0:
        talk(lambda: keys_of(far[...], far_rows, theirs) and None)
    else:
        part = keys_of(far[first:far_rows], far_rows - first, theirs + first)
        copies += begin([remote(part, part, send.at[5], recv.at[5], sibling)])
    end(copies)


def attend_part(layer, table, q, kv_all, mixed):
    @pl.loop(0, HEADS // 2)
    def _(pair):
        columns = columns_at(pair * 2 * HD, 2 * HD)

        def tile(side, slot):
            return kv_all[side, pl.ds(slot * BLOCK, BLOCK) if isinstance(slot, int) else rows_at(slot * BLOCK, BLOCK), columns]

        for i in range(3):
            rows = pl.ds(i * PIECE, PIECE)
            s0, live = slots_of(layer, *table, i, 2 * pair)
            if layer == 0:
                keys, values = tile(0, s0), tile(1, s0)
            else:
                s1, _ = slots_of(layer, *table, i, 2 * pair + 1)
                masks = [slot_mask(s0, s1, t, BF) for t in range(SLOTS)]
                keys, values = [sum(tile(side, t) * masks[t] for t in range(SLOTS)) for side in (0, 1)]
            scores = dot_nt(two_heads(q[rows, columns] * jnp.asarray(SCALE, BF)), keys)
            exps = jnp.exp(scores - jnp.max(scores, axis=1, keepdims=True))
            factor = live / jnp.sum(exps, axis=1, keepdims=True)
            mixed[rows, columns] = own_columns(dot(exps.astype(BF), values) * factor).astype(BF)


def tail_rows(layer, rows, h, mixed, wo, wes, wrs, vectors, r1, first, low, slope, r2, store, after_low):
    bo, g1, s1, be, br, g2, s2 = vectors
    residual = h[rows, :].astype(F32) + dot(mixed[rows, :], wo()[...]) + row_of(bo, layer)
    r1[rows, :] = residual
    normed, _ = norm_parts(residual)
    first[rows, :] = normed * row_of(g1, layer) + row_of(s1, layer)
    low[rows, :] = first[rows, :].astype(BF)
    after_low()
    total = first[rows, :] + row_of(br, layer)
    for j in range(STEPS):
        inner = dot(low[rows, :], wes[j]()[...]) + be[layer : layer + 1, j * CHUNK : (j + 1) * CHUNK].astype(F32)
        phi = 0.5 * (1.0 + lax.erf(inner * ROOT_HALF))
        low_act = (inner * phi).astype(BF)
        slope[j, rows, :] = (phi + inner * (INV_ROOT_TAU * jnp.exp(-0.5 * inner * inner))).astype(BF)
        store(j, low_act)
        total = total + dot(low_act, wrs[j]()[...])
    r2[rows, :] = total
    normed, _ = norm_parts(total)
    return normed * row_of(g2, layer) + row_of(s2, layer)


def weight_loads(layer, wq, wk, wv, wo, we, wr, held, sems):
    held_q, held_k, held_v, held_o, held_e, held_r = held
    wk, wv = Late(wk.at[layer], held_k, sems.at[0]), Late(wv.at[layer], held_v, sems.at[1])
    wq, wo = Late(wq.at[layer], held_q, sems.at[2]), Late(wo.at[layer], held_o, sems.at[3])
    wes = [Late(we.at[layer, :, chunk_columns(j)], held_e.at[j], sems.at[4 + 2 * j]) for j in range(STEPS)]
    wrs = [Late(wr.at[layer, chunk_columns(j)], held_r.at[j], sems.at[5 + 2 * j]) for j in range(STEPS)]
    return wq, wk, wv, wo, wes, wrs


def weight_scratch():
    square = pltpu.VMEM((D, D), BF)
    return [square] * 4 + [pltpu.VMEM((STEPS, D, CHUNK), BF), pltpu.VMEM((STEPS, CHUNK, D), BF), pltpu.SemaphoreType.DMA((2 * STEPS + 4,))]


def project_scratch(layer):
    dma = pltpu.SemaphoreType.DMA
    return [
        pltpu.VMEM((2, SLOTS * BLOCK, D), BF), pltpu.VMEM((ROWS, D), BF), pltpu.VMEM((FAR[layer], D), BF),
        dma((3,)), dma((6,)), dma((6,)),
    ]


def first_layer_kernel(tab, cnt, two, three, h, wq, wk, wv, wo, we, wr, bq, bv, bo, g1, s1, be, br, g2, s2, *refs):
    refs = list(refs)

    def take(count):
        out, refs[:count] = refs[:count], []
        return out

    q, kv_out, rows_all, r1_out, r2, out, slope_out, act_all, low_all, mixed_all, ahead = take(11)
    held, (wsems,) = take(6), take(1)
    kv_all, low_in, far, plocal, psend, precv = take(6)
    mixed, r1, first, low, act, slope, next_low, local, send, recv = take(10)
    y_hi, core, _ = places()
    sibling, partner = {"blk_1": 1 - core}, {"blk_0": 1 - y_hi}
    wq, wk, wv, wo, wes, wrs = weight_loads(0, wq, wk, wv, wo, we, wr, held, wsems)
    greet([sibling, partner, {"blk_0": 1 - y_hi, "blk_1": 1 - core}])
    project_part(0, h, None, wq, wk, wv, bq, bv, q, kv_all, rows_all, low_in, far, plocal, psend, precv)
    copies = begin([pltpu.make_async_copy(kv_all, kv_out, local.at[2 * STEPS + 3])])
    attend_part(0, (tab, cnt, two, three), q, kv_all, mixed)

    def both(src, dst, n):
        return [remote(src, dst, send.at[n], recv.at[n], sibling), pltpu.make_async_copy(src, dst, local.at[n])]

    copies += begin(both(mixed, mixed_all.at[core], STEPS))
    parts = [(0, EARLY), (EARLY, ROWS - EARLY)]
    for n, (start, count) in enumerate(parts):
        rows = pl.ds(start, count)
        final = n == len(parts) - 1

        def after_low():
            if final:
                copies.extend(begin(both(low, low_all.at[core], STEPS + 1)))
                copies.extend(begin([pltpu.make_async_copy(r1, r1_out, local.at[STEPS + 2])]))

        def store(j, low_act):
            act[j, rows, :] = low_act
            if final:
                copies.extend(begin(both(act.at[j], act_all.at[core, j], j)))
                copies.extend(
                    begin([pltpu.make_async_copy(slope.at[j], slope_out.at[:, chunk_columns(j)], local.at[STEPS + 3 + j])])
                )

        vectors = (bo, g1, s1, be, br, g2, s2)
        result = tail_rows(0, rows, h, mixed, wo, wes, wrs, vectors, r1, first, low, slope, r2, store, after_low)
        out[rows, :] = result
        if n == 0:
            next_low[...] = result.astype(BF)
            copies.extend(begin([remote(next_low, ahead, send.at[STEPS + 2], recv.at[STEPS + 2], partner)]))
    end(copies)


def weight_args(w):
    names = ("query_weight", "key_weight", "value_weight", "output_weight", "expand_weight", "reduce_weight", "query_bias",
             "value_bias", "output_bias", "first_gain", "first_shift", "expand_bias", "reduce_bias", "second_gain", "second_shift")
    return [w[name] for name in names]


def first_layer(h, table, w):
    dma, shape = pltpu.SemaphoreType.DMA, jax.ShapeDtypeStruct
    low, full = shape((ROWS, D), BF), shape((ROWS, D), F32)
    pair = shape((2, ROWS, D), BF)
    q, kv_all, rows_all, r1, r2, out, slope, act_all, low_all, mixed_all, early = pl.pallas_call(
        first_layer_kernel,
        out_shape=(
            low, shape((2, SLOTS * BLOCK, D), BF), shape((2, ROWS + FAR[0], D), BF), full, full, full, shape((ROWS, FF), BF),
            shape((2, STEPS, ROWS, CHUNK), BF), pair, pair, shape((EARLY, D), BF),
        ),
        in_specs=[SMEM] * 4 + [VMEM] + [ANY] * 6 + [VMEM] * 9,
        out_specs=(VMEM, ANY, ANY, ANY, VMEM, VMEM, ANY, ANY, ANY, ANY, ANY),
        scratch_shapes=weight_scratch() + project_scratch(0)
        + [pltpu.VMEM((ROWS, D), BF), pltpu.VMEM((ROWS, D), F32), pltpu.VMEM((ROWS, D), F32), pltpu.VMEM((ROWS, D), BF)]
        + [pltpu.VMEM((STEPS, ROWS, CHUNK), BF)] * 2
        + [pltpu.VMEM((EARLY, D), BF), dma((2 * STEPS + 4,)), dma((STEPS + 3,)), dma((STEPS + 3,))],
        compiler_params=pltpu.CompilerParams(collective_id=1, has_side_effects=True, vmem_limit_bytes=60 * MIB),
        name="first_layer",
    )(*table, h, *weight_args(w))
    saved = dict(
        rows_all=rows_all, q=q, kv_all=kv_all.reshape(2, SLOTS, BLOCK, D), r1=r1, r2=r2, slope=slope, act_all=act_all,
        low_all=low_all, mixed_all=mixed_all,
    )
    return out, early, saved


def second_layer_kernel(tab, cnt, two, three, h, early, g, wq, wk, wv, wo, we, wr, bq, bv, bo, g1, s1, be, br, g2, s2, *refs):
    refs = list(refs)

    def take(count):
        out, refs[:count] = refs[:count], []
        return out

    out, q, kv_out, rows_all, low_out, dwr_out, gi_out, dwo, gres, gm, vec, vec_e = take(12)
    held, (wsems,) = take(6), take(1)
    kv_all, low_in, far, plocal, psend, precv = take(6)
    r1, first, r2, act_all, low_all, mixed_all, slope, local, send, recv = take(10)
    scratch = take(11)
    _, core, _ = places()
    y_hi = lax.axis_index("blk_0")
    sibling, partner = {"blk_1": 1 - core}, {"blk_0": 1 - y_hi}
    wq, wk, wv, wo, wes, wrs = weight_loads(1, wq, wk, wv, wo, we, wr, held, wsems)
    greet([sibling, partner])
    project_part(1, h, early, wq, wk, wv, bq, bv, q, kv_all, rows_all, low_in, far, plocal, psend, precv)
    copies = begin([pltpu.make_async_copy(kv_all, kv_out, local.at[0])])
    mixed, low = mixed_all.at[core], low_all.at[core]
    attend_part(1, (tab, cnt, two, three), q, kv_all, mixed)

    def to_sibling(ref, n):
        return begin([remote(ref, ref, send.at[n], recv.at[n], sibling)])[0]

    shared = {"mixed": to_sibling(mixed, STEPS)}

    def after_low():
        shared["low"] = to_sibling(low, STEPS + 1)
        copies.extend(begin([pltpu.make_async_copy(low, low_out.at[core], local.at[1])]))

    def store(j, low_act):
        act_all[core, j] = low_act
        shared[j] = to_sibling(act_all.at[core, j], j)

    vectors = (bo, g1, s1, be, br, g2, s2)
    rows = pl.ds(0, ROWS)
    result = tail_rows(1, rows, h, mixed, wo, wes, wrs, vectors, r1, first, low, slope, r2, store, after_low)
    out[...] = result.astype(BF)

    def acts(j):
        shared[j].wait()
        return act_all[:, j]

    def mixed_pair():
        shared["mixed"].wait()
        return mixed_all[...]

    tail_back_part(
        1, g, lambda: r1[...], r2, acts, lambda j: slope[j], mixed_pair, None, wo, wes, wrs, g1, g2,
        (dwr_out, gi_out, dwo, gres, gm, vec, vec_e), scratch,
    )
    shared["low"].wait()
    copies += begin([pltpu.make_async_copy(low_all.at[1 - core], low_out.at[1 - core], local.at[2])])
    end(copies)


def second_layer(h, early, g, table, w):
    dma, shape = pltpu.SemaphoreType.DMA, jax.ShapeDtypeStruct
    low, full, pair = shape((ROWS, D), BF), shape((ROWS, D), F32), shape((2, ROWS, D), BF)
    whole = pltpu.VMEM((ROWS, D), F32)
    out, q, kv_all, rows_all, low_all, *rest = pl.pallas_call(
        second_layer_kernel,
        out_shape=(
            low, low, shape((2, SLOTS * BLOCK, D), BF), shape((2, ROWS + FAR[1], D), BF), pair,
            shape(WHOLE, BF), shape((2, ROWS, STEPS * HALF), BF), shape((D, HALF), BF), full, low,
            shape((8, D), F32), shape((1, FF), F32),
        ),
        in_specs=[SMEM] * 4 + [VMEM, ANY, VMEM] + [ANY] * 6 + [VMEM] * 9,
        out_specs=(VMEM, VMEM, ANY, ANY, ANY, ANY, ANY) + (VMEM,) * 5,
        scratch_shapes=weight_scratch() + project_scratch(1)
        + [whole, whole, whole, pltpu.VMEM((2, STEPS, ROWS, CHUNK), BF), pltpu.VMEM((2, ROWS, D), BF), pltpu.VMEM((2, ROWS, D), BF)]
        + [pltpu.VMEM((STEPS, ROWS, CHUNK), BF), dma((3,)), dma((STEPS + 2,)), dma((STEPS + 2,))]
        + tail_back_scratch(1),
        compiler_params=pltpu.CompilerParams(collective_id=2, has_side_effects=True, vmem_limit_bytes=62 * MIB),
        name="second_layer",
    )(*table, h, early, g, *weight_args(w))
    return out, dict(rows_all=rows_all, q=q, kv_all=kv_all.reshape(2, SLOTS, BLOCK, D), low_all=low_all), rest


def tail_back_part(layer, g, r1, r2, acts, slopes, mixed_all, low_all, wo, wes, wrs, g1, g2, outs, scratch):
    dwr_out, dwe_out, dwo, gres, gm, vec, vec_e = outs
    dwr, dwe, go, ga, gi, gocat, gacat, gicat, local, send, recv = scratch
    core = lax.axis_index("blk_1")
    sibling = {"blk_1": 1 - core}
    mine, yours = columns_at(core * HALF, HALF), columns_at((1 - core) * HALF, HALF)
    copies = []
    grad = g[...].astype(F32)
    normed, inv_std = norm_parts(r2[...])
    grad_r = norm_backward(grad, row_of(g2, layer), normed, inv_std)
    vec[0:1] = jnp.sum(grad * normed, axis=0, keepdims=True)
    vec[1:2] = jnp.sum(grad, axis=0, keepdims=True)
    total = grad_r
    go[...] = grad_r.astype(BF)
    vec[2:3] = jnp.sum(go[...].astype(F32), axis=0, keepdims=True)
    share_go = remote(go.at[:, yours], gocat.at[core], send.at[STEPS], recv.at[STEPS], sibling)
    share_go.start()
    gocat[core] = go[:, mine]
    shares = []

    def expand_gradient(j):
        shares[j].wait()
        part = dot_tn(low_all().reshape(2 * ROWS, D), gicat[j].reshape(2 * ROWS, HALF)).astype(BF)
        for k, piece in enumerate(pieces_of(part)):
            dwe[k, j] = piece
        copies.extend(begin([pltpu.make_async_copy(dwe.at[:, j], dwe_out.at[:, j], local.at[1, j])]))

    for j in range(STEPS):
        grad_inner = (dot_nt(go[...], wrs[j]()[...]) * slopes(j).astype(F32)).astype(BF)
        gi[j] = grad_inner
        if layer == 0:
            shares.append(remote(gi.at[j, :, yours], gicat.at[j, core], send.at[j], recv.at[j], sibling))
            shares[j].start()
            gicat[j, core] = gi[j, :, mine]
        else:
            for half in range(2):
                src = gi.at[j, :, pl.ds(half * HALF, HALF)]
                dst = dwe_out.at[half, :, pl.ds(j * HALF, HALF)]
                copies += begin([pltpu.make_async_copy(src, dst, local.at[1 + half, j])])
        vec_e[:, j * CHUNK : (j + 1) * CHUNK] = jnp.sum(grad_inner.astype(F32), axis=0, keepdims=True)
        total = total + dot_nt(grad_inner, wes[j]()[...])
        if j == 0:
            share_go.wait()
        part = dot_tn(acts(j).reshape(2 * ROWS, CHUNK), gocat[...].reshape(2 * ROWS, HALF)).astype(BF)
        for k, piece in enumerate(pieces_of(part)):
            dwr[k, j] = piece
        copies += begin([pltpu.make_async_copy(dwr.at[:, j], dwr_out.at[:, j], local.at[0, j])])
        if layer == 0 and j > 0:
            expand_gradient(j - 1)
    normed, inv_std = norm_parts(r1())
    grad_r = norm_backward(total, row_of(g1, layer), normed, inv_std)
    vec[3:4] = jnp.sum(total * normed, axis=0, keepdims=True)
    vec[4:5] = jnp.sum(total, axis=0, keepdims=True)
    gres[...] = grad_r
    ga[...] = grad_r.astype(BF)
    vec[5:6] = jnp.sum(ga[...].astype(F32), axis=0, keepdims=True)
    share_ga = remote(ga.at[:, yours], gacat.at[core], send.at[STEPS + 1], recv.at[STEPS + 1], sibling)
    share_ga.start()
    gacat[core] = ga[:, mine]
    if layer == 0:
        expand_gradient(STEPS - 1)
    gm[...] = dot_nt(ga[...], wo()[...]).astype(BF)
    share_ga.wait()
    dwo[...] = dot_tn(mixed_all().reshape(2 * ROWS, D), gacat[...].reshape(2 * ROWS, HALF)).astype(BF)
    end(copies)


def tail_back_scratch(layer):
    dma = pltpu.SemaphoreType.DMA
    return [
        pltpu.VMEM(WHOLE, BF), pltpu.VMEM(WHOLE if layer == 0 else (8, 128), BF),
        pltpu.VMEM((ROWS, D), BF), pltpu.VMEM((ROWS, D), BF), pltpu.VMEM((STEPS, ROWS, CHUNK), BF),
        pltpu.VMEM((2, ROWS, HALF), BF), pltpu.VMEM((2, ROWS, HALF), BF),
        pltpu.VMEM((STEPS, 2, ROWS, HALF) if layer == 0 else (8, 128), BF),
        dma((3, STEPS)), dma((STEPS + 2,)), dma((STEPS + 2,)),
    ]


def tail_back_kernel(g, r1, r2, low_all, act_all, slope, mixed_all, wo, we, wr, g1, g2, q_in, e_in, *refs):
    refs = list(refs)

    def take(count):
        out, refs[:count] = refs[:count], []
        return out

    outs, (got_q, got_e), scratch = take(7), take(2), take(11)
    held_wr, held_slope, held_we, held_act, held_r1, held_wo, held_mixed, held_low, late, csend, crecv = take(11)
    core = lax.axis_index("blk_1")
    wrs, slopes, wes, acts = [], [], [], []
    for j in range(STEPS):
        at = chunk_columns(j)
        wrs.append(Late(wr.at[0, at], held_wr.at[j], late.at[4 * j]))
        slopes.append(Late(slope.at[:, at], held_slope.at[j], late.at[4 * j + 1]))
        wes.append(Late(we.at[0, :, at], held_we.at[j], late.at[4 * j + 2]))
        acts.append(Late(act_all.at[:, j], held_act.at[j], late.at[4 * j + 3]))
    r1, wo = Late(r1, held_r1, late.at[4 * STEPS]), Late(wo.at[0], held_wo, late.at[4 * STEPS + 1])
    mixed_all = Late(mixed_all, held_mixed, late.at[4 * STEPS + 2])
    low_all = Late(low_all, held_low, late.at[4 * STEPS + 3])
    greet([{"blk_1": 1 - core}] + axis_peers((0, 1, 2)))
    carried = begin(stage_copies("q", 0, q_in, got_q, csend.at[0], crecv.at[0]))
    carried += begin(stage_copies("e", 0, e_in, got_e, csend.at[1], crecv.at[1]))
    tail_back_part(
        0, g, lambda: r1()[...], r2, lambda j: acts[j]()[...], lambda j: slopes[j]()[...], lambda: mixed_all()[...],
        lambda: low_all()[...], wo, wes, wrs, g1, g2, outs, scratch,
    )
    end(carried)


def tail_back(g, saved, w, carry):
    dma, shape = pltpu.SemaphoreType.DMA, jax.ShapeDtypeStruct
    return pl.pallas_call(
        tail_back_kernel,
        out_shape=(
            shape(WHOLE, BF), shape(WHOLE, BF), shape((D, HALF), BF), shape((ROWS, D), F32), shape((ROWS, D), BF),
            shape((8, D), F32), shape((1, FF), F32), landing(0), landing(0),
        ),
        in_specs=[VMEM, ANY, VMEM] + [ANY] * 7 + [VMEM, VMEM] + [ANY] * 2,
        out_specs=(ANY, ANY) + (VMEM,) * 5 + (ANY,) * 2,
        scratch_shapes=tail_back_scratch(0)
        + [
            pltpu.VMEM((STEPS, CHUNK, D), BF), pltpu.VMEM((STEPS, ROWS, CHUNK), BF), pltpu.VMEM((STEPS, D, CHUNK), BF),
            pltpu.VMEM((STEPS, 2, ROWS, CHUNK), BF), pltpu.VMEM((ROWS, D), F32), pltpu.VMEM((D, D), BF),
            pltpu.VMEM((2, ROWS, D), BF), pltpu.VMEM((2, ROWS, D), BF),
            dma((4 * STEPS + 4,)), dma((2, 3, 3)), dma((2, 3, 3)),
        ],
        compiler_params=pltpu.CompilerParams(collective_id=7, has_side_effects=True, vmem_limit_bytes=60 * MIB),
        name="tail_back_0",
    )(g, saved["r1"], saved["r2"], saved["low_all"], saved["act_all"], saved["slope"], saved["mixed_all"],
      w["output_weight"], w["expand_weight"], w["reduce_weight"], w["first_gain"], w["second_gain"], *carry)


VECTORS = 24


def last_kernel(*refs):
    refs = list(refs)

    def take(count):
        out, refs[:count] = refs[:count], []
        return out

    rows, gq, parts, gres, dwo, wq, wk, wv = take(8)
    e0, got_e0, r0, got_r0, q0_two, got_q0_two, e0_two, got_e0_two, r1_two, got_r1_two = take(10)
    vec_p, vec, vec_e, vec_p_two, vec_two, vec_e_two = take(6)
    gh, fix_got, rfix_got, v_out = take(4)
    scratch = take(18)
    p0, got_q0, own_q0, s_q0, got_q1, s_q1, got_q2 = take(7)
    own_e0, held_e0, s_e0, got_e1, s_e1, got_e2 = take(6)
    own_r0, held_r0, s_r0, got_r1, s_r1, got_r2 = take(6)
    own_q0_two, held_q0_two, s_q0_two, got_q1_two, s_q1_two, got_q2_two = take(6)
    own_e0_two, held_e0_two, s_e0_two, got_e1_two, s_e1_two, got_e2_two = take(6)
    own_r1_two, held_r1_two, s_r1_two, got_r2_two = take(4)
    fix_send, rfix_send, vsum, vgot, vtotal, vz, vx = take(7)
    local, send, recv, fsend, frecv, vsend, vrecv = take(7)

    place = chip_place()
    core = lax.axis_index("blk_1")
    pos = lax.axis_index("dp_2") * 4 + lax.axis_index("blk_0") * 2 + core
    other = 1 - core
    sibling = {"blk_1": other}
    loads, flights = [], {}

    def start_loads():
        loads.extend(
            [
                begin(own_loads("e", 0, e0, own_e0, got_e0, held_e0, local.at[0])),
                begin(own_loads("r", 0, r0, own_r0, got_r0, held_r0, local.at[1])),
                begin(own_loads("q", 0, q0_two, own_q0_two, got_q0_two, held_q0_two, local.at[2])),
                begin(own_loads("e", 0, e0_two, own_e0_two, got_e0_two, held_e0_two, local.at[3])),
                begin(own_loads("r", 1, r1_two, own_r1_two, got_r1_two, held_r1_two, local.at[4])),
            ]
        )
        vectors = [vec_p[0:1], vec_p[1:2]] + [vec[k : k + 1] for k in range(6)]
        vectors += [vec_p_two[0:1], vec_p_two[1:2]] + [vec_two[k : k + 1] for k in range(6)]
        vectors += [v[:, k * D : (k + 1) * D] for v in (vec_e, vec_e_two) for k in range(4)]
        for k, vector in enumerate(vectors):
            vsum[k // 3, k % 3 : k % 3 + 1] = vector
        for k in range(8):
            vsum[k, 3:8] = jnp.zeros((5, D), F32)

    def launch(key, group, stage, source, got, n):
        flights[key] = begin(stage_copies(group, stage, source, got, send.at[n], recv.at[n]))

    def to_all(source, dest, at):
        out = []
        for d in range(1, 8):
            t = lax.rem(pos + d, 8)
            out.append(remote(source(t), dest.at[pos], vsend.at[at + d], vrecv.at[at + d], pos_device(t)))
        return begin(out)

    def along(axis, got, at):
        return begin([remote(vtotal, got.at[d - 1], vsend.at[at + d], vrecv.at[at + d], peer_of(axis, place, d)) for d in (1, 2, 3)])

    def greeted():
        flights["vc"] = to_all(lambda t: vsum.at[t], vgot, 0)
        end(loads[0])
        add_held(own_e0, held_e0, s_e0)
        launch("e1", "e", 1, s_e0, got_e1, 0)
        end(loads[1])
        add_held(own_r0, held_r0, s_r0)
        launch("r1", "r", 1, s_r0, got_r1, 1)
        end(loads[2])
        add_held(own_q0_two, held_q0_two, s_q0_two)
        launch("q1_two", "q", 1, s_q0_two, got_q1_two, 2)
        end(loads[3])
        add_held(own_e0_two, held_e0_two, s_e0_two)
        launch("e1_two", "e", 1, s_e0_two, got_e1_two, 3)
        end(loads[4])
        add_held(own_r1_two, held_r1_two, s_r1_two)
        launch("r2_two", "r", 2, s_r1_two, got_r2_two, 4)

    def far_done():
        end(flights["vc"])
        vgot[pos] = vsum[pos]
        total = vgot[0]
        for k in range(1, 8):
            total = total + vgot[k]
        vtotal[...] = total
        flights["vz"] = along(0, vz, 7)

    def square_flights(half):
        out = []
        for d in (2, 1, 3):
            for n, axis in ((1, 1), (2, 0)):
                at, two = lax.rem(place[axis] + d, 4), pl.ds(2 * half, 2)
                src = p0.at[1, two, :, at] if n == 1 else p0.at[2, two, at]
                sems = send.at[12 + half, n, d - 1], recv.at[12 + half, n, d - 1]
                out.append(remote(src, got_q0.at[n, d - 1, two], *sems, peer_of(axis, place, d)))
        return out

    def square_along_y(d):
        to = lax.rem(place[2] + d, 4)
        return remote(p0.at[0, to], got_q0.at[0, d - 1], send.at[5, 0, d - 1], recv.at[5, 0, d - 1], peer_of(2, place, d))

    def launch_squares(half):
        for d in (2, 1, 3):
            pl.when(lax.rem(place[2] + d, 4) // 2 == half)(lambda d=d: square_along_y(d).start())
        begin(square_flights(half))

    def two_squares():
        launch_squares(0)

    def squares():
        launch_squares(1)
        end(flights["vz"])
        vtotal[...] = vtotal[...] + vz[0] + vz[1] + vz[2]
        flights["vx"] = along(1, vx, 10)
        end(flights["e1"])
        add_direct("e", 1, s_e0, got_e1, s_e1)
        launch("e2", "e", 2, s_e1, got_e2, 7)
        end(flights["r1"])
        add_direct("r", 1, s_r0, got_r1, s_r1)
        launch("r2", "r", 2, s_r1, got_r2, 8)
        end(flights["q1_two"])
        add_direct("q", 1, s_q0_two, got_q1_two, s_q1_two)
        launch("q2_two", "q", 2, s_q1_two, got_q2_two, 6)
        end(flights["e1_two"])
        add_direct("e", 1, s_e0_two, got_e1_two, s_e1_two)
        launch("e2_two", "e", 2, s_e1_two, got_e2_two, 11)

    peers = axis_peers((0, 1)) + [pos_device(lax.rem(pos + d, 8)) for d in range(1, 8)]
    hooks = dict(loads=start_loads, greeted=greeted, far=far_done, two_squares=two_squares, squares=squares)
    project_back_body(0, rows, gq, parts, gres, dwo, wq, wk, wv, p0, gh, scratch, peers, hooks)

    def last(group, source, got):
        thirds = []
        for n in range(3):
            total = own_share(group, 2, n, source)[...].astype(F32)
            for d in range(3):
                total += got[n, d].astype(F32)
            thirds.append(total)
        return jnp.concatenate(thirds, axis=1)

    def rows_out(layer, part, total):
        for k in range(8):
            fix_send[layer, part, k, 0:6] = total[6 * k : 6 * k + 6]
        out = []
        for d in range(1, 8):
            t = lax.rem(pos + d, 8)
            sems = fsend.at[layer, part, d], frecv.at[layer, part, d]
            out.append(remote(fix_send.at[layer, part, t], fix_got.at[layer, part, pos], *sems, pos_device(t)))
        return begin(out)

    def reduce_out(layer, total):
        rfix_send[layer] = total
        there, here = [pl.ds(pl.multiple_of(c * 24, 8), 24) for c in (other, core)]
        rfix_got[layer, core] = rfix_send[layer, here]
        sems = fsend.at[layer, 0, 0], frecv.at[layer, 0, 0]
        return begin([remote(rfix_send.at[layer, there], rfix_got.at[layer, core], *sems, sibling)])

    end(flights["vx"])
    vtotal[...] = vtotal[...] + vx[0] + vx[1] + vx[2]
    fixes = to_all(lambda t: vtotal, v_out, 13)
    v_out[pos] = vtotal[...]
    end(flights["r2_two"])
    fixes += reduce_out(1, last("r", s_r1_two, got_r2_two))
    end(flights["e2"])
    fixes += rows_out(0, 1, last("e", s_e1, got_e2))
    end(flights["r2"])
    fixes += reduce_out(0, last("r", s_r1, got_r2))
    end(flights["q2_two"])
    fixes += rows_out(1, 0, last("q", s_q1_two, got_q2_two))
    end(flights["e2_two"])
    fixes += rows_out(1, 1, last("e", s_e1_two, got_e2_two))
    for n in range(3):
        own_q0[n] = own_share("q", 0, n, p0)[...]
    end([square_along_y(d) for d in (1, 2, 3)] + square_flights(0) + square_flights(1))
    add_held(own_q0, got_q0, s_q0)
    launch("q1", "q", 1, s_q0, got_q1, 9)
    end(flights["q1"])
    add_direct("q", 1, s_q0, got_q1, s_q1)
    launch("q2", "q", 2, s_q1, got_q2, 10)
    end(flights["q2"])
    fixes += rows_out(0, 0, last("q", s_q1, got_q2))
    for layer in range(2):
        for part in range(2):
            fix_got[layer, part, pos] = fix_send[layer, part, pos]
    end(fixes)


def last_step(rows_all, gq, parts, gres, dwo, w, carry, vecs):
    dma, shape = pltpu.SemaphoreType.DMA, jax.ShapeDtypeStruct
    own, got = own_scratch, got_scratch
    return pl.pallas_call(
        last_kernel,
        out_shape=(shape((ROWS, D), BF), shape((2, 2, 8, 8, HALF), F32), shape((2, 2, 24, HALF), F32), shape((8, 8, D), F32)),
        in_specs=[ANY] * 18 + [VMEM] * 6,
        out_specs=[VMEM] * 4,
        scratch_shapes=project_back_scratch(0)
        + [pltpu.VMEM(WHOLE, BF), got(0), own(0), own(0), got(1), own(1), got(2)]
        + [own(0), got(0), own(0), got(1), own(1), got(2)] * 4
        + [own(1), got(1), own(1), got(2)]
        + [
            pltpu.VMEM((2, 2, 8, 8, HALF), F32),
            pltpu.VMEM((2, 48, HALF), F32),
            pltpu.VMEM((8, 8, D), F32),
            pltpu.VMEM((8, 8, D), F32),
            pltpu.VMEM((8, D), F32),
            pltpu.VMEM((3, 8, D), F32),
            pltpu.VMEM((3, 8, D), F32),
            dma((5, 4)), dma((14, 3, 3)), dma((14, 3, 3)), dma((2, 2, 8)), dma((2, 2, 8)), dma((21,)), dma((21,)),
        ],
        compiler_params=pltpu.CompilerParams(collective_id=3, has_side_effects=True, vmem_limit_bytes=60 * MIB),
        name="last_step",
    )(rows_all, gq, parts.reshape(2, SLOTS * BLOCK, D), gres, dwo, w["query_weight"], w["key_weight"], w["value_weight"], *carry, *vecs)


def finish_kernel(quads, rows, vecs, final, grad, *outs):
    me = lax.axis_index(DP_BLK)
    wq, wk, wv, wo, we, wr, q_b, v_b, s_g, s_s, r_b, f_g, f_s, o_b, e_b, final_out, grad_out = outs
    final_out[...] = final[...]
    grad_out[...] = grad[...]
    for layer in range(2):
        for s in range(8):
            y, c = (s // 2 % 2) * 2 + s // 4, s % 2
            (wq, wo, wk, wv)[y][:, layer, c * HALF : (c + 1) * HALF] = quads[layer, 0, s, 0:6]
            we[:, layer, y * D + c * HALF : y * D + (c + 1) * HALF] = quads[layer, 1, s, 0:6]
        for c in range(2):
            wr[layer, :, c * HALF : (c + 1) * HALF] = rows[layer, c]
    vectors = [vecs[k // 3, k % 3 : k % 3 + 1] for k in range(VECTORS)]
    turned = pltpu.roll(jnp.concatenate(vectors[0:16], axis=0), lax.rem(D - 6 * me, D), 1)
    for n, out in enumerate((q_b, v_b, s_g, s_s, r_b, f_g, f_s, o_b)):
        for layer in range(2):
            out[layer : layer + 1] = turned[8 * layer + n : 8 * layer + n + 1, 0:6]
    wide = pltpu.roll(jnp.concatenate(vectors[16:24], axis=0), lax.rem(D - 24 * lax.rem(me, 32), D), 1)
    for layer in range(2):
        total = jnp.zeros((1, 24), F32)
        for k in range(4):
            total = total + jnp.where(me // 32 == k, wide[4 * layer + k : 4 * layer + k + 1, 0:24], 0.0)
        e_b[layer : layer + 1] = total


def finish(quads, rows, vecs, final, grad):
    shape = jax.ShapeDtypeStruct
    square, small, hidden = shape((6, 2, D), F32), shape((2, 6), F32), shape((1, ROWS, D), BF)
    outs = pl.pallas_call(
        finish_kernel,
        out_shape=(square,) * 4 + (shape((6, 2, FF), F32), shape((2, 24, D), F32)) + (small,) * 8 + (shape((2, 24), F32),)
        + (hidden, hidden),
        in_specs=[VMEM] * 5,
        out_specs=(VMEM,) * 17,
        name="finish",
    )(quads, rows, vecs, final[None], grad[None])
    wq, wk, wv, wo, we = [o.transpose(1, 0, 2) for o in outs[:5]]
    wr, q_b, v_b, s_g, s_s, r_b, f_g, f_s, o_b, e_b, final, grad = outs[5:]
    return (final, grad, wq, wk, wv, wo, q_b, v_b, o_b, we, e_b, wr, r_b, f_g, f_s, s_g, s_s)


NAMES = (
    "query_weight", "key_weight", "value_weight", "output_weight", "query_bias", "value_bias", "output_bias", "expand_weight",
    "expand_bias", "reduce_weight", "reduce_bias", "first_gain", "first_shift", "second_gain", "second_shift",
)


def local(hidden, output_grad, block_counts, slot_table, block_order_two, block_order_three, *weights):
    w = dict(zip(NAMES, weights))
    table = (slot_table, block_counts, block_order_two, block_order_three)
    middle, early, saved_one = first_layer(hidden[0], table, w)
    final, saved_two, rest = second_layer(middle, early, output_grad[0], table, w)
    r_two, gi, dwo, gres, gm, vec_two, vec_e_two = rest
    gq, parts, vec_p_two, gi_other, got_r = attend_back(1, table, saved_two["q"], saved_two["kv_all"], gm, gi, r_two)
    carry = (gi, gi_other, r_two, got_r)
    q_two, grad_middle, e_two, r1, got_r = project_back_two(
        saved_two["rows_all"], gq, parts, gres, dwo, w, saved_two["low_all"], carry
    )
    r0, e0, dwo, gres, gm, vec, vec_e, got_q, got_e = tail_back(grad_middle, saved_one, w, (q_two, e_two))
    gq, parts, vec_p, got_e0, got_r0 = attend_back(0, table, saved_one["q"], saved_one["kv_all"], gm, e0, r0)
    carry = (e0, got_e0, r0, got_r0, q_two, got_q, e_two, got_e, r1, got_r)
    vecs = (vec_p, vec, vec_e, vec_p_two, vec_two, vec_e_two)
    grad_hidden, *sums = last_step(saved_one["rows_all"], gq, parts, gres, dwo, w, carry, vecs)
    return finish(*sums, final, grad_hidden)


def solution(mesh):
    finer = Mesh(mesh.devices.reshape(4, 4, 2, 2, 2), DP_BLK)
    in_specs = (P(DP, BLK, None), P(DP, BLK, None), P(DP), P(DP, None)) + (P(),) * 17
    wide, flat = P(None, DP_BLK, None), P(None, DP_BLK)
    out_specs = (P(DP, BLK, None), P(DP, BLK, None), wide, wide, wide, wide, flat, flat, flat, wide, flat, wide) + (flat,) * 5
    return jax.shard_map(local, mesh=finer, in_specs=in_specs, out_specs=out_specs, check_vma=False)
```

```python
import functools

import jax
import jax.numpy as jnp
from jax import lax
from jax.experimental import pallas as pl
from jax.experimental.pallas import tpu as pltpu
from jax.sharding import Mesh
from jax.sharding import PartitionSpec as P

D = 768
FF = 3072
HEADS = 12
HD = 64
BLOCK = 512
SLOTS = 3
ROWS = 384
PIECE = 128
CHUNK = 768
HALF = 384
BLK = ("blk_0", "blk_1")
DP_BLK = ("dp_0", "dp_1", "dp_2", "blk_0", "blk_1")
DP = ("dp_0", "dp_1", "dp_2")
EPSILON = 1e-06
ROOT_HALF = 0.7071067811865476
INV_ROOT_TAU = 0.3989422804014327
SCALE = HD ** (-0.5)
MESH = pl.DeviceIdType.MESH
BF = jnp.bfloat16
F32 = jnp.float32
MIB = 1024 * 1024
VMEM = pl.BlockSpec(memory_space=pltpu.VMEM)
SMEM = pl.BlockSpec(memory_space=pltpu.SMEM)
ANY = pl.BlockSpec(memory_space=pl.ANY)


def dot(left, right):
    return jnp.dot(left, right, preferred_element_type=F32)


def dot_nt(left, right):
    return lax.dot_general(left, right, (((1,), (1,)), ((), ())), preferred_element_type=F32)


def dot_tn(left, right):
    return lax.dot_general(left, right, (((0,), (0,)), ((), ())), preferred_element_type=F32)


def params(limit=60):
    return pltpu.CompilerParams(vmem_limit_bytes=limit * MIB)


def row_of(ref, layer):
    return ref[layer : layer + 1, :].astype(F32)


def norm_parts(residual):
    mean = jnp.mean(residual, axis=-1, keepdims=True)
    centred = residual - mean
    inv_std = lax.rsqrt(jnp.mean(centred * centred, axis=-1, keepdims=True) + EPSILON)
    return centred * inv_std, inv_std


def norm_backward(grad, gain, normed, inv_std):
    scaled = grad * gain
    return inv_std * (
        scaled
        - jnp.mean(scaled, axis=-1, keepdims=True)
        - normed * jnp.mean(scaled * normed, axis=-1, keepdims=True)
    )


def layer_block(layer, shape, index):
    return pl.BlockSpec((None,) + shape, lambda j: (layer,) + index(j))


def peer_of(axis, place, offset):
    at = lax.rem(place[axis] + offset, 4)
    if axis == 0:
        return {"dp_0": at}
    if axis == 1:
        return {"dp_1": at}
    return {"dp_2": lax.rem(at, 2), "blk_0": at // 2}


def pos_device(t):
    return {"dp_2": t // 4, "blk_0": lax.rem(t // 2, 2), "blk_1": lax.rem(t, 2)}


def columns_at(start, count):
    return pl.ds(pl.multiple_of(start, 128), count)


STREAM_ORDERS = ((2, 0, 1), (1, 2, 0), (0, 1, 2))
LAYOUT = {"q": (2, 0, 1), "e": (2, 0, 1), "r": (0, 1, 2)}
PIECES = (48, 128)
LEFT = ((4, 4) + PIECES, (4,) + PIECES, PIECES)
WHOLE = (3, 4) + LEFT[0]


def share(group, stage, stream, ref, at):
    order, left = STREAM_ORDERS[stream], list(LAYOUT[group])
    for done in order[:stage]:
        left.remove(done)
    if group == "r" and order[stage] == 2:
        at = lax.rem(at, 2) * 2 + at // 2
    index = [slice(None)] * left.index(order[stage]) + [at]
    return ref.at[(stream, *index)]


def add_up(own, got, out, streams=3):
    for n in range(streams):

        def part(at, n=n):
            total = own[n](at).astype(F32)
            for d in range(3):
                total += got[(n, d) + at].astype(F32)
            out[(n,) + at] = total.astype(out.dtype)

        if len(out.shape) == 5:
            pl.loop(0, 4)(lambda k, part=part: part((k,)))
        else:
            part((slice(None),))


def chip_place():
    y = lax.axis_index("blk_0") * 2 + lax.axis_index("dp_2")
    return (lax.axis_index("dp_0"), lax.axis_index("dp_1"), y)


def stage_copies(group, stage, source, got, send, recv, streams=(0, 1, 2)):
    place = chip_place()
    copies = []
    for d in (2, 1, 3):
        for n in streams:
            axis = STREAM_ORDERS[n][stage]
            src = share(group, stage, n, source, lax.rem(place[axis] + d, 4))
            copies.append(remote(src, got.at[n, d - 1], send.at[n, d - 1], recv.at[n, d - 1], peer_of(axis, place, d)))
    return copies


def own_share(group, stage, stream, source):
    return share(group, stage, stream, source, chip_place()[STREAM_ORDERS[stream][stage]])


def own_loads(group, stage, source, held, got, got_held, sems):
    out = [pltpu.make_async_copy(own_share(group, stage, n, source), held.at[n], sems.at[n]) for n in range(3)]
    return out + [pltpu.make_async_copy(got, got_held, sems.at[3])]


def add_held(held, got, out):
    add_up([lambda at, n=n: held[(n,) + at] for n in range(3)], got, out)


def add_direct(group, stage, source, got, out):
    views = [own_share(group, stage, n, source) for n in range(3)]
    add_up([lambda at, v=v: v[at] for v in views], got, out)


def axis_peers(axes, offsets=(1, 2, 3)):
    place = chip_place()
    return [peer_of(a, place, d) for a in axes for d in offsets]


def landing(stage):
    return jax.ShapeDtypeStruct((3, 3) + LEFT[stage], BF)


def summed(stage):
    return (3,) + LEFT[stage]


def begin(copies):
    for c in copies:
        c.start()
    return copies


def end(copies):
    for c in copies:
        c.wait()


class Late:
    def __init__(self, source, held, sem):
        self.copy, self.held, self.waited = pltpu.make_async_copy(source, held, sem), held, False
        self.copy.start()

    def __call__(self):
        if not self.waited:
            self.copy.wait()
            self.waited = True
        return self.held


def pieces_of(grad):
    return [grad[:, k * 128 : (k + 1) * 128].reshape(4, 4, 48, 128) for k in range(3)]


def places():
    y_hi, core = lax.axis_index("blk_0"), lax.axis_index("blk_1")
    return y_hi, core, y_hi * 2 + core


def remote(src, dst, send, recv, device):
    return pltpu.make_async_remote_copy(
        src_ref=src, dst_ref=dst, send_sem=send, recv_sem=recv, device_id=device, device_id_type=MESH
    )


def rows_at(start, count):
    return pl.ds(pl.multiple_of(start, PIECE), count)


def hail(devices):
    barrier = pltpu.get_barrier_semaphore()
    for device in devices:
        pl.semaphore_signal(barrier, inc=1, device_id=device, device_id_type=MESH)
    return lambda: pl.semaphore_wait(barrier, len(devices))


FAR = (256, ROWS)
EARLY = 192


def far_plan(layer, y_hi, core, block):
    if layer == 0:
        partner = {"blk_0": 1 - y_hi, "blk_1": 1 - core}
        return partner, jnp.where(block == 1, 128, 0), jnp.where(block == 1, 768, 512)
    return {"blk_0": 1 - y_hi}, 0, lax.rem(block + 2, 4) * ROWS


def is_middle(block):
    return jnp.logical_and(block >= 1, block <= 2)


def project_back_body(layer, rows, gq, parts, arrived, gres, dwo, weights, p0, gh, scratch, hooks):
    grads, near, far_near, gh_send, gh_got, qcat, kvcat, send, recv = scratch
    wq, wk, wv = weights
    y_hi, core, block = places()
    far_rows = FAR[layer]
    sibling = {"blk_1": 1 - core}
    partner, give, theirs = far_plan(layer, y_hi, core, block)
    mine = columns_at(core * HALF, HALF)
    yours = columns_at((1 - core) * HALF, HALF)

    def talk(step):
        if layer == 0:
            pl.when(is_middle(block))(step)
        else:
            step()

    half_q = remote(gq.at[:, yours], qcat.at[core], send.at[1], recv.at[1], sibling)
    half_q.start()
    end(arrived)
    far = parts[:, rows_at(theirs, far_rows)]
    if layer == 1:
        far = (far.astype(F32) + far_near[...].astype(F32)).astype(BF)
    grads[:, ROWS:] = far
    wk(), wv()
    hidden = remote(gh_send, gh_got, send.at[0], recv.at[0], partner)

    def far_part():
        gh_send[...] = (dot_nt(grads[0, ROWS:], wk()[...]) + dot_nt(grads[1, ROWS:], wv()[...])).astype(BF)
        hidden.start()

    talk(far_part)
    hooks["far"]()
    grads[:, 0:ROWS] = (parts[:, rows_at(block * ROWS, ROWS)].astype(F32) + near[...].astype(F32)).astype(BF)
    half_kv = remote(grads.at[:, :, yours], kvcat.at[:, core], send.at[2], recv.at[2], sibling)
    half_kv.start()
    qcat[core] = gq[:, mine]
    kvcat[:, core] = grads[:, :, mine]

    def place_square(y, grad):
        for k, piece in enumerate(pieces_of(grad)):
            p0[k, y] = piece

    place_square(1, dwo()[...])
    half_q.wait()
    rows = rows()
    place_square(0, (dot_tn(rows[0, 0:ROWS], qcat[0]) + dot_tn(rows[1, 0:ROWS], qcat[1])).astype(BF))
    hooks["two_squares"]()
    half_kv.wait()
    for side in (0, 1):
        cat = kvcat[side].reshape(2 * (ROWS + far_rows), HALF)
        place_square(2 + side, dot_tn(rows[...].reshape(2 * (ROWS + far_rows), D), cat).astype(BF))
    hooks["squares"]()
    total = gres()[...] + dot_nt(gq[...], wq()[...])
    total += dot_nt(grads[0, 0:ROWS], wk()[...]) + dot_nt(grads[1, 0:ROWS], wv()[...])
    if layer == 1:
        hidden.wait()
        gh[...] = (total + gh_got[...].astype(F32)).astype(gh.dtype)
    else:
        gh[...] = total.astype(gh.dtype)

        @pl.when(is_middle(block))
        def _():
            hidden.wait()
            here = rows_at(give, far_rows)
            gh[here, :] = (gh[here, :].astype(F32) + gh_got[...].astype(F32)).astype(gh.dtype)


def project_back_scratch(layer):
    far_rows, dma = FAR[layer], pltpu.SemaphoreType.DMA
    across = (2, far_rows, D) if layer == 1 else (8, 128)
    return [
        pltpu.VMEM((2, ROWS + far_rows, D), BF), pltpu.VMEM((2, ROWS, D), BF),
        pltpu.VMEM(across, BF), pltpu.VMEM((far_rows, D), BF), pltpu.VMEM((far_rows, D), BF),
        pltpu.VMEM((2, ROWS, HALF), BF), pltpu.VMEM((2, 2, ROWS + far_rows, HALF), BF),
        dma((3,)), dma((3,)),
    ]


def operand_scratch(layer):
    return [
        pltpu.VMEM((D, D), BF), pltpu.VMEM((D, D), BF), pltpu.VMEM((D, D), BF), pltpu.VMEM((2, ROWS + FAR[layer], D), BF),
        pltpu.VMEM((ROWS, D), F32), pltpu.VMEM((D, HALF), BF), pltpu.SemaphoreType.DMA((6,)),
    ]


def operand_loads(layer, wq, wk, wv, rows, gres, dwo, held):
    sems = held[-1]
    sources = (wq.at[layer], wk.at[layer], wv.at[layer], rows, gres, dwo)
    return [Late(source, into, sems.at[n]) for n, (source, into) in enumerate(zip(sources, held))]


def own_scratch(stage):
    return pltpu.VMEM(summed(stage), BF)


def got_scratch(stage):
    return pltpu.VMEM((3, 3) + LEFT[stage], BF)


def second_back_kernel(
    tab, cnt, two, three, q, kv, gm, gi, r0, low_all, rows, gres, dwo, wq, wk, wv, p0_out, gh, e_out, s_r, got_r, vec, got_e, *refs
):
    refs = list(refs)

    def take(count):
        out, refs[:count] = refs[:count], []
        return out

    held_q, held_kv, held_gm, gq, parts, acc, asems, asend, arecv = take(9)
    scratch, held = take(9), take(7)
    p0, e, gicat, held_low, own_r, held_r, csems, gsems, osems, rsend, rrecv, csend, crecv, esend, erecv = take(15)
    core = lax.axis_index("blk_1")
    table = (tab, cnt, two, three)
    met = hail([{"blk_1": 1 - core}] + axis_peers((0, 1, 2)))
    first = begin(
        [pltpu.make_async_copy(src, dst, asems.at[n]) for n, (src, dst) in enumerate(((q, held_q), (kv, held_kv), (gm, held_gm)))]
    )
    *weights, rows, gres, dwo = operand_loads(1, wq, wk, wv, rows, gres, dwo, held)
    loads = begin(
        [
            pltpu.make_async_copy(gi, gicat, gsems.at[0]),
            pltpu.make_async_copy(low_all, held_low, gsems.at[1]),
        ]
    )
    own_loads_r = begin([pltpu.make_async_copy(own_share("r", 0, n, r0), own_r.at[n], csems.at[n]) for n in range(3)])
    end(loads)
    for y in (0, 2):
        both = gicat[:, :, y * HALF : (y + 2) * HALF].reshape(2 * ROWS, 2 * HALF)
        grad = dot_tn(held_low[...].reshape(2 * ROWS, D), both).astype(BF)
        for k, piece in enumerate(pieces_of(grad[:, :HALF])):
            e[k, y] = piece
        for k, piece in enumerate(pieces_of(grad[:, HALF:])):
            e[k, y + 1] = piece
    met()
    travelling = begin(stage_copies("r", 0, r0, held_r, rsend, rrecv))
    carried = begin(stage_copies("e", 0, e, got_e, esend, erecv))
    carried += begin([pltpu.make_async_copy(e, e_out, osems.at[0])])
    end(first)
    arrived = attend_back_part(1, table, held_q, held_kv, held_gm, gq, parts, vec, acc, scratch[1], scratch[2], asend, arecv)

    def two_squares():
        end(own_loads_r + travelling)
        add_held(own_r, held_r, s_r)
        carried.extend(begin(stage_copies("r", 1, s_r, got_r, csend, crecv)))

    def squares():
        carried.extend(begin([pltpu.make_async_copy(p0, p0_out, osems.at[1])]))

    hooks = dict(far=lambda: None, two_squares=two_squares, squares=squares)
    project_back_body(1, rows, gq, parts, arrived, gres, dwo, weights, p0, gh, scratch, hooks)
    end(carried)


def second_back(table, saved, gm, gi, r0, gres, dwo, w):
    shape, dma = jax.ShapeDtypeStruct, pltpu.SemaphoreType.DMA
    return pl.pallas_call(
        second_back_kernel,
        out_shape=(
            shape(WHOLE, BF), shape((ROWS, D), F32), shape(WHOLE, BF), shape(summed(0), BF), landing(1), shape((2, D), F32),
            landing(0),
        ),
        in_specs=[SMEM] * 4 + [ANY] * 12,
        out_specs=(ANY, VMEM, ANY, VMEM, ANY, VMEM, ANY),
        scratch_shapes=attend_back_scratch() + project_back_scratch(1) + operand_scratch(1)
        + [pltpu.VMEM(WHOLE, BF), pltpu.VMEM(WHOLE, BF), pltpu.VMEM((2, ROWS, STEPS * HALF), BF), pltpu.VMEM((2, ROWS, D), BF)]
        + [own_scratch(0), got_scratch(0), dma((3,)), dma((2,)), dma((2,))] + [dma((3, 3))] * 6,
        compiler_params=pltpu.CompilerParams(collective_id=4, has_side_effects=True, vmem_limit_bytes=60 * MIB),
        name="second_back",
    )(*table, saved["q"], saved["kv_all"], gm, gi, r0, saved["low_all"], saved["rows_all"], gres, dwo,
      w["query_weight"], w["key_weight"], w["value_weight"])


def slots_of(layer, tab, cnt, two, three, piece, head):
    block = lax.axis_index("blk_0") * 2 + lax.axis_index("blk_1")
    t = (3 * block + piece) // 4
    j = jnp.where(tab[0, 1] == t, 1, jnp.where(tab[0, 2] == t, 2, 0))
    live = jnp.where(j < cnt[0], 1.0, 0.0)
    if layer == 0:
        return t, live
    from_two = jnp.where(j < 2, two[jnp.minimum(j, 1), head], j)
    chosen = jnp.where(cnt[0] == SLOTS, three[j, head], from_two)
    return tab[0, chosen], live


def left_lanes(rows=1):
    return lax.broadcasted_iota(jnp.int32, (rows, 2 * HD), 1) < HD


def two_heads(tile):
    left, none = left_lanes(PIECE), jnp.zeros_like(tile)
    return jnp.concatenate([jnp.where(left, tile, none), jnp.where(left, none, tile)], axis=0)


def own_columns(both):
    return jnp.where(left_lanes(PIECE), both[:PIECE], both[PIECE:])


def own_rows(both):
    top = lax.broadcasted_iota(jnp.int32, (2 * HD, PIECE), 0) < HD
    return jnp.where(top, both[:, :PIECE], both[:, PIECE:]).T


def slot_mask(s0, s1, t, kind):
    first, second = jnp.where(s0 == t, 1.0, 0.0), jnp.where(s1 == t, 1.0, 0.0)
    return jnp.where(left_lanes(), first, second).astype(kind)


def attend_back_step(layer, table, pair, columns, q, kv, gm, gq, parts, acc):
    masks = []
    if layer == 0:
        acc[...] = jnp.zeros_like(acc)
    for i in range(3):
        rows = pl.ds(i * PIECE, PIECE)
        s0, live = slots_of(layer, *table, i, 2 * pair)
        if layer == 0:
            keys, values = kv[0, s0, :, columns], kv[1, s0, :, columns]
        else:
            s1, _ = slots_of(layer, *table, i, 2 * pair + 1)
            low = [slot_mask(s0, s1, t, BF) for t in range(SLOTS)]
            masks.append([slot_mask(s0, s1, t, F32) for t in range(SLOTS)])
            keys, values = [sum(kv[side, t, :, columns] * low[t] for t in range(SLOTS)) for side in (0, 1)]
        qq = two_heads(q[rows, columns] * jnp.asarray(SCALE, BF))
        gg = two_heads((gm[rows, columns].astype(F32) * live).astype(BF))
        scores = dot_nt(keys, qq)
        exps = jnp.exp(scores - jnp.max(scores, axis=0, keepdims=True))
        factor = 1.0 / jnp.sum(exps, axis=0, keepdims=True)
        grad_weights = dot_nt(values, gg)
        delta = jnp.sum(exps * grad_weights, axis=0, keepdims=True) * factor
        weights = exps * factor
        grad_scores = (weights * (grad_weights - delta)).astype(BF)
        gq[rows, columns] = (own_rows(dot_tn(keys, grad_scores)) * SCALE).astype(BF)
        gk = dot(grad_scores, qq)
        gv = dot(weights.astype(BF), gg)
        if layer == 0:
            acc[0, s0] += gk
            acc[1, s0] += gv
        else:
            acc[0, i] = gk
            acc[1, i] = gv
    if layer == 0:
        parts[:, :, columns] = acc[...].reshape(2, SLOTS * BLOCK, 2 * HD).astype(BF)
    else:
        for side in range(2):
            for t in range(SLOTS):
                total = acc[side, 0] * masks[0][t] + acc[side, 1] * masks[1][t] + acc[side, 2] * masks[2][t]
                parts[side, t * BLOCK : (t + 1) * BLOCK, columns] = total.astype(BF)


def attend_back_part(layer, table, q, kv, gm, gq, parts, vec, acc, near, far_near, send, recv, halves=None):
    y_hi, core, _ = places()
    sibling = {"blk_1": 1 - core}

    def share(pair):
        columns = columns_at(pair * 2 * HD, 2 * HD)
        beside = rows_at((y_hi * 2 + 1 - core) * ROWS, ROWS)
        out = [remote(parts.at[:, beside, columns], near.at[:, :, columns], send.at[0, pair], recv.at[0, pair], sibling)]
        if layer == 1:
            across = rows_at(((1 - y_hi) * 2 + 1 - core) * ROWS, ROWS)
            out.append(
                remote(parts.at[:, across, columns], far_near.at[:, :, columns], send.at[1, pair], recv.at[1, pair], sibling)
            )
        return out

    def half_copies(i):
        theirs, hsend, hrecv = halves
        columns, to = columns_at(((1 - core) * 3 + i) * 2 * HD, 2 * HD), columns_at(i * 2 * HD, 2 * HD)
        out = []
        for n, (start, count, at) in enumerate(((y_hi * 2 * ROWS, 2 * ROWS, 0), (far_start(y_hi), FAR[0], 2 * ROWS))):
            src, dst = parts.at[:, rows_at(start, count), columns], theirs.at[:, pl.ds(at, count), to]
            out.append(remote(src, dst, hsend.at[n, i], hrecv.at[n, i], sibling))
        return out

    @pl.loop(0, HEADS // 2)
    def _(pair):
        columns = columns_at(pair * 2 * HD, 2 * HD)
        attend_back_step(layer, table, pair, columns, q, kv, gm, gq, parts, acc)
        if halves:

            @pl.when(pair // 3 == 1 - core)
            def _():
                begin(half_copies(lax.rem(pair, 3)))

        begin(share(pair))

    vec[0:1] = jnp.sum(gq[...].astype(F32), axis=0, keepdims=True)
    total = jnp.zeros((1, D), F32)
    for i in range(3):
        _, live = slots_of(0, *table, i, 0)
        total += live * jnp.sum(gm[i * PIECE : (i + 1) * PIECE, :].astype(F32), axis=0, keepdims=True)
    vec[1:2] = total
    arrived = [c for pair in range(HEADS // 2) for c in share(pair)]
    return (arrived, [c for i in range(3) for c in half_copies(i)]) if halves else arrived


def far_start(y_hi):
    return (1 - y_hi) * 256 + 512


def attend_back_scratch():
    dma = pltpu.SemaphoreType.DMA
    return [
        pltpu.VMEM((ROWS, D), BF), pltpu.VMEM((2, SLOTS, BLOCK, D), BF), pltpu.VMEM((ROWS, D), BF), pltpu.VMEM((ROWS, D), BF),
        pltpu.VMEM((2, SLOTS * BLOCK, D), BF), pltpu.VMEM((2, SLOTS, BLOCK, 2 * HD), F32),
        dma((3,)), dma((2, HEADS // 2)), dma((2, HEADS // 2)),
    ]


STEPS = FF // CHUNK


def chunk_columns(j):
    return pl.ds(j * CHUNK, CHUNK)


def project_part(layer, h, early, wq, wk, wv, bq, bv, q, kv_all, rows_all, low, far, local, send, recv):
    y_hi, core, block = places()
    far_rows = FAR[layer]
    sibling = {"blk_1": 1 - core}
    partner, give, theirs = far_plan(layer, y_hi, core, block)
    low[...] = h[...].astype(BF)
    first = 0 if layer == 0 else EARLY
    rest = far.at[pl.ds(first, far_rows - first)]
    hidden = remote(low.at[pl.ds(pl.multiple_of(give + first, 64), far_rows - first)], rest, send.at[0], recv.at[0], partner)

    def talk(step):
        if layer == 0:
            pl.when(is_middle(block))(step)
        else:
            step()

    talk(lambda: hidden.start())
    if layer == 1:
        there = pltpu.make_async_copy(early, far.at[pl.ds(0, EARLY)], local.at[0])
        there.start()
    own_dst = rows_all.at[core, pl.ds(0, ROWS)]
    copies, kept = [], begin([remote(low, own_dst, send.at[1], recv.at[1], sibling), pltpu.make_async_copy(low, own_dst, local.at[1])])

    def keys_of(source, count, start):
        at = rows_at(start, count) if count % PIECE == 0 else pl.ds(pl.multiple_of(start, 64), count)
        kv_all[0, at] = dot(source, wk()[...]).astype(BF)
        kv_all[1, at] = (dot(source, wv()[...]) + row_of(bv, layer)).astype(BF)
        return kv_all.at[:, at]

    mine = keys_of(low[...], ROWS, block * ROWS)
    copies += begin([remote(mine, mine, send.at[2], recv.at[2], sibling)])
    q[...] = (dot(low[...], wq()[...]) + row_of(bq, layer)).astype(BF)
    if layer == 1:
        there.wait()
        part = keys_of(far[0:EARLY], EARLY, theirs)
        copies += begin([remote(part, part, send.at[3], recv.at[3], sibling)])
    talk(lambda: hidden.wait())
    if layer == 0:

        @pl.when(jnp.logical_not(is_middle(block)))
        def _():
            far[...] = jnp.zeros_like(far)

    far_dst = rows_all.at[core, pl.ds(ROWS, far_rows)]
    kept += begin([remote(far, far_dst, send.at[4], recv.at[4], sibling), pltpu.make_async_copy(far, far_dst, local.at[2])])
    if layer == 0:
        talk(lambda: keys_of(far[...], far_rows, theirs) and None)
    else:
        part = keys_of(far[first:far_rows], far_rows - first, theirs + first)
        copies += begin([remote(part, part, send.at[5], recv.at[5], sibling)])
    end(copies)
    return kept


def attend_part(layer, table, q, kv_all, mixed):
    @pl.loop(0, HEADS // 2)
    def _(pair):
        columns = columns_at(pair * 2 * HD, 2 * HD)

        def tile(side, slot):
            return kv_all[side, pl.ds(slot * BLOCK, BLOCK) if isinstance(slot, int) else rows_at(slot * BLOCK, BLOCK), columns]

        for i in range(3):
            rows = pl.ds(i * PIECE, PIECE)
            s0, live = slots_of(layer, *table, i, 2 * pair)
            if layer == 0:
                keys, values = tile(0, s0), tile(1, s0)
            else:
                s1, _ = slots_of(layer, *table, i, 2 * pair + 1)
                masks = [slot_mask(s0, s1, t, BF) for t in range(SLOTS)]
                keys, values = [sum(tile(side, t) * masks[t] for t in range(SLOTS)) for side in (0, 1)]
            scores = dot_nt(two_heads(q[rows, columns] * jnp.asarray(SCALE, BF)), keys)
            exps = jnp.exp(scores - jnp.max(scores, axis=1, keepdims=True))
            factor = live / jnp.sum(exps, axis=1, keepdims=True)
            mixed[rows, columns] = own_columns(dot(exps.astype(BF), values) * factor).astype(BF)


def tail_rows(layer, rows, h, mixed, wo, wes, wrs, vectors, r1, first, low, slope, r2, store, after_low):
    bo, g1, s1, be, br, g2, s2 = vectors
    residual = h[rows, :].astype(F32) + dot(mixed[rows, :], wo()[...]) + row_of(bo, layer)
    r1[rows, :] = residual
    normed, _ = norm_parts(residual)
    first[rows, :] = normed * row_of(g1, layer) + row_of(s1, layer)
    low[rows, :] = first[rows, :].astype(BF)
    after_low()
    total = first[rows, :] + row_of(br, layer)
    for j in range(STEPS):
        inner = dot(low[rows, :], wes[j]()[...]) + be[layer : layer + 1, j * CHUNK : (j + 1) * CHUNK].astype(F32)
        phi = 0.5 * (1.0 + lax.erf(inner * ROOT_HALF))
        low_act = (inner * phi).astype(BF)
        slope[j, rows, :] = (phi + inner * (INV_ROOT_TAU * jnp.exp(-0.5 * inner * inner))).astype(BF)
        store(j, low_act)
        total = total + dot(low_act, wrs[j]()[...])
    r2[rows, :] = total
    normed, _ = norm_parts(total)
    return normed * row_of(g2, layer) + row_of(s2, layer)


def weight_loads(layer, wq, wk, wv, wo, we, wr, held, sems):
    held_q, held_k, held_v, held_o, held_e, held_r = held
    wk, wv = Late(wk.at[layer], held_k, sems.at[0]), Late(wv.at[layer], held_v, sems.at[1])
    wq, wo = Late(wq.at[layer], held_q, sems.at[2]), Late(wo.at[layer], held_o, sems.at[3])
    wes = [Late(we.at[layer, :, chunk_columns(j)], held_e.at[j], sems.at[4 + 2 * j]) for j in range(STEPS)]
    wrs = [Late(wr.at[layer, chunk_columns(j)], held_r.at[j], sems.at[5 + 2 * j]) for j in range(STEPS)]
    return wq, wk, wv, wo, wes, wrs


def weight_scratch():
    square = pltpu.VMEM((D, D), BF)
    return [square] * 4 + [pltpu.VMEM((STEPS, D, CHUNK), BF), pltpu.VMEM((STEPS, CHUNK, D), BF), pltpu.SemaphoreType.DMA((2 * STEPS + 4,))]


def project_scratch(layer):
    dma = pltpu.SemaphoreType.DMA
    return [
        pltpu.VMEM((2, SLOTS * BLOCK, D), BF), pltpu.VMEM((ROWS, D), BF), pltpu.VMEM((FAR[layer], D), BF),
        dma((3,)), dma((6,)), dma((6,)),
    ]


def first_layer_kernel(tab, cnt, two, three, h, wq, wk, wv, wo, we, wr, bq, bv, bo, g1, s1, be, br, g2, s2, *refs):
    refs = list(refs)

    def take(count):
        out, refs[:count] = refs[:count], []
        return out

    q, kv_out, rows_all, r1_out, r2, out, slope_out, act_all, low_all, mixed_all, ahead = take(11)
    held, (wsems,) = take(6), take(1)
    kv_all, low_in, far, plocal, psend, precv = take(6)
    mixed, r1, first, low, act, slope, next_low, local, send, recv = take(10)
    y_hi, core, _ = places()
    sibling, partner = {"blk_1": 1 - core}, {"blk_0": 1 - y_hi}
    met = hail([sibling, partner, {"blk_0": 1 - y_hi, "blk_1": 1 - core}])
    wq, wk, wv, wo, wes, wrs = weight_loads(0, wq, wk, wv, wo, we, wr, held, wsems)
    met()
    kept = project_part(0, h, None, wq, wk, wv, bq, bv, q, kv_all, rows_all, low_in, far, plocal, psend, precv)
    copies = kept + begin([pltpu.make_async_copy(kv_all, kv_out, local.at[2 * STEPS + 3])])
    attend_part(0, (tab, cnt, two, three), q, kv_all, mixed)

    def both(src, dst, n):
        return [remote(src, dst, send.at[n], recv.at[n], sibling), pltpu.make_async_copy(src, dst, local.at[n])]

    copies += begin(both(mixed, mixed_all.at[core], STEPS))
    parts = [(0, EARLY), (EARLY, ROWS - EARLY)]
    for n, (start, count) in enumerate(parts):
        rows = pl.ds(start, count)
        final = n == len(parts) - 1

        def after_low():
            if final:
                copies.extend(begin(both(low, low_all.at[core], STEPS + 1)))
                copies.extend(begin([pltpu.make_async_copy(r1, r1_out, local.at[STEPS + 2])]))

        def store(j, low_act):
            act[j, rows, :] = low_act
            if final:
                copies.extend(begin(both(act.at[j], act_all.at[core, j], j)))
                copies.extend(
                    begin([pltpu.make_async_copy(slope.at[j], slope_out.at[:, chunk_columns(j)], local.at[STEPS + 3 + j])])
                )

        vectors = (bo, g1, s1, be, br, g2, s2)
        result = tail_rows(0, rows, h, mixed, wo, wes, wrs, vectors, r1, first, low, slope, r2, store, after_low)
        out[rows, :] = result
        if n == 0:
            next_low[...] = result.astype(BF)
            copies.extend(begin([remote(next_low, ahead, send.at[STEPS + 2], recv.at[STEPS + 2], partner)]))
    end(copies)


def weight_args(w):
    names = ("query_weight", "key_weight", "value_weight", "output_weight", "expand_weight", "reduce_weight", "query_bias",
             "value_bias", "output_bias", "first_gain", "first_shift", "expand_bias", "reduce_bias", "second_gain", "second_shift")
    return [w[name] for name in names]


def first_layer(h, table, w):
    dma, shape = pltpu.SemaphoreType.DMA, jax.ShapeDtypeStruct
    low, full = shape((ROWS, D), BF), shape((ROWS, D), F32)
    pair = shape((2, ROWS, D), BF)
    q, kv_all, rows_all, r1, r2, out, slope, act_all, low_all, mixed_all, early = pl.pallas_call(
        first_layer_kernel,
        out_shape=(
            low, shape((2, SLOTS * BLOCK, D), BF), shape((2, ROWS + FAR[0], D), BF), full, full, full, shape((ROWS, FF), BF),
            shape((2, STEPS, ROWS, CHUNK), BF), pair, pair, shape((EARLY, D), BF),
        ),
        in_specs=[SMEM] * 4 + [VMEM] + [ANY] * 6 + [VMEM] * 9,
        out_specs=(VMEM, ANY, ANY, ANY, VMEM, VMEM, ANY, ANY, ANY, ANY, ANY),
        scratch_shapes=weight_scratch() + project_scratch(0)
        + [pltpu.VMEM((ROWS, D), BF), pltpu.VMEM((ROWS, D), F32), pltpu.VMEM((ROWS, D), F32), pltpu.VMEM((ROWS, D), BF)]
        + [pltpu.VMEM((STEPS, ROWS, CHUNK), BF)] * 2
        + [pltpu.VMEM((EARLY, D), BF), dma((2 * STEPS + 4,)), dma((STEPS + 3,)), dma((STEPS + 3,))],
        compiler_params=pltpu.CompilerParams(collective_id=1, has_side_effects=True, vmem_limit_bytes=60 * MIB),
        name="first_layer",
    )(*table, h, *weight_args(w))
    saved = dict(
        rows_all=rows_all, q=q, kv_all=kv_all.reshape(2, SLOTS, BLOCK, D), r1=r1, r2=r2, slope=slope, act_all=act_all,
        low_all=low_all, mixed_all=mixed_all,
    )
    return out, early, saved


def second_layer_kernel(tab, cnt, two, three, h, early, g, wq, wk, wv, wo, we, wr, bq, bv, bo, g1, s1, be, br, g2, s2, *refs):
    refs = list(refs)

    def take(count):
        out, refs[:count] = refs[:count], []
        return out

    out, q, kv_out, rows_all, low_out, dwr_out, gi_out, dwo, gres, gm, vec, vec_e = take(12)
    held, (wsems,) = take(6), take(1)
    kv_all, low_in, far, plocal, psend, precv = take(6)
    r1, first, r2, act_all, low_all, mixed_all, slope, local, send, recv = take(10)
    scratch = take(11)
    _, core, _ = places()
    y_hi = lax.axis_index("blk_0")
    sibling, partner = {"blk_1": 1 - core}, {"blk_0": 1 - y_hi}
    met = hail([sibling, partner])
    wq, wk, wv, wo, wes, wrs = weight_loads(1, wq, wk, wv, wo, we, wr, held, wsems)
    met()
    kept = project_part(1, h, early, wq, wk, wv, bq, bv, q, kv_all, rows_all, low_in, far, plocal, psend, precv)
    copies = kept + begin([pltpu.make_async_copy(kv_all, kv_out, local.at[0])])
    mixed, low = mixed_all.at[core], low_all.at[core]
    attend_part(1, (tab, cnt, two, three), q, kv_all, mixed)

    def to_sibling(ref, n):
        return begin([remote(ref, ref, send.at[n], recv.at[n], sibling)])[0]

    shared = {"mixed": to_sibling(mixed, STEPS)}

    def after_low():
        shared["low"] = to_sibling(low, STEPS + 1)
        copies.extend(begin([pltpu.make_async_copy(low, low_out.at[core], local.at[1])]))

    def store(j, low_act):
        act_all[core, j] = low_act
        shared[j] = to_sibling(act_all.at[core, j], j)

    vectors = (bo, g1, s1, be, br, g2, s2)
    rows = pl.ds(0, ROWS)
    result = tail_rows(1, rows, h, mixed, wo, wes, wrs, vectors, r1, first, low, slope, r2, store, after_low)
    out[...] = result.astype(BF)

    def acts(j):
        shared[j].wait()
        return act_all[:, j]

    def mixed_pair():
        shared["mixed"].wait()
        return mixed_all[...]

    tail_back_part(
        1, g, lambda: r1[...], r2, acts, lambda j: slope[j], mixed_pair, None, wo, wes, wrs, g1, g2,
        (dwr_out, gi_out, dwo, gres, gm, vec, vec_e), scratch,
    )
    shared["low"].wait()
    copies += begin([pltpu.make_async_copy(low_all.at[1 - core], low_out.at[1 - core], local.at[2])])
    end(copies)


def second_layer(h, early, g, table, w):
    dma, shape = pltpu.SemaphoreType.DMA, jax.ShapeDtypeStruct
    low, full, pair = shape((ROWS, D), BF), shape((ROWS, D), F32), shape((2, ROWS, D), BF)
    whole = pltpu.VMEM((ROWS, D), F32)
    out, q, kv_all, rows_all, low_all, *rest = pl.pallas_call(
        second_layer_kernel,
        out_shape=(
            low, low, shape((2, SLOTS * BLOCK, D), BF), shape((2, ROWS + FAR[1], D), BF), pair,
            shape(WHOLE, BF), shape((2, ROWS, STEPS * HALF), BF), shape((D, HALF), BF), full, low,
            shape((8, D), F32), shape((1, FF), F32),
        ),
        in_specs=[SMEM] * 4 + [VMEM, ANY, VMEM] + [ANY] * 6 + [VMEM] * 9,
        out_specs=(VMEM, VMEM, ANY, ANY, ANY, ANY, ANY) + (VMEM,) * 5,
        scratch_shapes=weight_scratch() + project_scratch(1)
        + [whole, whole, whole, pltpu.VMEM((2, STEPS, ROWS, CHUNK), BF), pltpu.VMEM((2, ROWS, D), BF), pltpu.VMEM((2, ROWS, D), BF)]
        + [pltpu.VMEM((STEPS, ROWS, CHUNK), BF), dma((3,)), dma((STEPS + 2,)), dma((STEPS + 2,))]
        + tail_back_scratch(1),
        compiler_params=pltpu.CompilerParams(collective_id=2, has_side_effects=True, vmem_limit_bytes=62 * MIB),
        name="second_layer",
    )(*table, h, early, g, *weight_args(w))
    return out, dict(rows_all=rows_all, q=q, kv_all=kv_all.reshape(2, SLOTS, BLOCK, D), low_all=low_all), rest


def chunk_of(layer, j):
    return j if layer == 1 else lax.rem(lax.axis_index("dp_0") + 1 + j, STEPS)


def tail_back_part(layer, g, r1, r2, acts, slopes, mixed_all, low_all, wo, wes, wrs, g1, g2, outs, scratch, send_chunk=None):
    dwr_out, dwe_out, dwo, gres, gm, vec, vec_e = outs
    dwr, dwe, go, ga, gi, gocat, gacat, gicat, local, send, recv = scratch
    core = lax.axis_index("blk_1")
    sibling = {"blk_1": 1 - core}
    mine, yours = columns_at(core * HALF, HALF), columns_at((1 - core) * HALF, HALF)
    copies = []
    grad = g[...].astype(F32)
    normed, inv_std = norm_parts(r2[...])
    grad_r = norm_backward(grad, row_of(g2, layer), normed, inv_std)
    vec[0:1] = jnp.sum(grad * normed, axis=0, keepdims=True)
    vec[1:2] = jnp.sum(grad, axis=0, keepdims=True)
    total = grad_r
    go[...] = grad_r.astype(BF)
    vec[2:3] = jnp.sum(go[...].astype(F32), axis=0, keepdims=True)
    share_go = remote(go.at[:, yours], gocat.at[core], send.at[STEPS], recv.at[STEPS], sibling)
    share_go.start()
    gocat[core] = go[:, mine]
    shares = []

    def expand_gradient(j):
        shares[j].wait()
        part = dot_tn(low_all().reshape(2 * ROWS, D), gicat[j].reshape(2 * ROWS, HALF)).astype(BF)
        at = chunk_of(layer, j)
        for k, piece in enumerate(pieces_of(part)):
            dwe[k, at] = piece
        copies.extend(begin([pltpu.make_async_copy(dwe.at[:, at], dwe_out.at[:, at], local.at[1, j])]))

    for j in range(STEPS):
        grad_inner = (dot_nt(go[...], wrs[j]()[...]) * slopes(j).astype(F32)).astype(BF)
        gi[j] = grad_inner
        if layer == 0:
            shares.append(remote(gi.at[j, :, yours], gicat.at[j, core], send.at[j], recv.at[j], sibling))
            shares[j].start()
            gicat[j, core] = gi[j, :, mine]
        else:
            dst = dwe_out.at[core, :, pl.ds(j * HALF, HALF)]
            copies += begin([pltpu.make_async_copy(gi.at[j, :, mine], dst, local.at[1, j])])
            copies += begin([remote(gi.at[j, :, yours], dst, send.at[j], recv.at[j], sibling)])
        at = chunk_of(layer, j)
        vec_e[:, columns_at(at * CHUNK, CHUNK)] = jnp.sum(grad_inner.astype(F32), axis=0, keepdims=True)
        total = total + dot_nt(grad_inner, wes[j]()[...])
        if j == 0:
            share_go.wait()
        part = dot_tn(acts(j).reshape(2 * ROWS, CHUNK), gocat[...].reshape(2 * ROWS, HALF)).astype(BF)
        for k, piece in enumerate(pieces_of(part)):
            dwr[k, at] = piece
        copies += begin([pltpu.make_async_copy(dwr.at[:, at], dwr_out.at[:, at], local.at[0, j])])
        if send_chunk:
            send_chunk(j, at, dwr)
        if layer == 0 and j > 0:
            expand_gradient(j - 1)
    normed, inv_std = norm_parts(r1())
    grad_r = norm_backward(total, row_of(g1, layer), normed, inv_std)
    vec[3:4] = jnp.sum(total * normed, axis=0, keepdims=True)
    vec[4:5] = jnp.sum(total, axis=0, keepdims=True)
    gres[...] = grad_r
    ga[...] = grad_r.astype(BF)
    vec[5:6] = jnp.sum(ga[...].astype(F32), axis=0, keepdims=True)
    share_ga = remote(ga.at[:, yours], gacat.at[core], send.at[STEPS + 1], recv.at[STEPS + 1], sibling)
    share_ga.start()
    gacat[core] = ga[:, mine]
    if layer == 0:
        expand_gradient(STEPS - 1)
    gm[...] = dot_nt(ga[...], wo()[...]).astype(BF)
    share_ga.wait()
    dwo[...] = dot_tn(mixed_all().reshape(2 * ROWS, D), gacat[...].reshape(2 * ROWS, HALF)).astype(BF)
    end(copies)


def tail_back_scratch(layer):
    dma = pltpu.SemaphoreType.DMA
    return [
        pltpu.VMEM(WHOLE, BF), pltpu.VMEM(WHOLE if layer == 0 else (8, 128), BF),
        pltpu.VMEM((ROWS, D), BF), pltpu.VMEM((ROWS, D), BF), pltpu.VMEM((STEPS, ROWS, CHUNK), BF),
        pltpu.VMEM((2, ROWS, HALF), BF), pltpu.VMEM((2, ROWS, HALF), BF),
        pltpu.VMEM((STEPS, 2, ROWS, HALF) if layer == 0 else (8, 128), BF),
        dma((3, STEPS)), dma((STEPS + 2,)), dma((STEPS + 2,)),
    ]


def tail_back_kernel(g, r1, r2, low_all, act_all, slope, mixed_all, wo, we, wr, g1, g2, q_in, *refs):
    refs = list(refs)

    def take(count):
        out, refs[:count] = refs[:count], []
        return out

    outs, (got_q, got_r), scratch = take(7), take(2), take(11)
    held_wr, held_slope, held_we, held_act, held_r1, held_wo, held_mixed, held_low, late, csend, crecv, rsend, rrecv = take(13)
    core = lax.axis_index("blk_1")
    met = hail([{"blk_1": 1 - core}] + axis_peers((0, 1, 2)))
    wrs, slopes, wes, acts = [], [], [], []
    for j in range(STEPS):
        at = columns_at(chunk_of(0, j) * CHUNK, CHUNK)
        wrs.append(Late(wr.at[0, at], held_wr.at[j], late.at[4 * j]))
        slopes.append(Late(slope.at[:, at], held_slope.at[j], late.at[4 * j + 1]))
        wes.append(Late(we.at[0, :, at], held_we.at[j], late.at[4 * j + 2]))
        acts.append(Late(act_all.at[:, chunk_of(0, j)], held_act.at[j], late.at[4 * j + 3]))
    r1, wo = Late(r1, held_r1, late.at[4 * STEPS]), Late(wo.at[0], held_wo, late.at[4 * STEPS + 1])
    mixed_all = Late(mixed_all, held_mixed, late.at[4 * STEPS + 2])
    low_all = Late(low_all, held_low, late.at[4 * STEPS + 3])
    met()
    carried = begin(stage_copies("q", 0, q_in, got_q, csend, crecv))
    place = chip_place()

    def send_chunk(j, at, dwr):
        for d in (2, 1, 3):
            for n, axis in ((0, 2), (1, 1)):
                to = lax.rem(place[axis] + d, 4)
                src = dwr.at[0, at, :, lax.rem(to, 2) * 2 + to // 2] if n == 0 else dwr.at[1, at, to]
                sems = rsend.at[n, d - 1, j], rrecv.at[n, d - 1, j]
                carried.extend(begin([remote(src, got_r.at[n, d - 1, at], *sems, peer_of(axis, place, d))]))
        if j < STEPS - 1:
            sems = rsend.at[2, j, 0], rrecv.at[2, j, 0]
            carried.extend(begin([remote(dwr.at[2, at], got_r.at[2, j], *sems, peer_of(0, place, j + 1))]))

    tail_back_part(
        0, g, lambda: r1()[...], r2, lambda j: acts[j]()[...], lambda j: slopes[j]()[...], lambda: mixed_all()[...],
        lambda: low_all()[...], wo, wes, wrs, g1, g2, outs, scratch, send_chunk,
    )
    end(carried)


def tail_back(g, saved, w, carry):
    dma, shape = pltpu.SemaphoreType.DMA, jax.ShapeDtypeStruct
    return pl.pallas_call(
        tail_back_kernel,
        out_shape=(
            shape(WHOLE, BF), shape(WHOLE, BF), shape((D, HALF), BF), shape((ROWS, D), F32), shape((ROWS, D), BF),
            shape((8, D), F32), shape((1, FF), F32), landing(0), landing(0),
        ),
        in_specs=[VMEM, ANY, VMEM] + [ANY] * 7 + [VMEM, VMEM, ANY],
        out_specs=(ANY, ANY) + (VMEM,) * 5 + (ANY,) * 2,
        scratch_shapes=tail_back_scratch(0)
        + [
            pltpu.VMEM((STEPS, CHUNK, D), BF), pltpu.VMEM((STEPS, ROWS, CHUNK), BF), pltpu.VMEM((STEPS, D, CHUNK), BF),
            pltpu.VMEM((STEPS, 2, ROWS, CHUNK), BF), pltpu.VMEM((ROWS, D), F32), pltpu.VMEM((D, D), BF),
            pltpu.VMEM((2, ROWS, D), BF), pltpu.VMEM((2, ROWS, D), BF),
            dma((4 * STEPS + 4,)), dma((3, 3)), dma((3, 3)), dma((3, 3, STEPS)), dma((3, 3, STEPS)),
        ],
        compiler_params=pltpu.CompilerParams(collective_id=7, has_side_effects=True, vmem_limit_bytes=60 * MIB),
        name="tail_back_0",
    )(g, saved["r1"], saved["r2"], saved["low_all"], saved["act_all"], saved["slope"], saved["mixed_all"],
      w["output_weight"], w["expand_weight"], w["reduce_weight"], w["first_gain"], w["second_gain"], *carry)


VECTORS = 24


def last_kernel(*refs):
    refs = list(refs)

    def take(count):
        out, refs[:count] = refs[:count], []
        return out

    table, (q, kv, gm, rows, gres, dwo, wq, wk, wv, e0, r0, got_r0) = take(4), take(12)
    q0_two, got_q0_two, e0_two, got_e0_two, r1_two, got_r1_two = take(6)
    vec, vec_e, vec_p_two, vec_two, vec_e_two = take(5)
    gh, fix_got, rfix_got, v_out = take(4)
    held_q, held_kv, held_gm, gq, parts, acc, asems, asend, arecv = take(9)
    scratch, held = take(9), take(7)
    p0, got_q0, s_q0, got_q1, s_q1, got_q2 = take(6)
    own_e0, held_e0, s_e0, got_e1, s_e1, got_e2 = take(6)
    own_r0, held_r0, s_r0, got_r1, s_r1, got_r2 = take(6)
    own_q0_two, held_q0_two, s_q0_two, got_q1_two, s_q1_two, got_q2_two = take(6)
    own_e0_two, held_e0_two, s_e0_two, got_e1_two, s_e1_two, got_e2_two = take(6)
    own_r1_two, held_r1_two, s_r1_two, got_r2_two = take(4)
    fix_send, rfix_send, vsum, vgot, vtotal, vz, vx, vec_p, half_got = take(9)
    local, send, recv, fsend, frecv, vsend, vrecv, hsend, hrecv = take(9)

    place = chip_place()
    core = lax.axis_index("blk_1")
    pos = lax.axis_index("dp_2") * 4 + lax.axis_index("blk_0") * 2 + core
    other = 1 - core
    sibling = {"blk_1": other}
    flights = {}
    met = hail(axis_peers((0, 1)) + [pos_device(lax.rem(pos + d, 8)) for d in range(1, 8)])
    first = begin(
        [pltpu.make_async_copy(src, dst, asems.at[n]) for n, (src, dst) in enumerate(((q, held_q), (kv, held_kv), (gm, held_gm)))]
    )
    loads = [
        begin(own_loads("q", 0, q0_two, own_q0_two, got_q0_two, held_q0_two, local.at[0])),
        begin(own_loads("e", 0, e0_two, own_e0_two, got_e0_two, held_e0_two, local.at[1])),
        begin(own_loads("r", 1, r1_two, own_r1_two, got_r1_two, held_r1_two, local.at[2])),
        begin([pltpu.make_async_copy(own_share("e", 0, n, e0), own_e0.at[n], local.at[3, n]) for n in range(3)]),
        begin(own_loads("r", 0, r0, own_r0, got_r0, held_r0, local.at[4])),
    ]
    *weights, rows, gres, dwo = operand_loads(0, wq, wk, wv, rows, gres, dwo, held)

    def launch(key, group, stage, source, got, n):
        flights[key] = begin(stage_copies(group, stage, source, got, send.at[n], recv.at[n]))

    def to_all(source, dest, at):
        out = []
        for d in range(1, 8):
            t = lax.rem(pos + d, 8)
            out.append(remote(source(t), dest.at[pos], vsend.at[at + d], vrecv.at[at + d], pos_device(t)))
        return begin(out)

    def along(axis, got, at):
        return begin([remote(vtotal, got.at[d - 1], vsend.at[at + d], vrecv.at[at + d], peer_of(axis, place, d)) for d in (1, 2, 3)])

    def far_done():
        end(flights["vc"])
        vgot[pos] = vsum[pos]
        total = vgot[0]
        for k in range(1, 8):
            total = total + vgot[k]
        vtotal[...] = total
        flights["vz"] = along(0, vz, 7)

    def square_flights(half):
        out = []
        for d in (2, 1, 3):
            for n, axis in ((1, 1), (2, 0)):
                at, two = lax.rem(place[axis] + d, 4), pl.ds(2 * half, 2)
                src = p0.at[1, two, :, at] if n == 1 else p0.at[2, two, at]
                sems = send.at[12 + half, n, d - 1], recv.at[12 + half, n, d - 1]
                out.append(remote(src, got_q0.at[n, d - 1, two], *sems, peer_of(axis, place, d)))
        return out

    def square_along_y(d):
        to = lax.rem(place[2] + d, 4)
        return remote(p0.at[0, to], got_q0.at[0, d - 1], send.at[5, 0, d - 1], recv.at[5, 0, d - 1], peer_of(2, place, d))

    def launch_squares(half):
        for d in (2, 1, 3):
            pl.when(lax.rem(place[2] + d, 4) // 2 == half)(lambda d=d: square_along_y(d).start())
        begin(square_flights(half))

    def forward_two():
        end(flights["vz"])
        vtotal[...] = vtotal[...] + vz[0] + vz[1] + vz[2]
        flights["vx"] = along(1, vx, 10)
        end(flights["q1_two"])
        add_direct("q", 1, s_q0_two, got_q1_two, s_q1_two)
        launch("q2_two", "q", 2, s_q1_two, got_q2_two, 6)
        end(flights["e1_two"])
        add_direct("e", 1, s_e0_two, got_e1_two, s_e1_two)
        launch("e2_two", "e", 2, s_e1_two, got_e2_two, 11)

    met()
    end(loads[0])
    add_held(own_q0_two, held_q0_two, s_q0_two)
    launch("q1_two", "q", 1, s_q0_two, got_q1_two, 2)
    end(loads[1])
    add_held(own_e0_two, held_e0_two, s_e0_two)
    launch("e1_two", "e", 1, s_e0_two, got_e1_two, 3)
    end(loads[4])
    add_held(own_r0, held_r0, s_r0)
    launch("r1", "r", 1, s_r0, got_r1, 1)
    launch("e0", "e", 0, e0, held_e0, 14)
    end(loads[2])
    add_held(own_r1_two, held_r1_two, s_r1_two)
    launch("r2_two", "r", 2, s_r1_two, got_r2_two, 4)
    end(first)
    halves = (half_got, hsend, hrecv)
    arrived, halves_arrived = attend_back_part(
        0, table, held_q, held_kv, held_gm, gq, parts, vec_p, acc, scratch[1], None, asend, arecv, halves
    )
    vectors = [vec_p[0:1], vec_p[1:2]] + [vec[k : k + 1] for k in range(6)]
    vectors += [vec_p_two[0:1], vec_p_two[1:2]] + [vec_two[k : k + 1] for k in range(6)]
    vectors += [v[:, k * D : (k + 1) * D] for v in (vec_e, vec_e_two) for k in range(4)]
    for k, vector in enumerate(vectors):
        vsum[k // 3, k % 3 : k % 3 + 1] = vector
    for k in range(8):
        vsum[k, 3:8] = jnp.zeros((5, D), F32)
    flights["vc"] = to_all(lambda t: vsum.at[t], vgot, 0)
    grads, near, _, gh_send, gh_got, qcat, kvcat, psend, precv = scratch
    wq, wk, wv = weights
    y_hi, _, block = places()
    mine, yours = columns_at(core * HALF, HALF), columns_at(other * HALF, HALF)
    half_q = remote(gq.at[:, yours], qcat.at[core], psend.at[1], precv.at[1], sibling)
    half_q.start()
    qcat[core] = gq[:, mine]

    def place_square(y, grad):
        for k, piece in enumerate(pieces_of(grad)):
            p0[k, y] = piece

    place_square(1, dwo()[...])
    end(halves_arrived)
    far_at = rows_at(far_start(y_hi), FAR[0])
    for side in range(2):
        far = (parts[side, far_at, mine].astype(F32) + half_got[side, 2 * ROWS :].astype(F32)).astype(BF)
        for c in range(2):
            here = rows_at((y_hi * 2 + c) * ROWS, ROWS)
            own = parts[side, here, mine].astype(F32) + half_got[side, c * ROWS : (c + 1) * ROWS].astype(F32)
            kvcat[side, c, 0:ROWS] = own.astype(BF)
            kvcat[side, c, ROWS:] = far
    rows = rows()
    half_q.wait()
    place_square(0, (dot_tn(rows[0, 0:ROWS], qcat[0]) + dot_tn(rows[1, 0:ROWS], qcat[1])).astype(BF))
    launch_squares(0)
    chip_rows = rows[...].reshape(2 * (ROWS + FAR[0]), D)
    for side in range(2):
        place_square(2 + side, dot_tn(chip_rows, kvcat[side].reshape(2 * (ROWS + FAR[0]), HALF)).astype(BF))
    launch_squares(1)
    partner, give, theirs = far_plan(0, y_hi, core, block)
    hidden = remote(gh_send, gh_got, psend.at[0], precv.at[0], partner)
    wk(), wv()

    @pl.when(is_middle(block))
    def _():
        far_k, far_v = parts[0, rows_at(theirs, FAR[0])], parts[1, rows_at(theirs, FAR[0])]
        gh_send[...] = (dot_nt(far_k, wk()[...]) + dot_nt(far_v, wv()[...])).astype(BF)
        hidden.start()

    def last(group, source, got):
        thirds = []
        for n in range(3):
            total = own_share(group, 2, n, source)[...].astype(F32)
            for d in range(3):
                total += got[n, d].astype(F32)
            thirds.append(total)
        return jnp.concatenate(thirds, axis=1)

    def rows_out(layer, part, total):
        for k in range(8):
            fix_send[layer, part, k, 0:6] = total[6 * k : 6 * k + 6]
        out = []
        for d in range(1, 8):
            t = lax.rem(pos + d, 8)
            sems = fsend.at[layer, part, d], frecv.at[layer, part, d]
            out.append(remote(fix_send.at[layer, part, t], fix_got.at[layer, part, pos], *sems, pos_device(t)))
        return begin(out)

    def reduce_out(layer, total):
        rfix_send[layer] = total
        there, here = [pl.ds(pl.multiple_of(c * 24, 8), 24) for c in (other, core)]
        rfix_got[layer, core] = rfix_send[layer, here]
        sems = fsend.at[layer, 0, 0], frecv.at[layer, 0, 0]
        return begin([remote(rfix_send.at[layer, there], rfix_got.at[layer, core], *sems, sibling)])

    far_done()
    end(arrived)
    grads[:, 0:ROWS] = (parts[:, rows_at(block * ROWS, ROWS)].astype(F32) + near[...].astype(F32)).astype(BF)
    total = gres()[...] + dot_nt(gq[...], wq()[...])
    gh[...] = (total + dot_nt(grads[0, 0:ROWS], wk()[...]) + dot_nt(grads[1, 0:ROWS], wv()[...])).astype(BF)
    end([square_along_y(d) for d in (1, 2, 3)] + square_flights(0) + square_flights(1))
    add_direct("q", 0, p0, got_q0, s_q0)
    launch("q1", "q", 1, s_q0, got_q1, 9)
    end(loads[3] + flights["e0"])
    add_held(own_e0, held_e0, s_e0)
    launch("e1", "e", 1, s_e0, got_e1, 0)
    forward_two()
    end(flights["r1"])
    add_direct("r", 1, s_r0, got_r1, s_r1)
    launch("r2", "r", 2, s_r1, got_r2, 8)
    end(flights["q1"])
    add_direct("q", 1, s_q0, got_q1, s_q1)
    launch("q2", "q", 2, s_q1, got_q2, 10)
    end(flights["e1"])
    add_direct("e", 1, s_e0, got_e1, s_e1)
    launch("e2", "e", 2, s_e1, got_e2, 7)
    end(flights["r2_two"])
    fixes = reduce_out(1, last("r", s_r1_two, got_r2_two))
    end(flights["q2_two"])
    fixes += rows_out(1, 0, last("q", s_q1_two, got_q2_two))
    end(flights["e2_two"])
    fixes += rows_out(1, 1, last("e", s_e1_two, got_e2_two))
    end(flights["vx"])
    vtotal[...] = vtotal[...] + vx[0] + vx[1] + vx[2]
    fixes += to_all(lambda t: vtotal, v_out, 13)
    v_out[pos] = vtotal[...]
    end(flights["q2"])
    fixes += rows_out(0, 0, last("q", s_q1, got_q2))
    end(flights["r2"])
    fixes += reduce_out(0, last("r", s_r1, got_r2))
    end(flights["e2"])
    fixes += rows_out(0, 1, last("e", s_e1, got_e2))

    @pl.when(is_middle(block))
    def _():
        hidden.wait()
        here = rows_at(give, FAR[0])
        gh[here, :] = (gh[here, :].astype(F32) + gh_got[...].astype(F32)).astype(BF)

    for layer in range(2):
        for part in range(2):
            fix_got[layer, part, pos] = fix_send[layer, part, pos]
    end(fixes)


def last_step(table, saved, gm, e0, r0, got_r0, gres, dwo, w, carry, vecs):
    dma, shape = pltpu.SemaphoreType.DMA, jax.ShapeDtypeStruct
    own, got = own_scratch, got_scratch
    return pl.pallas_call(
        last_kernel,
        out_shape=(shape((ROWS, D), BF), shape((2, 2, 8, 8, HALF), F32), shape((2, 2, 24, HALF), F32), shape((8, 8, D), F32)),
        in_specs=[SMEM] * 4 + [ANY] * 18 + [VMEM] * 5,
        out_specs=[VMEM] * 4,
        scratch_shapes=attend_back_scratch() + project_back_scratch(0) + operand_scratch(0)
        + [pltpu.VMEM(WHOLE, BF), got(0), own(0), got(1), own(1), got(2)]
        + [own(0), got(0), own(0), got(1), own(1), got(2)] * 4
        + [own(1), got(1), own(1), got(2)]
        + [
            pltpu.VMEM((2, 2, 8, 8, HALF), F32),
            pltpu.VMEM((2, 48, HALF), F32),
            pltpu.VMEM((8, 8, D), F32),
            pltpu.VMEM((8, 8, D), F32),
            pltpu.VMEM((8, D), F32),
            pltpu.VMEM((3, 8, D), F32),
            pltpu.VMEM((3, 8, D), F32),
            pltpu.VMEM((2, D), F32),
            pltpu.VMEM((2, 2 * ROWS + FAR[0], HALF), BF),
            dma((5, 4)), dma((15, 3, 3)), dma((15, 3, 3)), dma((2, 2, 8)), dma((2, 2, 8)), dma((21,)), dma((21,)), dma((2, 3)), dma((2, 3)),
        ],
        compiler_params=pltpu.CompilerParams(collective_id=3, has_side_effects=True, vmem_limit_bytes=62 * MIB),
        name="last_step",
    )(*table, saved["q"], saved["kv_all"], gm, saved["rows_all"], gres, dwo, w["query_weight"], w["key_weight"], w["value_weight"],
      e0, r0, got_r0, *carry, *vecs)


def finish_kernel(quads, rows, vecs, final, grad, *outs):
    me = lax.axis_index(DP_BLK)
    wq, wk, wv, wo, we, wr, q_b, v_b, s_g, s_s, r_b, f_g, f_s, o_b, e_b, final_out, grad_out = outs
    final_out[...] = final[...]
    grad_out[...] = grad[...]
    for layer in range(2):
        for s in range(8):
            y, c = (s // 2 % 2) * 2 + s // 4, s % 2
            (wq, wo, wk, wv)[y][:, layer, c * HALF : (c + 1) * HALF] = quads[layer, 0, s, 0:6]
            we[:, layer, y * D + c * HALF : y * D + (c + 1) * HALF] = quads[layer, 1, s, 0:6]
        for c in range(2):
            wr[layer, :, c * HALF : (c + 1) * HALF] = rows[layer, c]
    vectors = [vecs[k // 3, k % 3 : k % 3 + 1] for k in range(VECTORS)]
    turned = pltpu.roll(jnp.concatenate(vectors[0:16], axis=0), lax.rem(D - 6 * me, D), 1)
    for n, out in enumerate((q_b, v_b, s_g, s_s, r_b, f_g, f_s, o_b)):
        for layer in range(2):
            out[layer : layer + 1] = turned[8 * layer + n : 8 * layer + n + 1, 0:6]
    wide = pltpu.roll(jnp.concatenate(vectors[16:24], axis=0), lax.rem(D - 24 * lax.rem(me, 32), D), 1)
    for layer in range(2):
        total = jnp.zeros((1, 24), F32)
        for k in range(4):
            total = total + jnp.where(me // 32 == k, wide[4 * layer + k : 4 * layer + k + 1, 0:24], 0.0)
        e_b[layer : layer + 1] = total


def finish(quads, rows, vecs, final, grad):
    shape = jax.ShapeDtypeStruct
    square, small, hidden = shape((6, 2, D), F32), shape((2, 6), F32), shape((1, ROWS, D), BF)
    outs = pl.pallas_call(
        finish_kernel,
        out_shape=(square,) * 4 + (shape((6, 2, FF), F32), shape((2, 24, D), F32)) + (small,) * 8 + (shape((2, 24), F32),)
        + (hidden, hidden),
        in_specs=[VMEM] * 5,
        out_specs=(VMEM,) * 17,
        name="finish",
    )(quads, rows, vecs, final[None], grad[None])
    wq, wk, wv, wo, we = [o.transpose(1, 0, 2) for o in outs[:5]]
    wr, q_b, v_b, s_g, s_s, r_b, f_g, f_s, o_b, e_b, final, grad = outs[5:]
    return (final, grad, wq, wk, wv, wo, q_b, v_b, o_b, we, e_b, wr, r_b, f_g, f_s, s_g, s_s)


NAMES = (
    "query_weight", "key_weight", "value_weight", "output_weight", "query_bias", "value_bias", "output_bias", "expand_weight",
    "expand_bias", "reduce_weight", "reduce_bias", "first_gain", "first_shift", "second_gain", "second_shift",
)


def local(hidden, output_grad, block_counts, slot_table, block_order_two, block_order_three, *weights):
    w = dict(zip(NAMES, weights))
    table = (slot_table, block_counts, block_order_two.T, block_order_three.T)
    middle, early, saved_one = first_layer(hidden[0], table, w)
    final, saved_two, rest = second_layer(middle, early, output_grad[0], table, w)
    r_two, gi, dwo, gres, gm, vec_two, vec_e_two = rest
    q_two, grad_middle, e_two, r1, got_r, vec_p_two, got_e = second_back(table, saved_two, gm, gi, r_two, gres, dwo, w)
    r0, e0, dwo, gres, gm, vec, vec_e, got_q, got_r0 = tail_back(grad_middle, saved_one, w, (q_two,))
    carry = (q_two, got_q, e_two, got_e, r1, got_r)
    vecs = (vec, vec_e, vec_p_two, vec_two, vec_e_two)
    grad_hidden, *sums = last_step(table, saved_one, gm, e0, r0, got_r0, gres, dwo, w, carry, vecs)
    return finish(*sums, final, grad_hidden)


def solution(mesh):
    finer = Mesh(mesh.devices.reshape(4, 4, 2, 2, 2), DP_BLK)
    in_specs = (P(DP, BLK, None), P(DP, BLK, None), P(DP), P(DP, None)) + (P(),) * 17
    wide, flat = P(None, DP_BLK, None), P(None, DP_BLK)
    out_specs = (P(DP, BLK, None), P(DP, BLK, None), wide, wide, wide, wide, flat, flat, flat, wide, flat, wide) + (flat,) * 5
    return jax.shard_map(local, mesh=finer, in_specs=in_specs, out_specs=out_specs, check_vma=False)
```

```python
import functools

import jax
import jax.numpy as jnp
from jax import lax
from jax.experimental import pallas as pl
from jax.experimental.pallas import tpu as pltpu
from jax.sharding import Mesh
from jax.sharding import PartitionSpec as P

D = 768
FF = 3072
HEADS = 12
HD = 64
BLOCK = 512
SLOTS = 3
ROWS = 384
PIECE = 128
CHUNK = 768
HALF = 384
BLK = ("blk_0", "blk_1")
DP_BLK = ("dp_0", "dp_1", "dp_2", "blk_0", "blk_1")
DP = ("dp_0", "dp_1", "dp_2")
EPSILON = 1e-06
ROOT_HALF = 0.7071067811865476
INV_ROOT_TAU = 0.3989422804014327
SCALE = HD ** (-0.5)
MESH = pl.DeviceIdType.MESH
BF = jnp.bfloat16
F32 = jnp.float32
MIB = 1024 * 1024
VMEM = pl.BlockSpec(memory_space=pltpu.VMEM)
SMEM = pl.BlockSpec(memory_space=pltpu.SMEM)
ANY = pl.BlockSpec(memory_space=pl.ANY)


def dot(left, right):
    return jnp.dot(left, right, preferred_element_type=F32)


def dot_nt(left, right):
    return lax.dot_general(left, right, (((1,), (1,)), ((), ())), preferred_element_type=F32)


def dot_tn(left, right):
    return lax.dot_general(left, right, (((0,), (0,)), ((), ())), preferred_element_type=F32)


def params(limit=60):
    return pltpu.CompilerParams(vmem_limit_bytes=limit * MIB)


def row_of(ref, layer):
    return ref[layer : layer + 1, :].astype(F32)


def norm_parts(residual):
    mean = jnp.mean(residual, axis=-1, keepdims=True)
    centred = residual - mean
    inv_std = lax.rsqrt(jnp.mean(centred * centred, axis=-1, keepdims=True) + EPSILON)
    return centred * inv_std, inv_std


def norm_backward(grad, gain, normed, inv_std):
    scaled = grad * gain
    return inv_std * (
        scaled
        - jnp.mean(scaled, axis=-1, keepdims=True)
        - normed * jnp.mean(scaled * normed, axis=-1, keepdims=True)
    )


def layer_block(layer, shape, index):
    return pl.BlockSpec((None,) + shape, lambda j: (layer,) + index(j))


def peer_of(axis, place, offset):
    at = lax.rem(place[axis] + offset, 4)
    if axis == 0:
        return {"dp_0": at}
    if axis == 1:
        return {"dp_1": at}
    return {"dp_2": lax.rem(at, 2), "blk_0": at // 2}


def pos_device(t):
    return {"dp_2": t // 4, "blk_0": lax.rem(t // 2, 2), "blk_1": lax.rem(t, 2)}


def columns_at(start, count):
    return pl.ds(pl.multiple_of(start, 128), count)


STREAM_ORDERS = ((2, 0, 1), (1, 2, 0), (0, 1, 2))
LAYOUT = {"q": (2, 0, 1), "e": (2, 0, 1), "r": (0, 1, 2)}
PIECES = (48, 128)
LEFT = ((4, 4) + PIECES, (4,) + PIECES, PIECES)
WHOLE = (3, 4) + LEFT[0]


def share(group, stage, stream, ref, at):
    order, left = STREAM_ORDERS[stream], list(LAYOUT[group])
    for done in order[:stage]:
        left.remove(done)
    if group == "r" and order[stage] == 2:
        at = lax.rem(at, 2) * 2 + at // 2
    index = [slice(None)] * left.index(order[stage]) + [at]
    return ref.at[(stream, *index)]


def add_up(own, got, out, streams=3):
    for n in range(streams):

        def part(at, n=n):
            total = own[n](at).astype(F32)
            for d in range(3):
                total += got[(n, d) + at].astype(F32)
            out[(n,) + at] = total.astype(out.dtype)

        if len(out.shape) == 5:
            pl.loop(0, 4)(lambda k, part=part: part((k,)))
        else:
            part((slice(None),))


def chip_place():
    y = lax.axis_index("blk_0") * 2 + lax.axis_index("dp_2")
    return (lax.axis_index("dp_0"), lax.axis_index("dp_1"), y)


def stage_copies(group, stage, source, got, send, recv, streams=(0, 1, 2)):
    place = chip_place()
    copies = []
    for d in (2, 1, 3):
        for n in streams:
            axis = STREAM_ORDERS[n][stage]
            src = share(group, stage, n, source, lax.rem(place[axis] + d, 4))
            copies.append(remote(src, got.at[n, d - 1], send.at[n, d - 1], recv.at[n, d - 1], peer_of(axis, place, d)))
    return copies


def own_share(group, stage, stream, source):
    return share(group, stage, stream, source, chip_place()[STREAM_ORDERS[stream][stage]])


def own_loads(group, stage, source, held, got, got_held, sems):
    out = [pltpu.make_async_copy(own_share(group, stage, n, source), held.at[n], sems.at[n]) for n in range(3)]
    return out + [pltpu.make_async_copy(got, got_held, sems.at[3])]


def add_held(held, got, out):
    add_up([lambda at, n=n: held[(n,) + at] for n in range(3)], got, out)


def add_direct(group, stage, source, got, out):
    views = [own_share(group, stage, n, source) for n in range(3)]
    add_up([lambda at, v=v: v[at] for v in views], got, out)


def axis_peers(axes, offsets=(1, 2, 3)):
    place = chip_place()
    return [peer_of(a, place, d) for a in axes for d in offsets]


def landing(stage):
    return jax.ShapeDtypeStruct((3, 3) + LEFT[stage], BF)


def summed(stage):
    return (3,) + LEFT[stage]


def begin(copies):
    for c in copies:
        c.start()
    return copies


def end(copies):
    for c in copies:
        c.wait()


class Late:
    def __init__(self, source, held, sem):
        self.copy, self.held, self.waited = pltpu.make_async_copy(source, held, sem), held, False
        self.copy.start()

    def __call__(self):
        if not self.waited:
            self.copy.wait()
            self.waited = True
        return self.held


def pieces_of(grad):
    return [grad[:, k * 128 : (k + 1) * 128].reshape(4, 4, 48, 128) for k in range(3)]


def places():
    y_hi, core = lax.axis_index("blk_0"), lax.axis_index("blk_1")
    return y_hi, core, y_hi * 2 + core


def remote(src, dst, send, recv, device):
    return pltpu.make_async_remote_copy(
        src_ref=src, dst_ref=dst, send_sem=send, recv_sem=recv, device_id=device, device_id_type=MESH
    )


def rows_at(start, count):
    return pl.ds(pl.multiple_of(start, PIECE), count)


def hail(devices):
    barrier = pltpu.get_barrier_semaphore()
    for device in devices:
        pl.semaphore_signal(barrier, inc=1, device_id=device, device_id_type=MESH)
    return lambda: pl.semaphore_wait(barrier, len(devices))


FAR = (256, ROWS)
EARLY = 192


def far_plan(layer, y_hi, core, block):
    if layer == 0:
        partner = {"blk_0": 1 - y_hi, "blk_1": 1 - core}
        return partner, jnp.where(block == 1, 128, 0), jnp.where(block == 1, 768, 512)
    return {"blk_0": 1 - y_hi}, 0, lax.rem(block + 2, 4) * ROWS


def is_middle(block):
    return jnp.logical_and(block >= 1, block <= 2)


def project_back_body(layer, rows, gq, parts, arrived, gres, dwo, weights, p0, gh, scratch, hooks):
    grads, near, far_near, gh_send, gh_got, qcat, kvcat, send, recv = scratch
    wq, wk, wv = weights
    y_hi, core, block = places()
    far_rows = FAR[layer]
    sibling = {"blk_1": 1 - core}
    partner, give, theirs = far_plan(layer, y_hi, core, block)
    mine = columns_at(core * HALF, HALF)
    yours = columns_at((1 - core) * HALF, HALF)

    def talk(step):
        if layer == 0:
            pl.when(is_middle(block))(step)
        else:
            step()

    half_q = remote(gq.at[:, yours], qcat.at[core], send.at[1], recv.at[1], sibling)
    half_q.start()
    end(arrived)
    far = parts[:, rows_at(theirs, far_rows)]
    if layer == 1:
        far = (far.astype(F32) + far_near[...].astype(F32)).astype(BF)
    grads[:, ROWS:] = far
    wk(), wv()
    hidden = remote(gh_send, gh_got, send.at[0], recv.at[0], partner)

    def far_part():
        gh_send[...] = (dot_nt(grads[0, ROWS:], wk()[...]) + dot_nt(grads[1, ROWS:], wv()[...])).astype(BF)
        hidden.start()

    talk(far_part)
    hooks["far"]()
    grads[:, 0:ROWS] = (parts[:, rows_at(block * ROWS, ROWS)].astype(F32) + near[...].astype(F32)).astype(BF)
    half_kv = remote(grads.at[:, :, yours], kvcat.at[:, core], send.at[2], recv.at[2], sibling)
    half_kv.start()
    qcat[core] = gq[:, mine]
    kvcat[:, core] = grads[:, :, mine]

    def place_square(y, grad):
        for k, piece in enumerate(pieces_of(grad)):
            p0[k, y] = piece

    place_square(1, dwo()[...])
    half_q.wait()
    rows = rows()
    place_square(0, (dot_tn(rows[0, 0:ROWS], qcat[0]) + dot_tn(rows[1, 0:ROWS], qcat[1])).astype(BF))
    hooks["two_squares"]()
    half_kv.wait()
    for side in (0, 1):
        cat = kvcat[side].reshape(2 * (ROWS + far_rows), HALF)
        place_square(2 + side, dot_tn(rows[...].reshape(2 * (ROWS + far_rows), D), cat).astype(BF))
    hooks["squares"]()
    total = gres()[...] + dot_nt(gq[...], wq()[...])
    total += dot_nt(grads[0, 0:ROWS], wk()[...]) + dot_nt(grads[1, 0:ROWS], wv()[...])
    if layer == 1:
        hidden.wait()
        gh[...] = (total + gh_got[...].astype(F32)).astype(gh.dtype)
    else:
        gh[...] = total.astype(gh.dtype)

        @pl.when(is_middle(block))
        def _():
            hidden.wait()
            here = rows_at(give, far_rows)
            gh[here, :] = (gh[here, :].astype(F32) + gh_got[...].astype(F32)).astype(gh.dtype)


def project_back_scratch(layer):
    far_rows, dma = FAR[layer], pltpu.SemaphoreType.DMA
    across = (2, far_rows, D) if layer == 1 else (8, 128)
    return [
        pltpu.VMEM((2, ROWS + far_rows, D), BF), pltpu.VMEM((2, ROWS, D), BF),
        pltpu.VMEM(across, BF), pltpu.VMEM((far_rows, D), BF), pltpu.VMEM((far_rows, D), BF),
        pltpu.VMEM((2, ROWS, HALF), BF), pltpu.VMEM((2, 2, ROWS + far_rows, HALF), BF),
        dma((3,)), dma((3,)),
    ]


def operand_scratch(layer):
    return [
        pltpu.VMEM((D, D), BF), pltpu.VMEM((D, D), BF), pltpu.VMEM((D, D), BF), pltpu.VMEM((2, ROWS + FAR[layer], D), BF),
        pltpu.VMEM((ROWS, D), F32), pltpu.VMEM((D, HALF), BF), pltpu.SemaphoreType.DMA((6,)),
    ]


def operand_loads(layer, wq, wk, wv, rows, gres, dwo, held):
    sems = held[-1]
    sources = (wq.at[layer], wk.at[layer], wv.at[layer], rows, gres, dwo)
    return [Late(source, into, sems.at[n]) for n, (source, into) in enumerate(zip(sources, held))]


def own_scratch(stage):
    return pltpu.VMEM(summed(stage), BF)


def got_scratch(stage):
    return pltpu.VMEM((3, 3) + LEFT[stage], BF)


def second_back_kernel(
    tab, cnt, two, three, q, kv, gm, gi, r0, low_all, rows, gres, dwo, wq, wk, wv, p0_out, gh, e_out, s_r, got_r, vec, got_e, *refs
):
    refs = list(refs)

    def take(count):
        out, refs[:count] = refs[:count], []
        return out

    held_q, held_kv, held_gm, gq, parts, acc, asems, asend, arecv = take(9)
    scratch, held = take(9), take(7)
    p0, e, gicat, held_low, own_r, held_r, csems, gsems, osems, rsend, rrecv, csend, crecv, esend, erecv = take(15)
    core = lax.axis_index("blk_1")
    table = (tab, cnt, two, three)
    met = hail([{"blk_1": 1 - core}] + axis_peers((0, 1, 2)))
    loads = begin(
        [
            pltpu.make_async_copy(gi, gicat, gsems.at[0]),
            pltpu.make_async_copy(low_all, held_low, gsems.at[1]),
        ]
    )
    first = begin(
        [pltpu.make_async_copy(src, dst, asems.at[n]) for n, (src, dst) in enumerate(((q, held_q), (kv, held_kv), (gm, held_gm)))]
    )
    *weights, rows, gres, dwo = operand_loads(1, wq, wk, wv, rows, gres, dwo, held)
    own_loads_r = begin([pltpu.make_async_copy(own_share("r", 0, n, r0), own_r.at[n], csems.at[n]) for n in range(3)])
    end(loads)
    for y in (0, 2):
        both = gicat[:, :, y * HALF : (y + 2) * HALF].reshape(2 * ROWS, 2 * HALF)
        grad = dot_tn(held_low[...].reshape(2 * ROWS, D), both).astype(BF)
        for k, piece in enumerate(pieces_of(grad[:, :HALF])):
            e[k, y] = piece
        for k, piece in enumerate(pieces_of(grad[:, HALF:])):
            e[k, y + 1] = piece
    met()
    travelling = begin(stage_copies("r", 0, r0, held_r, rsend, rrecv))
    carried = begin(stage_copies("e", 0, e, got_e, esend, erecv))
    carried += begin([pltpu.make_async_copy(e, e_out, osems.at[0])])
    end(first)
    arrived = attend_back_part(1, table, held_q, held_kv, held_gm, gq, parts, vec, acc, scratch[1], scratch[2], asend, arecv)

    def two_squares():
        end(own_loads_r + travelling)
        add_held(own_r, held_r, s_r)
        carried.extend(begin(stage_copies("r", 1, s_r, got_r, csend, crecv)))

    def squares():
        carried.extend(begin([pltpu.make_async_copy(p0, p0_out, osems.at[1])]))

    hooks = dict(far=lambda: None, two_squares=two_squares, squares=squares)
    project_back_body(1, rows, gq, parts, arrived, gres, dwo, weights, p0, gh, scratch, hooks)
    end(carried)


def second_back(table, saved, gm, gi, r0, gres, dwo, w):
    shape, dma = jax.ShapeDtypeStruct, pltpu.SemaphoreType.DMA
    return pl.pallas_call(
        second_back_kernel,
        out_shape=(
            shape(WHOLE, BF), shape((ROWS, D), F32), shape(WHOLE, BF), shape(summed(0), BF), landing(1), shape((2, D), F32),
            landing(0),
        ),
        in_specs=[SMEM] * 4 + [ANY] * 12,
        out_specs=(ANY, VMEM, ANY, VMEM, ANY, VMEM, ANY),
        scratch_shapes=attend_back_scratch() + project_back_scratch(1) + operand_scratch(1)
        + [pltpu.VMEM(WHOLE, BF), pltpu.VMEM(WHOLE, BF), pltpu.VMEM((2, ROWS, STEPS * HALF), BF), pltpu.VMEM((2, ROWS, D), BF)]
        + [own_scratch(0), got_scratch(0), dma((3,)), dma((2,)), dma((2,))] + [dma((3, 3))] * 6,
        compiler_params=pltpu.CompilerParams(collective_id=4, has_side_effects=True, vmem_limit_bytes=60 * MIB),
        name="second_back",
    )(*table, saved["q"], saved["kv_all"], gm, gi, r0, saved["low_all"], saved["rows_all"], gres, dwo,
      w["query_weight"], w["key_weight"], w["value_weight"])


def slots_of(layer, tab, cnt, two, three, piece, head):
    block = lax.axis_index("blk_0") * 2 + lax.axis_index("blk_1")
    t = (3 * block + piece) // 4
    j = jnp.where(tab[0, 1] == t, 1, jnp.where(tab[0, 2] == t, 2, 0))
    live = jnp.where(j < cnt[0], 1.0, 0.0)
    if layer == 0:
        return t, live
    from_two = jnp.where(j < 2, two[jnp.minimum(j, 1), head], j)
    chosen = jnp.where(cnt[0] == SLOTS, three[j, head], from_two)
    return tab[0, chosen], live


def left_lanes(rows=1):
    return lax.broadcasted_iota(jnp.int32, (rows, 2 * HD), 1) < HD


def two_heads(tile):
    left, none = left_lanes(PIECE), jnp.zeros_like(tile)
    return jnp.concatenate([jnp.where(left, tile, none), jnp.where(left, none, tile)], axis=0)


def own_columns(both):
    return jnp.where(left_lanes(PIECE), both[:PIECE], both[PIECE:])


def own_rows(both):
    top = lax.broadcasted_iota(jnp.int32, (2 * HD, PIECE), 0) < HD
    return jnp.where(top, both[:, :PIECE], both[:, PIECE:]).T


def slot_mask(s0, s1, t, kind):
    first, second = jnp.where(s0 == t, 1.0, 0.0), jnp.where(s1 == t, 1.0, 0.0)
    return jnp.where(left_lanes(), first, second).astype(kind)


def attend_back_step(layer, table, pair, columns, q, kv, gm, gq, parts, acc):
    masks = []
    if layer == 0:
        acc[...] = jnp.zeros_like(acc)
    for i in range(3):
        rows = pl.ds(i * PIECE, PIECE)
        s0, live = slots_of(layer, *table, i, 2 * pair)
        if layer == 0:
            keys, values = kv[0, s0, :, columns], kv[1, s0, :, columns]
        else:
            s1, _ = slots_of(layer, *table, i, 2 * pair + 1)
            low = [slot_mask(s0, s1, t, BF) for t in range(SLOTS)]
            masks.append([slot_mask(s0, s1, t, F32) for t in range(SLOTS)])
            keys, values = [sum(kv[side, t, :, columns] * low[t] for t in range(SLOTS)) for side in (0, 1)]
        qq = two_heads(q[rows, columns] * jnp.asarray(SCALE, BF))
        gg = two_heads((gm[rows, columns].astype(F32) * live).astype(BF))
        scores = dot_nt(keys, qq)
        exps = jnp.exp(scores - jnp.max(scores, axis=0, keepdims=True))
        factor = 1.0 / jnp.sum(exps, axis=0, keepdims=True)
        grad_weights = dot_nt(values, gg)
        delta = jnp.sum(exps * grad_weights, axis=0, keepdims=True) * factor
        weights = exps * factor
        grad_scores = (weights * (grad_weights - delta)).astype(BF)
        gq[rows, columns] = (own_rows(dot_tn(keys, grad_scores)) * SCALE).astype(BF)
        gk = dot(grad_scores, qq)
        gv = dot(weights.astype(BF), gg)
        if layer == 0:
            acc[0, s0] += gk
            acc[1, s0] += gv
        else:
            acc[0, i] = gk
            acc[1, i] = gv
    if layer == 0:
        parts[:, :, columns] = acc[...].reshape(2, SLOTS * BLOCK, 2 * HD).astype(BF)
    else:
        for side in range(2):
            for t in range(SLOTS):
                total = acc[side, 0] * masks[0][t] + acc[side, 1] * masks[1][t] + acc[side, 2] * masks[2][t]
                parts[side, t * BLOCK : (t + 1) * BLOCK, columns] = total.astype(BF)


def attend_back_part(layer, table, q, kv, gm, gq, parts, vec, acc, near, far_near, send, recv, halves=None):
    y_hi, core, _ = places()
    sibling = {"blk_1": 1 - core}

    def share(pair):
        columns = columns_at(pair * 2 * HD, 2 * HD)
        beside = rows_at((y_hi * 2 + 1 - core) * ROWS, ROWS)
        out = [remote(parts.at[:, beside, columns], near.at[:, :, columns], send.at[0, pair], recv.at[0, pair], sibling)]
        if layer == 1:
            across = rows_at(((1 - y_hi) * 2 + 1 - core) * ROWS, ROWS)
            out.append(
                remote(parts.at[:, across, columns], far_near.at[:, :, columns], send.at[1, pair], recv.at[1, pair], sibling)
            )
        return out

    def half_copies(i):
        theirs, hsend, hrecv = halves
        columns, to = columns_at(((1 - core) * 3 + i) * 2 * HD, 2 * HD), columns_at(i * 2 * HD, 2 * HD)
        out = []
        for n, (start, count, at) in enumerate(((y_hi * 2 * ROWS, 2 * ROWS, 0), (far_start(y_hi), FAR[0], 2 * ROWS))):
            src, dst = parts.at[:, rows_at(start, count), columns], theirs.at[:, pl.ds(at, count), to]
            out.append(remote(src, dst, hsend.at[n, i], hrecv.at[n, i], sibling))
        return out

    @pl.loop(0, HEADS // 2)
    def _(pair):
        columns = columns_at(pair * 2 * HD, 2 * HD)
        attend_back_step(layer, table, pair, columns, q, kv, gm, gq, parts, acc)
        if halves:

            @pl.when(pair // 3 == 1 - core)
            def _():
                begin(half_copies(lax.rem(pair, 3)))

        begin(share(pair))

    vec[0:1] = jnp.sum(gq[...].astype(F32), axis=0, keepdims=True)
    total = jnp.zeros((1, D), F32)
    for i in range(3):
        _, live = slots_of(0, *table, i, 0)
        total += live * jnp.sum(gm[i * PIECE : (i + 1) * PIECE, :].astype(F32), axis=0, keepdims=True)
    vec[1:2] = total
    arrived = [c for pair in range(HEADS // 2) for c in share(pair)]
    return (arrived, [c for i in range(3) for c in half_copies(i)]) if halves else arrived


def far_start(y_hi):
    return (1 - y_hi) * 256 + 512


def attend_back_scratch():
    dma = pltpu.SemaphoreType.DMA
    return [
        pltpu.VMEM((ROWS, D), BF), pltpu.VMEM((2, SLOTS, BLOCK, D), BF), pltpu.VMEM((ROWS, D), BF), pltpu.VMEM((ROWS, D), BF),
        pltpu.VMEM((2, SLOTS * BLOCK, D), BF), pltpu.VMEM((2, SLOTS, BLOCK, 2 * HD), F32),
        dma((3,)), dma((2, HEADS // 2)), dma((2, HEADS // 2)),
    ]


STEPS = FF // CHUNK


def chunk_columns(j):
    return pl.ds(j * CHUNK, CHUNK)


def project_part(layer, h, early, wq, wk, wv, bq, bv, q, kv_all, rows_all, low, far, local, send, recv):
    y_hi, core, block = places()
    far_rows = FAR[layer]
    sibling = {"blk_1": 1 - core}
    partner, give, theirs = far_plan(layer, y_hi, core, block)
    low[...] = h[...].astype(BF)
    first = 0 if layer == 0 else EARLY
    rest = far.at[pl.ds(first, far_rows - first)]
    hidden = remote(low.at[pl.ds(pl.multiple_of(give + first, 64), far_rows - first)], rest, send.at[0], recv.at[0], partner)

    def talk(step):
        if layer == 0:
            pl.when(is_middle(block))(step)
        else:
            step()

    talk(lambda: hidden.start())
    if layer == 1:
        there = pltpu.make_async_copy(early, far.at[pl.ds(0, EARLY)], local.at[0])
        there.start()
    own_dst = rows_all.at[core, pl.ds(0, ROWS)]
    copies, kept = [], begin([remote(low, own_dst, send.at[1], recv.at[1], sibling), pltpu.make_async_copy(low, own_dst, local.at[1])])

    def keys_of(source, count, start):
        at = rows_at(start, count) if count % PIECE == 0 else pl.ds(pl.multiple_of(start, 64), count)
        kv_all[0, at] = dot(source, wk()[...]).astype(BF)
        kv_all[1, at] = (dot(source, wv()[...]) + row_of(bv, layer)).astype(BF)
        return kv_all.at[:, at]

    mine = keys_of(low[...], ROWS, block * ROWS)
    copies += begin([remote(mine, mine, send.at[2], recv.at[2], sibling)])
    q[...] = (dot(low[...], wq()[...]) + row_of(bq, layer)).astype(BF)
    if layer == 1:
        there.wait()
        part = keys_of(far[0:EARLY], EARLY, theirs)
        copies += begin([remote(part, part, send.at[3], recv.at[3], sibling)])
    talk(lambda: hidden.wait())
    if layer == 0:

        @pl.when(jnp.logical_not(is_middle(block)))
        def _():
            far[...] = jnp.zeros_like(far)

    far_dst = rows_all.at[core, pl.ds(ROWS, far_rows)]
    kept += begin([remote(far, far_dst, send.at[4], recv.at[4], sibling), pltpu.make_async_copy(far, far_dst, local.at[2])])
    if layer == 0:
        talk(lambda: keys_of(far[...], far_rows, theirs) and None)
    else:
        part = keys_of(far[first:far_rows], far_rows - first, theirs + first)
        copies += begin([remote(part, part, send.at[5], recv.at[5], sibling)])
    end(copies)
    return kept


def attend_part(layer, table, q, kv_all, mixed):
    @pl.loop(0, HEADS // 2)
    def _(pair):
        columns = columns_at(pair * 2 * HD, 2 * HD)

        def tile(side, slot):
            return kv_all[side, pl.ds(slot * BLOCK, BLOCK) if isinstance(slot, int) else rows_at(slot * BLOCK, BLOCK), columns]

        for i in range(3):
            rows = pl.ds(i * PIECE, PIECE)
            s0, live = slots_of(layer, *table, i, 2 * pair)
            if layer == 0:
                keys, values = tile(0, s0), tile(1, s0)
            else:
                s1, _ = slots_of(layer, *table, i, 2 * pair + 1)
                masks = [slot_mask(s0, s1, t, BF) for t in range(SLOTS)]
                keys, values = [sum(tile(side, t) * masks[t] for t in range(SLOTS)) for side in (0, 1)]
            scores = dot_nt(two_heads(q[rows, columns] * jnp.asarray(SCALE, BF)), keys)
            exps = jnp.exp(scores - jnp.max(scores, axis=1, keepdims=True))
            factor = live / jnp.sum(exps, axis=1, keepdims=True)
            mixed[rows, columns] = own_columns(dot(exps.astype(BF), values) * factor).astype(BF)


def tail_rows(layer, rows, h, mixed, wo, wes, wrs, vectors, r1, first, low, slope, r2, store, after_low):
    bo, g1, s1, be, br, g2, s2 = vectors
    residual = h[rows, :].astype(F32) + dot(mixed[rows, :], wo()[...]) + row_of(bo, layer)
    r1[rows, :] = residual
    normed, _ = norm_parts(residual)
    first[rows, :] = normed * row_of(g1, layer) + row_of(s1, layer)
    low[rows, :] = first[rows, :].astype(BF)
    after_low()
    total = first[rows, :] + row_of(br, layer)
    for j in range(STEPS):
        inner = dot(low[rows, :], wes[j]()[...]) + be[layer : layer + 1, j * CHUNK : (j + 1) * CHUNK].astype(F32)
        phi = 0.5 * (1.0 + lax.erf(inner * ROOT_HALF))
        low_act = (inner * phi).astype(BF)
        slope[j, rows, :] = (phi + inner * (INV_ROOT_TAU * jnp.exp(-0.5 * inner * inner))).astype(BF)
        store(j, low_act)
        total = total + dot(low_act, wrs[j]()[...])
    r2[rows, :] = total
    normed, _ = norm_parts(total)
    return normed * row_of(g2, layer) + row_of(s2, layer)


def weight_loads(layer, wq, wk, wv, wo, we, wr, held, sems):
    held_q, held_k, held_v, held_o, held_e, held_r = held
    wk, wv = Late(wk.at[layer], held_k, sems.at[0]), Late(wv.at[layer], held_v, sems.at[1])
    wq, wo = Late(wq.at[layer], held_q, sems.at[2]), Late(wo.at[layer], held_o, sems.at[3])
    wes = [Late(we.at[layer, :, chunk_columns(j)], held_e.at[j], sems.at[4 + 2 * j]) for j in range(STEPS)]
    wrs = [Late(wr.at[layer, chunk_columns(j)], held_r.at[j], sems.at[5 + 2 * j]) for j in range(STEPS)]
    return wq, wk, wv, wo, wes, wrs


def weight_scratch():
    square = pltpu.VMEM((D, D), BF)
    return [square] * 4 + [pltpu.VMEM((STEPS, D, CHUNK), BF), pltpu.VMEM((STEPS, CHUNK, D), BF), pltpu.SemaphoreType.DMA((2 * STEPS + 4,))]


def project_scratch(layer):
    dma = pltpu.SemaphoreType.DMA
    return [
        pltpu.VMEM((2, SLOTS * BLOCK, D), BF), pltpu.VMEM((ROWS, D), BF), pltpu.VMEM((FAR[layer], D), BF),
        dma((3,)), dma((6,)), dma((6,)),
    ]


def first_layer_kernel(tab, cnt, two, three, h, wq, wk, wv, wo, we, wr, bq, bv, bo, g1, s1, be, br, g2, s2, *refs):
    refs = list(refs)

    def take(count):
        out, refs[:count] = refs[:count], []
        return out

    q, kv_out, rows_all, r1_out, r2, out, slope_out, act_all, low_all, mixed_all, ahead = take(11)
    held, (wsems,) = take(6), take(1)
    kv_all, low_in, far, plocal, psend, precv = take(6)
    mixed, r1, first, low, act, slope, next_low, local, send, recv = take(10)
    y_hi, core, _ = places()
    sibling, partner = {"blk_1": 1 - core}, {"blk_0": 1 - y_hi}
    met = hail([sibling, partner, {"blk_0": 1 - y_hi, "blk_1": 1 - core}])
    wq, wk, wv, wo, wes, wrs = weight_loads(0, wq, wk, wv, wo, we, wr, held, wsems)
    met()
    kept = project_part(0, h, None, wq, wk, wv, bq, bv, q, kv_all, rows_all, low_in, far, plocal, psend, precv)
    copies = kept + begin([pltpu.make_async_copy(kv_all, kv_out, local.at[2 * STEPS + 3])])
    attend_part(0, (tab, cnt, two, three), q, kv_all, mixed)

    def both(src, dst, n):
        return [remote(src, dst, send.at[n], recv.at[n], sibling), pltpu.make_async_copy(src, dst, local.at[n])]

    copies += begin(both(mixed, mixed_all.at[core], STEPS))
    parts = [(0, EARLY), (EARLY, ROWS - EARLY)]
    for n, (start, count) in enumerate(parts):
        rows = pl.ds(start, count)
        final = n == len(parts) - 1

        def after_low():
            if final:
                copies.extend(begin(both(low, low_all.at[core], STEPS + 1)))
                copies.extend(begin([pltpu.make_async_copy(r1, r1_out, local.at[STEPS + 2])]))

        def store(j, low_act):
            act[j, rows, :] = low_act
            if final:
                copies.extend(begin(both(act.at[j], act_all.at[core, j], j)))
                copies.extend(
                    begin([pltpu.make_async_copy(slope.at[j], slope_out.at[:, chunk_columns(j)], local.at[STEPS + 3 + j])])
                )

        vectors = (bo, g1, s1, be, br, g2, s2)
        result = tail_rows(0, rows, h, mixed, wo, wes, wrs, vectors, r1, first, low, slope, r2, store, after_low)
        out[rows, :] = result
        if n == 0:
            next_low[...] = result.astype(BF)
            copies.extend(begin([remote(next_low, ahead, send.at[STEPS + 2], recv.at[STEPS + 2], partner)]))
    end(copies)


def weight_args(w):
    names = ("query_weight", "key_weight", "value_weight", "output_weight", "expand_weight", "reduce_weight", "query_bias",
             "value_bias", "output_bias", "first_gain", "first_shift", "expand_bias", "reduce_bias", "second_gain", "second_shift")
    return [w[name] for name in names]


def first_layer(h, table, w):
    dma, shape = pltpu.SemaphoreType.DMA, jax.ShapeDtypeStruct
    low, full = shape((ROWS, D), BF), shape((ROWS, D), F32)
    pair = shape((2, ROWS, D), BF)
    q, kv_all, rows_all, r1, r2, out, slope, act_all, low_all, mixed_all, early = pl.pallas_call(
        first_layer_kernel,
        out_shape=(
            low, shape((2, SLOTS * BLOCK, D), BF), shape((2, ROWS + FAR[0], D), BF), full, full, full, shape((ROWS, FF), BF),
            shape((2, STEPS, ROWS, CHUNK), BF), pair, pair, shape((EARLY, D), BF),
        ),
        in_specs=[SMEM] * 4 + [VMEM] + [ANY] * 6 + [VMEM] * 9,
        out_specs=(VMEM, ANY, ANY, ANY, VMEM, VMEM, ANY, ANY, ANY, ANY, ANY),
        scratch_shapes=weight_scratch() + project_scratch(0)
        + [pltpu.VMEM((ROWS, D), BF), pltpu.VMEM((ROWS, D), F32), pltpu.VMEM((ROWS, D), F32), pltpu.VMEM((ROWS, D), BF)]
        + [pltpu.VMEM((STEPS, ROWS, CHUNK), BF)] * 2
        + [pltpu.VMEM((EARLY, D), BF), dma((2 * STEPS + 4,)), dma((STEPS + 3,)), dma((STEPS + 3,))],
        compiler_params=pltpu.CompilerParams(collective_id=1, has_side_effects=True, vmem_limit_bytes=60 * MIB),
        name="first_layer",
    )(*table, h, *weight_args(w))
    saved = dict(
        rows_all=rows_all, q=q, kv_all=kv_all.reshape(2, SLOTS, BLOCK, D), r1=r1, r2=r2, slope=slope, act_all=act_all,
        low_all=low_all, mixed_all=mixed_all,
    )
    return out, early, saved


def second_layer_kernel(tab, cnt, two, three, h, early, g, wq, wk, wv, wo, we, wr, bq, bv, bo, g1, s1, be, br, g2, s2, *refs):
    refs = list(refs)

    def take(count):
        out, refs[:count] = refs[:count], []
        return out

    out, q, kv_out, rows_all, low_out, dwr_out, gi_out, dwo, gres, gm, vec, vec_e = take(12)
    held, (wsems,) = take(6), take(1)
    kv_all, low_in, far, plocal, psend, precv = take(6)
    r1, first, r2, act_all, low_all, mixed_all, slope, local, send, recv = take(10)
    scratch = take(11)
    _, core, _ = places()
    y_hi = lax.axis_index("blk_0")
    sibling, partner = {"blk_1": 1 - core}, {"blk_0": 1 - y_hi}
    met = hail([sibling, partner])
    wq, wk, wv, wo, wes, wrs = weight_loads(1, wq, wk, wv, wo, we, wr, held, wsems)
    met()
    kept = project_part(1, h, early, wq, wk, wv, bq, bv, q, kv_all, rows_all, low_in, far, plocal, psend, precv)
    copies = kept + begin([pltpu.make_async_copy(kv_all, kv_out, local.at[0])])
    mixed, low = mixed_all.at[core], low_all.at[core]
    attend_part(1, (tab, cnt, two, three), q, kv_all, mixed)

    def to_sibling(ref, n):
        return begin([remote(ref, ref, send.at[n], recv.at[n], sibling)])[0]

    shared = {"mixed": to_sibling(mixed, STEPS)}

    def after_low():
        shared["low"] = to_sibling(low, STEPS + 1)
        copies.extend(begin([pltpu.make_async_copy(low, low_out.at[core], local.at[1])]))

    def store(j, low_act):
        act_all[core, j] = low_act
        shared[j] = to_sibling(act_all.at[core, j], j)

    vectors = (bo, g1, s1, be, br, g2, s2)
    rows = pl.ds(0, ROWS)
    result = tail_rows(1, rows, h, mixed, wo, wes, wrs, vectors, r1, first, low, slope, r2, store, after_low)
    out[...] = result.astype(BF)

    def acts(j):
        shared[j].wait()
        return act_all[:, j]

    def mixed_pair():
        shared["mixed"].wait()
        return mixed_all[...]

    tail_back_part(
        1, g, lambda: r1[...], r2, acts, lambda j: slope[j], mixed_pair, None, wo, wes, wrs, g1, g2,
        (dwr_out, gi_out, dwo, gres, gm, vec, vec_e), scratch,
    )
    shared["low"].wait()
    copies += begin([pltpu.make_async_copy(low_all.at[1 - core], low_out.at[1 - core], local.at[2])])
    end(copies)


def second_layer(h, early, g, table, w):
    dma, shape = pltpu.SemaphoreType.DMA, jax.ShapeDtypeStruct
    low, full, pair = shape((ROWS, D), BF), shape((ROWS, D), F32), shape((2, ROWS, D), BF)
    whole = pltpu.VMEM((ROWS, D), F32)
    out, q, kv_all, rows_all, low_all, *rest = pl.pallas_call(
        second_layer_kernel,
        out_shape=(
            low, low, shape((2, SLOTS * BLOCK, D), BF), shape((2, ROWS + FAR[1], D), BF), pair,
            shape(WHOLE, BF), shape((2, ROWS, STEPS * HALF), BF), shape((D, HALF), BF), full, low,
            shape((8, D), F32), shape((1, FF), F32),
        ),
        in_specs=[SMEM] * 4 + [VMEM, ANY, VMEM] + [ANY] * 6 + [VMEM] * 9,
        out_specs=(VMEM, VMEM, ANY, ANY, ANY, ANY, ANY) + (VMEM,) * 5,
        scratch_shapes=weight_scratch() + project_scratch(1)
        + [whole, whole, whole, pltpu.VMEM((2, STEPS, ROWS, CHUNK), BF), pltpu.VMEM((2, ROWS, D), BF), pltpu.VMEM((2, ROWS, D), BF)]
        + [pltpu.VMEM((STEPS, ROWS, CHUNK), BF), dma((3,)), dma((STEPS + 2,)), dma((STEPS + 2,))]
        + tail_back_scratch(1),
        compiler_params=pltpu.CompilerParams(collective_id=2, has_side_effects=True, vmem_limit_bytes=62 * MIB),
        name="second_layer",
    )(*table, h, early, g, *weight_args(w))
    return out, dict(rows_all=rows_all, q=q, kv_all=kv_all.reshape(2, SLOTS, BLOCK, D), low_all=low_all), rest


def chunk_of(layer, j):
    return j if layer == 1 else lax.rem(lax.axis_index("dp_0") + 1 + j, STEPS)


def tail_back_part(layer, g, r1, r2, acts, slopes, mixed_all, low_all, wo, wes, wrs, g1, g2, outs, scratch, send_chunk=None):
    dwr_out, dwe_out, dwo, gres, gm, vec, vec_e = outs
    dwr, dwe, go, ga, gi, gocat, gacat, gicat, local, send, recv = scratch
    core = lax.axis_index("blk_1")
    sibling = {"blk_1": 1 - core}
    mine, yours = columns_at(core * HALF, HALF), columns_at((1 - core) * HALF, HALF)
    copies = []
    grad = g[...].astype(F32)
    normed, inv_std = norm_parts(r2[...])
    grad_r = norm_backward(grad, row_of(g2, layer), normed, inv_std)
    vec[0:1] = jnp.sum(grad * normed, axis=0, keepdims=True)
    vec[1:2] = jnp.sum(grad, axis=0, keepdims=True)
    total = grad_r
    go[...] = grad_r.astype(BF)
    vec[2:3] = jnp.sum(go[...].astype(F32), axis=0, keepdims=True)
    share_go = remote(go.at[:, yours], gocat.at[core], send.at[STEPS], recv.at[STEPS], sibling)
    share_go.start()
    gocat[core] = go[:, mine]
    shares = []

    def expand_gradient(j):
        shares[j].wait()
        part = dot_tn(low_all().reshape(2 * ROWS, D), gicat[j].reshape(2 * ROWS, HALF)).astype(BF)
        at = chunk_of(layer, j)
        for k, piece in enumerate(pieces_of(part)):
            dwe[k, at] = piece
        copies.extend(begin([pltpu.make_async_copy(dwe.at[:, at], dwe_out.at[:, at], local.at[1, j])]))

    for j in range(STEPS):
        grad_inner = (dot_nt(go[...], wrs[j]()[...]) * slopes(j).astype(F32)).astype(BF)
        gi[j] = grad_inner
        if layer == 0:
            shares.append(remote(gi.at[j, :, yours], gicat.at[j, core], send.at[j], recv.at[j], sibling))
            shares[j].start()
            gicat[j, core] = gi[j, :, mine]
        else:
            dst = dwe_out.at[core, :, pl.ds(j * HALF, HALF)]
            copies += begin([pltpu.make_async_copy(gi.at[j, :, mine], dst, local.at[1, j])])
            copies += begin([remote(gi.at[j, :, yours], dst, send.at[j], recv.at[j], sibling)])
        at = chunk_of(layer, j)
        vec_e[:, columns_at(at * CHUNK, CHUNK)] = jnp.sum(grad_inner.astype(F32), axis=0, keepdims=True)
        total = total + dot_nt(grad_inner, wes[j]()[...])
        if j == 0:
            share_go.wait()
        part = dot_tn(acts(j).reshape(2 * ROWS, CHUNK), gocat[...].reshape(2 * ROWS, HALF)).astype(BF)
        for k, piece in enumerate(pieces_of(part)):
            dwr[k, at] = piece
        copies += begin([pltpu.make_async_copy(dwr.at[:, at], dwr_out.at[:, at], local.at[0, j])])
        if send_chunk:
            send_chunk(j, at, dwr)
        if layer == 0 and j > 0:
            expand_gradient(j - 1)
    normed, inv_std = norm_parts(r1())
    grad_r = norm_backward(total, row_of(g1, layer), normed, inv_std)
    vec[3:4] = jnp.sum(total * normed, axis=0, keepdims=True)
    vec[4:5] = jnp.sum(total, axis=0, keepdims=True)
    gres[...] = grad_r
    ga[...] = grad_r.astype(BF)
    vec[5:6] = jnp.sum(ga[...].astype(F32), axis=0, keepdims=True)
    share_ga = remote(ga.at[:, yours], gacat.at[core], send.at[STEPS + 1], recv.at[STEPS + 1], sibling)
    share_ga.start()
    gacat[core] = ga[:, mine]
    if layer == 0:
        expand_gradient(STEPS - 1)
    gm[...] = dot_nt(ga[...], wo()[...]).astype(BF)
    share_ga.wait()
    dwo[...] = dot_tn(mixed_all().reshape(2 * ROWS, D), gacat[...].reshape(2 * ROWS, HALF)).astype(BF)
    end(copies)


def tail_back_scratch(layer):
    dma = pltpu.SemaphoreType.DMA
    return [
        pltpu.VMEM(WHOLE, BF), pltpu.VMEM(WHOLE if layer == 0 else (8, 128), BF),
        pltpu.VMEM((ROWS, D), BF), pltpu.VMEM((ROWS, D), BF), pltpu.VMEM((STEPS, ROWS, CHUNK), BF),
        pltpu.VMEM((2, ROWS, HALF), BF), pltpu.VMEM((2, ROWS, HALF), BF),
        pltpu.VMEM((STEPS, 2, ROWS, HALF) if layer == 0 else (8, 128), BF),
        dma((3, STEPS)), dma((STEPS + 2,)), dma((STEPS + 2,)),
    ]


def tail_back_kernel(g, r1, r2, low_all, act_all, slope, mixed_all, wo, we, wr, g1, g2, q_in, *refs):
    refs = list(refs)

    def take(count):
        out, refs[:count] = refs[:count], []
        return out

    outs, (got_q, got_r), scratch = take(7), take(2), take(11)
    held_wr, held_slope, held_we, held_act, held_r1, held_wo, held_mixed, held_low, late, csend, crecv, rsend, rrecv = take(13)
    core = lax.axis_index("blk_1")
    met = hail([{"blk_1": 1 - core}] + axis_peers((0, 1, 2)))
    wrs, slopes, wes, acts = [], [], [], []
    for j in range(STEPS):
        at = columns_at(chunk_of(0, j) * CHUNK, CHUNK)
        wrs.append(Late(wr.at[0, at], held_wr.at[j], late.at[4 * j]))
        slopes.append(Late(slope.at[:, at], held_slope.at[j], late.at[4 * j + 1]))
        wes.append(Late(we.at[0, :, at], held_we.at[j], late.at[4 * j + 2]))
        acts.append(Late(act_all.at[:, chunk_of(0, j)], held_act.at[j], late.at[4 * j + 3]))
    r1, wo = Late(r1, held_r1, late.at[4 * STEPS]), Late(wo.at[0], held_wo, late.at[4 * STEPS + 1])
    mixed_all = Late(mixed_all, held_mixed, late.at[4 * STEPS + 2])
    low_all = Late(low_all, held_low, late.at[4 * STEPS + 3])
    met()
    carried = begin(stage_copies("q", 0, q_in, got_q, csend, crecv))
    place = chip_place()

    def send_chunk(j, at, dwr):
        for d in (2, 1, 3):
            for n, axis in ((0, 2), (1, 1)):
                to = lax.rem(place[axis] + d, 4)
                src = dwr.at[0, at, :, lax.rem(to, 2) * 2 + to // 2] if n == 0 else dwr.at[1, at, to]
                sems = rsend.at[n, d - 1, j], rrecv.at[n, d - 1, j]
                carried.extend(begin([remote(src, got_r.at[n, d - 1, at], *sems, peer_of(axis, place, d))]))
        if j < STEPS - 1:
            sems = rsend.at[2, j, 0], rrecv.at[2, j, 0]
            carried.extend(begin([remote(dwr.at[2, at], got_r.at[2, j], *sems, peer_of(0, place, j + 1))]))

    tail_back_part(
        0, g, lambda: r1()[...], r2, lambda j: acts[j]()[...], lambda j: slopes[j]()[...], lambda: mixed_all()[...],
        lambda: low_all()[...], wo, wes, wrs, g1, g2, outs, scratch, send_chunk,
    )
    end(carried)


def tail_back(g, saved, w, carry):
    dma, shape = pltpu.SemaphoreType.DMA, jax.ShapeDtypeStruct
    return pl.pallas_call(
        tail_back_kernel,
        out_shape=(
            shape(WHOLE, BF), shape(WHOLE, BF), shape((D, HALF), BF), shape((ROWS, D), F32), shape((ROWS, D), BF),
            shape((8, D), F32), shape((1, FF), F32), landing(0), landing(0),
        ),
        in_specs=[VMEM, ANY, VMEM] + [ANY] * 7 + [VMEM, VMEM, ANY],
        out_specs=(ANY, ANY) + (VMEM,) * 5 + (ANY,) * 2,
        scratch_shapes=tail_back_scratch(0)
        + [
            pltpu.VMEM((STEPS, CHUNK, D), BF), pltpu.VMEM((STEPS, ROWS, CHUNK), BF), pltpu.VMEM((STEPS, D, CHUNK), BF),
            pltpu.VMEM((STEPS, 2, ROWS, CHUNK), BF), pltpu.VMEM((ROWS, D), F32), pltpu.VMEM((D, D), BF),
            pltpu.VMEM((2, ROWS, D), BF), pltpu.VMEM((2, ROWS, D), BF),
            dma((4 * STEPS + 4,)), dma((3, 3)), dma((3, 3)), dma((3, 3, STEPS)), dma((3, 3, STEPS)),
        ],
        compiler_params=pltpu.CompilerParams(collective_id=7, has_side_effects=True, vmem_limit_bytes=60 * MIB),
        name="tail_back_0",
    )(g, saved["r1"], saved["r2"], saved["low_all"], saved["act_all"], saved["slope"], saved["mixed_all"],
      w["output_weight"], w["expand_weight"], w["reduce_weight"], w["first_gain"], w["second_gain"], *carry)


VECTORS = 24


def last_kernel(*refs):
    refs = list(refs)

    def take(count):
        out, refs[:count] = refs[:count], []
        return out

    table, (q, kv, gm, rows, gres, dwo, wq, wk, wv, e0, r0, got_r0) = take(4), take(12)
    q0_two, got_q0_two, e0_two, got_e0_two, r1_two, got_r1_two = take(6)
    vec, vec_e, vec_p_two, vec_two, vec_e_two = take(5)
    gh, fix_got, rfix_got, v_out = take(4)
    held_q, held_kv, held_gm, gq, parts, acc, asems, asend, arecv = take(9)
    scratch, held = take(9), take(7)
    p0, got_q0, s_q0, got_q1, s_q1, got_q2 = take(6)
    own_e0, held_e0, s_e0, got_e1, s_e1, got_e2 = take(6)
    own_r0, held_r0, s_r0, got_r1, s_r1, got_r2 = take(6)
    own_q0_two, held_q0_two, s_q0_two, got_q1_two, s_q1_two, got_q2_two = take(6)
    own_e0_two, held_e0_two, s_e0_two, got_e1_two, s_e1_two, got_e2_two = take(6)
    own_r1_two, held_r1_two, s_r1_two, got_r2_two = take(4)
    fix_send, rfix_send, vsum, vgot, vtotal, vz, vx, vec_p, half_got = take(9)
    local, send, recv, fsend, frecv, vsend, vrecv, hsend, hrecv = take(9)

    place = chip_place()
    core = lax.axis_index("blk_1")
    pos = lax.axis_index("dp_2") * 4 + lax.axis_index("blk_0") * 2 + core
    other = 1 - core
    sibling = {"blk_1": other}
    flights = {}
    met = hail(axis_peers((0, 1)) + [pos_device(lax.rem(pos + d, 8)) for d in range(1, 8)])
    first = begin(
        [pltpu.make_async_copy(src, dst, asems.at[n]) for n, (src, dst) in enumerate(((q, held_q), (kv, held_kv), (gm, held_gm)))]
    )
    loads = [
        begin(own_loads("q", 0, q0_two, own_q0_two, got_q0_two, held_q0_two, local.at[0])),
        begin(own_loads("e", 0, e0_two, own_e0_two, got_e0_two, held_e0_two, local.at[1])),
        begin(own_loads("r", 1, r1_two, own_r1_two, got_r1_two, held_r1_two, local.at[2])),
        begin([pltpu.make_async_copy(own_share("e", 0, n, e0), own_e0.at[n], local.at[3, n]) for n in range(3)]),
        begin(own_loads("r", 0, r0, own_r0, got_r0, held_r0, local.at[4])),
    ]
    *weights, rows, gres, dwo = operand_loads(0, wq, wk, wv, rows, gres, dwo, held)

    def launch(key, group, stage, source, got, n):
        flights[key] = begin(stage_copies(group, stage, source, got, send.at[n], recv.at[n]))

    def to_all(source, dest, at):
        out = []
        for d in range(1, 8):
            t = lax.rem(pos + d, 8)
            out.append(remote(source(t), dest.at[pos], vsend.at[at + d], vrecv.at[at + d], pos_device(t)))
        return begin(out)

    def along(axis, got, at):
        return begin([remote(vtotal, got.at[d - 1], vsend.at[at + d], vrecv.at[at + d], peer_of(axis, place, d)) for d in (1, 2, 3)])

    def far_done():
        end(flights["vc"])
        vgot[pos] = vsum[pos]
        total = vgot[0]
        for k in range(1, 8):
            total = total + vgot[k]
        vtotal[...] = total
        flights["vz"] = along(0, vz, 7)

    def square_flights(half):
        out = []
        for d in (2, 1, 3):
            for n, axis in ((1, 1), (2, 0)):
                at, two = lax.rem(place[axis] + d, 4), pl.ds(2 * half, 2)
                src = p0.at[1, two, :, at] if n == 1 else p0.at[2, two, at]
                sems = send.at[12 + half, n, d - 1], recv.at[12 + half, n, d - 1]
                out.append(remote(src, got_q0.at[n, d - 1, two], *sems, peer_of(axis, place, d)))
        return out

    def square_along_y(d):
        to = lax.rem(place[2] + d, 4)
        return remote(p0.at[0, to], got_q0.at[0, d - 1], send.at[5, 0, d - 1], recv.at[5, 0, d - 1], peer_of(2, place, d))

    def launch_squares(half):
        for d in (2, 1, 3):
            pl.when(lax.rem(place[2] + d, 4) // 2 == half)(lambda d=d: square_along_y(d).start())
        begin(square_flights(half))

    def forward_two():
        end(flights["vz"])
        vtotal[...] = vtotal[...] + vz[0] + vz[1] + vz[2]
        flights["vx"] = along(1, vx, 10)
        end(flights["q1_two"])
        add_direct("q", 1, s_q0_two, got_q1_two, s_q1_two)
        launch("q2_two", "q", 2, s_q1_two, got_q2_two, 6)
        end(flights["e1_two"])
        add_direct("e", 1, s_e0_two, got_e1_two, s_e1_two)
        launch("e2_two", "e", 2, s_e1_two, got_e2_two, 11)

    met()
    end(loads[0])
    add_held(own_q0_two, held_q0_two, s_q0_two)
    launch("q1_two", "q", 1, s_q0_two, got_q1_two, 2)
    end(loads[1])
    add_held(own_e0_two, held_e0_two, s_e0_two)
    launch("e1_two", "e", 1, s_e0_two, got_e1_two, 3)
    end(loads[4])
    add_held(own_r0, held_r0, s_r0)
    launch("r1", "r", 1, s_r0, got_r1, 1)
    launch("e0", "e", 0, e0, held_e0, 14)
    end(loads[2])
    add_held(own_r1_two, held_r1_two, s_r1_two)
    launch("r2_two", "r", 2, s_r1_two, got_r2_two, 4)
    end(first)
    halves = (half_got, hsend, hrecv)
    arrived, halves_arrived = attend_back_part(
        0, table, held_q, held_kv, held_gm, gq, parts, vec_p, acc, scratch[1], None, asend, arecv, halves
    )
    vectors = [vec_p[0:1], vec_p[1:2]] + [vec[k : k + 1] for k in range(6)]
    vectors += [vec_p_two[0:1], vec_p_two[1:2]] + [vec_two[k : k + 1] for k in range(6)]
    vectors += [v[:, k * D : (k + 1) * D] for v in (vec_e, vec_e_two) for k in range(4)]
    for k, vector in enumerate(vectors):
        vsum[k // 3, k % 3 : k % 3 + 1] = vector
    for k in range(8):
        vsum[k, 3:8] = jnp.zeros((5, D), F32)
    flights["vc"] = to_all(lambda t: vsum.at[t], vgot, 0)
    grads, near, _, gh_send, gh_got, qcat, kvcat, psend, precv = scratch
    wq, wk, wv = weights
    y_hi, _, block = places()
    mine, yours = columns_at(core * HALF, HALF), columns_at(other * HALF, HALF)
    half_q = remote(gq.at[:, yours], qcat.at[core], psend.at[1], precv.at[1], sibling)
    half_q.start()
    qcat[core] = gq[:, mine]

    def place_square(y, grad):
        for k, piece in enumerate(pieces_of(grad)):
            p0[k, y] = piece

    place_square(1, dwo()[...])
    end(halves_arrived)
    far_at = rows_at(far_start(y_hi), FAR[0])
    for side in range(2):
        far = (parts[side, far_at, mine].astype(F32) + half_got[side, 2 * ROWS :].astype(F32)).astype(BF)
        for c in range(2):
            here = rows_at((y_hi * 2 + c) * ROWS, ROWS)
            own = parts[side, here, mine].astype(F32) + half_got[side, c * ROWS : (c + 1) * ROWS].astype(F32)
            kvcat[side, c, 0:ROWS] = own.astype(BF)
            kvcat[side, c, ROWS:] = far
    rows = rows()
    half_q.wait()
    place_square(0, (dot_tn(rows[0, 0:ROWS], qcat[0]) + dot_tn(rows[1, 0:ROWS], qcat[1])).astype(BF))
    launch_squares(0)
    end(loads[3] + flights["e0"])
    add_held(own_e0, held_e0, s_e0)
    launch("e1", "e", 1, s_e0, got_e1, 0)
    chip_rows = rows[...].reshape(2 * (ROWS + FAR[0]), D)
    for side in range(2):
        place_square(2 + side, dot_tn(chip_rows, kvcat[side].reshape(2 * (ROWS + FAR[0]), HALF)).astype(BF))
    launch_squares(1)
    partner, give, theirs = far_plan(0, y_hi, core, block)
    hidden = remote(gh_send, gh_got, psend.at[0], precv.at[0], partner)
    wk(), wv()

    @pl.when(is_middle(block))
    def _():
        far_k, far_v = parts[0, rows_at(theirs, FAR[0])], parts[1, rows_at(theirs, FAR[0])]
        gh_send[...] = (dot_nt(far_k, wk()[...]) + dot_nt(far_v, wv()[...])).astype(BF)
        hidden.start()

    def last(group, source, got):
        thirds = []
        for n in range(3):
            total = own_share(group, 2, n, source)[...].astype(F32)
            for d in range(3):
                total += got[n, d].astype(F32)
            thirds.append(total)
        return jnp.concatenate(thirds, axis=1)

    def rows_out(layer, part, total):
        for k in range(8):
            fix_send[layer, part, k, 0:6] = total[6 * k : 6 * k + 6]
        out = []
        for d in range(1, 8):
            t = lax.rem(pos + d, 8)
            sems = fsend.at[layer, part, d], frecv.at[layer, part, d]
            out.append(remote(fix_send.at[layer, part, t], fix_got.at[layer, part, pos], *sems, pos_device(t)))
        return begin(out)

    def reduce_out(layer, total):
        rfix_send[layer] = total
        there, here = [pl.ds(pl.multiple_of(c * 24, 8), 24) for c in (other, core)]
        rfix_got[layer, core] = rfix_send[layer, here]
        sems = fsend.at[layer, 0, 0], frecv.at[layer, 0, 0]
        return begin([remote(rfix_send.at[layer, there], rfix_got.at[layer, core], *sems, sibling)])

    far_done()
    end(arrived)
    grads[:, 0:ROWS] = (parts[:, rows_at(block * ROWS, ROWS)].astype(F32) + near[...].astype(F32)).astype(BF)
    total = gres()[...] + dot_nt(gq[...], wq()[...])
    gh[...] = (total + dot_nt(grads[0, 0:ROWS], wk()[...]) + dot_nt(grads[1, 0:ROWS], wv()[...])).astype(BF)
    end([square_along_y(d) for d in (1, 2, 3)] + square_flights(0) + square_flights(1))
    add_direct("q", 0, p0, got_q0, s_q0)
    launch("q1", "q", 1, s_q0, got_q1, 9)
    end(flights["e1"])
    add_direct("e", 1, s_e0, got_e1, s_e1)
    launch("e2", "e", 2, s_e1, got_e2, 7)
    forward_two()
    end(flights["r1"])
    add_direct("r", 1, s_r0, got_r1, s_r1)
    launch("r2", "r", 2, s_r1, got_r2, 8)
    end(flights["q1"])
    add_direct("q", 1, s_q0, got_q1, s_q1)
    launch("q2", "q", 2, s_q1, got_q2, 10)
    end(flights["r2_two"])
    fixes = reduce_out(1, last("r", s_r1_two, got_r2_two))
    end(flights["q2_two"])
    fixes += rows_out(1, 0, last("q", s_q1_two, got_q2_two))
    end(flights["e2_two"])
    fixes += rows_out(1, 1, last("e", s_e1_two, got_e2_two))
    end(flights["vx"])
    vtotal[...] = vtotal[...] + vx[0] + vx[1] + vx[2]
    fixes += to_all(lambda t: vtotal, v_out, 13)
    v_out[pos] = vtotal[...]
    end(flights["q2"])
    fixes += rows_out(0, 0, last("q", s_q1, got_q2))
    end(flights["r2"])
    fixes += reduce_out(0, last("r", s_r1, got_r2))
    end(flights["e2"])
    fixes += rows_out(0, 1, last("e", s_e1, got_e2))

    @pl.when(is_middle(block))
    def _():
        hidden.wait()
        here = rows_at(give, FAR[0])
        gh[here, :] = (gh[here, :].astype(F32) + gh_got[...].astype(F32)).astype(BF)

    for layer in range(2):
        for part in range(2):
            fix_got[layer, part, pos] = fix_send[layer, part, pos]
    end(fixes)


def last_step(table, saved, gm, e0, r0, got_r0, gres, dwo, w, carry, vecs):
    dma, shape = pltpu.SemaphoreType.DMA, jax.ShapeDtypeStruct
    own, got = own_scratch, got_scratch
    return pl.pallas_call(
        last_kernel,
        out_shape=(shape((ROWS, D), BF), shape((2, 2, 8, 8, HALF), F32), shape((2, 2, 24, HALF), F32), shape((8, 8, D), F32)),
        in_specs=[SMEM] * 4 + [ANY] * 18 + [VMEM] * 5,
        out_specs=[VMEM] * 4,
        scratch_shapes=attend_back_scratch() + project_back_scratch(0) + operand_scratch(0)
        + [pltpu.VMEM(WHOLE, BF), got(0), own(0), got(1), own(1), got(2)]
        + [own(0), got(0), own(0), got(1), own(1), got(2)] * 4
        + [own(1), got(1), own(1), got(2)]
        + [
            pltpu.VMEM((2, 2, 8, 8, HALF), F32),
            pltpu.VMEM((2, 48, HALF), F32),
            pltpu.VMEM((8, 8, D), F32),
            pltpu.VMEM((8, 8, D), F32),
            pltpu.VMEM((8, D), F32),
            pltpu.VMEM((3, 8, D), F32),
            pltpu.VMEM((3, 8, D), F32),
            pltpu.VMEM((2, D), F32),
            pltpu.VMEM((2, 2 * ROWS + FAR[0], HALF), BF),
            dma((5, 4)), dma((15, 3, 3)), dma((15, 3, 3)), dma((2, 2, 8)), dma((2, 2, 8)), dma((21,)), dma((21,)), dma((2, 3)), dma((2, 3)),
        ],
        compiler_params=pltpu.CompilerParams(collective_id=3, has_side_effects=True, vmem_limit_bytes=62 * MIB),
        name="last_step",
    )(*table, saved["q"], saved["kv_all"], gm, saved["rows_all"], gres, dwo, w["query_weight"], w["key_weight"], w["value_weight"],
      e0, r0, got_r0, *carry, *vecs)


def finish_kernel(quads, rows, vecs, final, grad, *outs):
    me = lax.axis_index(DP_BLK)
    wq, wk, wv, wo, we, wr, q_b, v_b, s_g, s_s, r_b, f_g, f_s, o_b, e_b, final_out, grad_out = outs
    final_out[...] = final[...]
    grad_out[...] = grad[...]
    for layer in range(2):
        for s in range(8):
            y, c = (s // 2 % 2) * 2 + s // 4, s % 2
            (wq, wo, wk, wv)[y][:, layer, c * HALF : (c + 1) * HALF] = quads[layer, 0, s, 0:6]
            we[:, layer, y * D + c * HALF : y * D + (c + 1) * HALF] = quads[layer, 1, s, 0:6]
        for c in range(2):
            wr[layer, :, c * HALF : (c + 1) * HALF] = rows[layer, c]
    vectors = [vecs[k // 3, k % 3 : k % 3 + 1] for k in range(VECTORS)]
    turned = pltpu.roll(jnp.concatenate(vectors[0:16], axis=0), lax.rem(D - 6 * me, D), 1)
    for n, out in enumerate((q_b, v_b, s_g, s_s, r_b, f_g, f_s, o_b)):
        for layer in range(2):
            out[layer : layer + 1] = turned[8 * layer + n : 8 * layer + n + 1, 0:6]
    wide = pltpu.roll(jnp.concatenate(vectors[16:24], axis=0), lax.rem(D - 24 * lax.rem(me, 32), D), 1)
    for layer in range(2):
        total = jnp.zeros((1, 24), F32)
        for k in range(4):
            total = total + jnp.where(me // 32 == k, wide[4 * layer + k : 4 * layer + k + 1, 0:24], 0.0)
        e_b[layer : layer + 1] = total


def finish(quads, rows, vecs, final, grad):
    shape = jax.ShapeDtypeStruct
    square, small, hidden = shape((6, 2, D), F32), shape((2, 6), F32), shape((1, ROWS, D), BF)
    outs = pl.pallas_call(
        finish_kernel,
        out_shape=(square,) * 4 + (shape((6, 2, FF), F32), shape((2, 24, D), F32)) + (small,) * 8 + (shape((2, 24), F32),)
        + (hidden, hidden),
        in_specs=[VMEM] * 5,
        out_specs=(VMEM,) * 17,
        name="finish",
    )(quads, rows, vecs, final[None], grad[None])
    wq, wk, wv, wo, we = [o.transpose(1, 0, 2) for o in outs[:5]]
    wr, q_b, v_b, s_g, s_s, r_b, f_g, f_s, o_b, e_b, final, grad = outs[5:]
    return (final, grad, wq, wk, wv, wo, q_b, v_b, o_b, we, e_b, wr, r_b, f_g, f_s, s_g, s_s)


NAMES = (
    "query_weight", "key_weight", "value_weight", "output_weight", "query_bias", "value_bias", "output_bias", "expand_weight",
    "expand_bias", "reduce_weight", "reduce_bias", "first_gain", "first_shift", "second_gain", "second_shift",
)


def local(hidden, output_grad, block_counts, slot_table, block_order_two, block_order_three, *weights):
    w = dict(zip(NAMES, weights))
    table = (slot_table, block_counts, block_order_two.T, block_order_three.T)
    middle, early, saved_one = first_layer(hidden[0], table, w)
    final, saved_two, rest = second_layer(middle, early, output_grad[0], table, w)
    r_two, gi, dwo, gres, gm, vec_two, vec_e_two = rest
    q_two, grad_middle, e_two, r1, got_r, vec_p_two, got_e = second_back(table, saved_two, gm, gi, r_two, gres, dwo, w)
    r0, e0, dwo, gres, gm, vec, vec_e, got_q, got_r0 = tail_back(grad_middle, saved_one, w, (q_two,))
    carry = (q_two, got_q, e_two, got_e, r1, got_r)
    vecs = (vec, vec_e, vec_p_two, vec_two, vec_e_two)
    grad_hidden, *sums = last_step(table, saved_one, gm, e0, r0, got_r0, gres, dwo, w, carry, vecs)
    return finish(*sums, final, grad_hidden)


def solution(mesh):
    finer = Mesh(mesh.devices.reshape(4, 4, 2, 2, 2), DP_BLK)
    in_specs = (P(DP, BLK, None), P(DP, BLK, None), P(DP), P(DP, None)) + (P(),) * 17
    wide, flat = P(None, DP_BLK, None), P(None, DP_BLK)
    out_specs = (P(DP, BLK, None), P(DP, BLK, None), wide, wide, wide, wide, flat, flat, flat, wide, flat, wide) + (flat,) * 5
    return jax.shard_map(local, mesh=finer, in_specs=in_specs, out_specs=out_specs, check_vma=False)
```
